32 devices in a mesh: expert: 4 (over y, core), shard: 8 (over z, x).
Axes of the slice: x: 2, y: 2, z: 4, core: 2. Of those that a mesh axis runs over, the one named last changes fastest.
Arguments:
- inputs: bfloat16 [2, 4096, 1536], P(None, ('expert', 'shard')), may hold values from -6 to 6
- cotangent: bfloat16 [2, 4096, 1536], P(None, ('expert', 'shard')), may hold values from -6 to 6
- lengths: int32 [2, 32, 3], P(None, ('expert', 'shard')), may hold values from 1 to 64, 128 in all within a row
- routes: int32 [2, 4096, 8], P(None, ('expert', 'shard')), may hold values from 0 to 39, all different within a row; in each aligned block of 128 rows (0 to 127, 128 to 255, ..., all dimensions but the last counted through in order) at most 40 rows name the same one
- norm_gain_one: bfloat16 [1536], P(('expert', 'shard')), may hold values from 0.5 to 1.5
- w_query: bfloat16 [1536, 1536], P(('expert', 'shard')), may hold values from -0.15625 to 0.15625
- key_projection_weight: bfloat16 [1536, 512], P(('expert', 'shard')), may hold values from -0.15625 to 0.15625
- value_projection_weight: bfloat16 [1536, 512], P(('expert', 'shard')), may hold values from -0.15625 to 0.15625
- w_out: bfloat16 [1536, 1536], P(('expert', 'shard')), may hold values from -0.4375 to 0.4375
- norm_gain_two: bfloat16 [1536], P(('expert', 'shard')), may hold values from 0.5 to 1.5
- w_router: bfloat16 [1536, 40], P(('expert', 'shard')), may hold values from -0.078125 to 0.078125
- w_gate: bfloat16 [40, 1536, 512], P('expert', 'shard'), may hold values from -0.15625 to 0.15625
- w_up: bfloat16 [40, 1536, 512], P('expert', 'shard'), may hold values from -0.15625 to 0.15625
- w_down: bfloat16 [40, 512, 1536], P('expert', 'shard'), may hold values from -0.5 to 0.5
Outputs:
- outputs: bfloat16 [2, 4096, 1536], P(None, ('expert', 'shard'))
- grad_inputs: float32 [2, 4096, 1536], P(None, ('expert', 'shard'))
- grad_norm_gain_one: float32 [1536], P(('expert', 'shard'))
- grad_w_query: float32 [1536, 1536], P(('expert', 'shard'))
- grad_w_key: float32 [1536, 512], P(('expert', 'shard'))
- grad_w_value: float32 [1536, 512], P(('expert', 'shard'))
- grad_w_out: float32 [1536, 1536], P(('expert', 'shard'))
- grad_norm_gain_two: float32 [1536], P(('expert', 'shard'))
- grad_w_router: float32 [1536, 40], P(('expert', 'shard'))
- grad_w_gate: float32 [40, 1536, 512], P('expert', 'shard')
- grad_w_up: float32 [40, 1536, 512], P('expert', 'shard')
- grad_w_down: float32 [40, 512, 1536], P('expert', 'shard')
The draws below stay inside these ranges and needn't reach their ends.
Inputs may be any that keep to these rules, and one draw needn't show every extreme that they name: `routes`: in the rows of one device in one micro-batch no expert is named more than 40 times, a bound that some devices reach for some expert; each row names 8 different experts. The 3 lengths of one device in one micro-batch sum to 128, the largest being exactly 64.
All inputs are finite; a program needn't handle non-finite values.
Results may differ from the reference program's by a relative error of at most 0.015.
Values may be sent and summed in bfloat16 or wider, within the bound.
No kernel may reach another device: no remote copies, remote signals or barrier semaphores. Data moves between devices by JAX's collectives and lax.ppermute only.
A program may use at most 384 MiB of HBM per device.

```python
import math
import jax
import jax.numpy as jnp
import numpy as np
from jax import lax

MODEL_WIDTH = 1536
QUERY_HEADS = 24
KEY_VALUE_HEADS = 8
HEAD_SIZE = 64
E = 40
FF = 512
TOPK = 8
TOKENS_PER_BATCH = 128
MICRO = 2
SEQS = 3
LONGEST = 64
CAP = 40
TOKENS = 4096
N_EXPERT = 4
N_SHARD = 8


def strengthened(array, key, source, target, shards_of, factor):
    owner, partner = [(jnp.arange(array.shape[position]) // (array.shape[position] // shards_of)).reshape([-1 if axis == position else 1 for axis in range(array.ndim)]) for position in (source, target)]
    chosen = jax.random.permutation(key, shards_of)[partner]
    strong = (owner == chosen) | (owner == (partner + shards_of // 2) % shards_of)
    return jnp.where(strong, factor * array, array)


def level_of(own_key, extent, shards, low, largest):
    loudness, own = 1.0, jax.random.fold_in(own_key, 6)
    for position, parts in shards:
        steps = jnp.exp(jax.random.uniform(jax.random.fold_in(own, position), (parts,), jnp.float32, low / len(shards), largest / len(shards)))
        loudness = loudness * jnp.repeat(steps, extent[position] // parts).reshape([-1 if axis == position else 1 for axis in range(len(extent))])
    return loudness


def length_profile(number_of, total, limit, lean):
    loads = [(1 << 20) // math.isqrt(grade ** lean) + 1 for grade in range(2, number_of + 1)]
    spare, given = total - limit - (number_of - 1), [1] * (number_of - 1)
    while spare > 0:
        candidates = [i for i in range(number_of - 1) if given[i] < limit]
        mass, left = sum([loads[i] for i in candidates]), spare
        for i in candidates:
            extra = min(limit - given[i], max(1, left * loads[i] // mass), spare)
            given[i] = given[i] + extra
            spare = spare - extra
    return np.array([limit] + given)


def ragged(rng, number_of, total, most, lean):
    if number_of == 2:
        one = jax.random.randint(rng, (), max(1, total - most), min(most, total - 1) + 1)
        return jnp.stack([one, total - one])
    tallies = jnp.asarray(length_profile(number_of, total, most, lean), jnp.int32)
    couples = (number_of - 1) // 2
    giver, taker = tallies[1:1 + 2 * couples:2], tallies[2:2 + 2 * couples:2]
    room = jnp.minimum(giver - 1, most - taker)
    passed = jax.random.randint(jax.random.fold_in(rng, 1), (couples,), 0, 1 << 20) % (room + 1)
    tallies = tallies.at[1:1 + 2 * couples:2].set(giver - passed).at[2:2 + 2 * couples:2].set(taker + passed)
    return tallies[jax.random.permutation(jax.random.fold_in(rng, 2), number_of)]


def shared_out(key, own, number, rows, amount, top, reach, slope):
    order = jax.random.permutation(key, amount)
    crowded, usual = portions_of(amount, rows * top, reach, slope, True), portions_of(amount, rows * top, reach, slope, False)
    places = jnp.arange(amount)

    def named(sizes, turn):
        used = int((sizes > 0).sum())
        fixed = max(1, used // 4)
        shifted = fixed + (places - fixed + turn * (used - fixed)) % max(1, amount - fixed)
        return jnp.zeros((amount,), jnp.int32).at[order[jnp.where(places < fixed, places, shifted)]].set(jnp.asarray(sizes, jnp.int32))

    sizes = jnp.where(number % 4 == 0, named(crowded, number // 4), named(usual, number - number // 4 - 1))
    mixed = jax.random.permutation(jax.random.fold_in(own, 3), amount)
    donor, taker = mixed[0:amount // 2 * 2:2], mixed[1:amount // 2 * 2:2]
    room = jnp.minimum(sizes[donor] - 1, reach - sizes[taker]) // 2
    room = jnp.where((donor == order[0]) | (taker == order[0]) | (sizes[taker] == 0), 0, jnp.maximum(room, 0))
    shifted = jax.random.randint(jax.random.fold_in(own, 4), (amount // 2,), 0, 1 << 20) % (room + 1)
    sizes = sizes.at[donor].add(-shifted).at[taker].add(shifted)
    members = jnp.searchsorted(jnp.cumsum(sizes), jnp.arange(rows * top), side="right").astype(jnp.int32)
    table = members.reshape(top, rows).T
    table = table[jax.random.permutation(jax.random.fold_in(own, 1), rows)]
    turn = jax.random.randint(jax.random.fold_in(own, 2), (rows, 1), 0, top)
    return jnp.take_along_axis(table, (jnp.arange(top)[None, :] + turn) % top, axis=1)


def portions_of(number_of, total, reach, skew, full):
    portions = [(1 << 20) // math.isqrt(standing ** skew) + 1 for standing in range(1, number_of + 1)]
    largest = reach if full else min(reach, max(-(-total // number_of), total * portions[0] // sum(portions)))
    least = 1 if total - largest >= number_of - 1 else 0
    holding, spare = [largest] + [least] * (number_of - 1), total - largest - least * (number_of - 1)
    while spare > 0:
        movable = [i for i in range(1, number_of) if holding[i] < largest] or [i for i in range(1, number_of) if holding[i] < reach]
        pool, left = sum([portions[i] for i in movable]), spare
        for i in movable:
            extra = min(reach - holding[i], max(1, left * portions[i] // pool), spare)
            holding[i] = holding[i] + extra
            spare = spare - extra
    return np.array(holding)


def bell_draw(stream_key, shape, deviation, reach, cuts=(), kind=jnp.bfloat16):
    entries = deviation * jax.random.normal(stream_key, shape, jnp.float32)
    if cuts:
        entries = entries * level_of(stream_key, shape, cuts, -0.22, 0.18)
    return jnp.clip(entries, -reach, reach).astype(kind)


def noise_with(stream_key, shape, spread, most, pieces, heavy, kind=jnp.bfloat16):
    values = spread * jax.random.normal(stream_key, shape, jnp.float32)
    if pieces:
        values = values * level_of(stream_key, shape, pieces, -0.22, 0.18)
    return jnp.clip(strengthened(values, jax.random.fold_in(stream_key, 3), *heavy), -most, most).astype(kind)


def setup_inputs(seed: int = 0) -> dict:
    seeds = jax.random.split(jax.random.key(seed), 15)
    inputs = noise_with(seeds[0], (MICRO, TOKENS, MODEL_WIDTH), 1.0, 6.0, ((1, 32),), (1, 2, 32, 2.75))
    cotangent = bell_draw(seeds[1], (MICRO, TOKENS, MODEL_WIDTH), 1.0, 6.0, ((1, 32),))
    lengths = jax.vmap(lambda own: ragged(own, SEQS, TOKENS_PER_BATCH, LONGEST, 2))(jax.random.split(seeds[2], MICRO * (N_EXPERT * N_SHARD))).reshape((MICRO, N_EXPERT * N_SHARD, SEQS)).astype(jnp.int32)
    routes_keys = jax.random.split(jax.random.fold_in(seeds[3], 1), MICRO * TOKENS // TOKENS_PER_BATCH)
    routes_turns = jax.random.permutation(jax.random.fold_in(seeds[3], 3), MICRO * TOKENS // TOKENS_PER_BATCH)
    routes = jax.vmap(lambda own, number: shared_out(jax.random.fold_in(seeds[3], 2), own, number, TOKENS_PER_BATCH, E, TOPK, CAP, 2))(routes_keys, routes_turns).reshape((MICRO, TOKENS, TOPK))
    norm_gain_one = jnp.clip(1.0 + 0.1 * jax.random.normal(seeds[4], (MODEL_WIDTH,), jnp.float32), 0.5, 1.5).astype(jnp.bfloat16)
    w_query = bell_draw(seeds[5], (MODEL_WIDTH, QUERY_HEADS * HEAD_SIZE), MODEL_WIDTH ** -0.5, 0.15625, ((0, 32),))
    key_projection_weight = bell_draw(seeds[6], (MODEL_WIDTH, KEY_VALUE_HEADS * HEAD_SIZE), MODEL_WIDTH ** -0.5, 0.15625, ((0, 32),))
    value_projection_weight = bell_draw(seeds[7], (MODEL_WIDTH, KEY_VALUE_HEADS * HEAD_SIZE), MODEL_WIDTH ** -0.5, 0.15625, ((0, 32),))
    w_out = bell_draw(seeds[8], (QUERY_HEADS * HEAD_SIZE, MODEL_WIDTH), (QUERY_HEADS * HEAD_SIZE // 8) ** -0.5, 0.4375, ((0, 32),))
    norm_gain_two = jnp.clip(1.0 + 0.1 * jax.random.normal(seeds[9], (MODEL_WIDTH,), jnp.float32), 0.5, 1.5).astype(jnp.bfloat16)
    w_router = bell_draw(seeds[10], (MODEL_WIDTH, E), (4 * MODEL_WIDTH) ** -0.5, 0.078125, ((0, 32),))
    w_gate = bell_draw(seeds[11], (E, MODEL_WIDTH, FF), MODEL_WIDTH ** -0.5, 0.15625, ((0, 4), (1, 8)))
    w_up = bell_draw(seeds[12], (E, MODEL_WIDTH, FF), MODEL_WIDTH ** -0.5, 0.15625, ((0, 4), (1, 8)))
    w_down = bell_draw(seeds[13], (E, FF, MODEL_WIDTH), (FF // 4) ** -0.5, 0.5, ((0, 4), (1, 8)))
    return {"inputs": inputs, "cotangent": cotangent, "lengths": lengths, "routes": routes, "norm_gain_one": norm_gain_one, "w_query": w_query, "key_projection_weight": key_projection_weight, "value_projection_weight": value_projection_weight, "w_out": w_out, "norm_gain_two": norm_gain_two, "w_router": w_router, "w_gate": w_gate, "w_up": w_up, "w_down": w_down}


@jax.custom_vjp
def reduced_copy(v):
    return lax.optimization_barrier(v.astype(jnp.bfloat16)).astype(jnp.float32)

@jax.custom_vjp
def reduced_copy_backward(v):
    return v

def low_keep(v):
    return (reduced_copy(v), None)

def low_pass(kept, grad):
    return (grad,)

def back_keep(v):
    return (v, None)

def back_low(kept, grad):
    return (reduced_copy(grad),)
reduced_copy.defvjp(low_keep, low_pass)
reduced_copy_backward.defvjp(back_keep, back_low)
epsilon = 1e-05
highest = lax.Precision.HIGHEST

def matrix_product(left, right):
    return jnp.dot(left, right, preferred_element_type=jnp.float32, precision=highest)

def positions(lengths):
    seq_ends = jnp.cumsum(lengths, axis=-1)
    starts = seq_ends - lengths
    token_index = jnp.arange(TOKENS_PER_BATCH, dtype=jnp.int32)
    segment = lax.optimization_barrier(jnp.sum((token_index[:, None] >= seq_ends[..., None, :]).astype(jnp.int32), axis=-1))
    choose = segment[..., None] == jnp.arange(SEQS, dtype=jnp.int32)
    offset = lax.optimization_barrier(jnp.sum(jnp.where(choose, starts[..., None, :], 0), axis=-1))
    return (segment, token_index - offset)

def rotary_embedding(values_in, token_position, direction):
    half_size = values_in.shape[-1] // 2
    frequency = jnp.exp(jnp.arange(half_size, dtype=jnp.float32) * (-math.log(10000.0) / half_size))
    angles = token_position.astype(jnp.float32)[..., None] * frequency
    cosine = jnp.cos(angles)[..., None, :]
    sine_part = jnp.sin(angles)[..., None, :]
    first_half = values_in[..., :half_size]
    second_half = values_in[..., half_size:]
    return jnp.concatenate([first_half * cosine - direction * second_half * sine_part, second_half * cosine + direction * first_half * sine_part], axis=-1)

def slot_positions(routes):
    flat_routes = routes.reshape(routes.shape[:-2] + (-1,))
    onehot = (flat_routes[..., None] == jnp.arange(E, dtype=jnp.int32)).astype(jnp.int32)
    before = jnp.cumsum(onehot, axis=-2) - onehot
    return lax.optimization_barrier(jnp.sum(before * onehot, axis=-1)).reshape(routes.shape)

def block_forward(params, block_item):
    gain_one, w_query, key_projection_weight, value_projection_weight, w_out, gain_two, w_router, w_gate, w_up, w_down = params
    inputs, lengths, routes = block_item
    count_of_blocks = inputs.shape[0]
    segment, token_position = positions(lengths)
    slot_index = slot_positions(routes)
    act_rows = inputs.reshape(-1, MODEL_WIDTH)
    r_one = lax.rsqrt(lax.optimization_barrier(jnp.mean(act_rows * act_rows, axis=-1, keepdims=True)) + epsilon)
    normalized_input = reduced_copy(act_rows * r_one * gain_one)
    query_rows_rotated = reduced_copy_backward(matrix_product(normalized_input, w_query)).reshape(count_of_blocks, TOKENS_PER_BATCH, QUERY_HEADS, HEAD_SIZE)
    projected_key_rows = reduced_copy_backward(matrix_product(normalized_input, key_projection_weight)).reshape(count_of_blocks, TOKENS_PER_BATCH, KEY_VALUE_HEADS, HEAD_SIZE)
    projected_value_rows = reduced_copy(reduced_copy_backward(matrix_product(normalized_input, value_projection_weight))).reshape(count_of_blocks, TOKENS_PER_BATCH, KEY_VALUE_HEADS, HEAD_SIZE)
    query_rows_rotated = reduced_copy(rotary_embedding(query_rows_rotated, token_position, 1.0)).reshape(count_of_blocks, TOKENS_PER_BATCH, KEY_VALUE_HEADS, QUERY_HEADS // KEY_VALUE_HEADS, HEAD_SIZE)
    projected_key_rows = reduced_copy(rotary_embedding(projected_key_rows, token_position, 1.0))
    score_scale = 1.0 / math.sqrt(HEAD_SIZE)
    scores = reduced_copy_backward(jnp.einsum('bqkgd,bskd->bkgqs', query_rows_rotated, projected_key_rows, precision=highest) * score_scale)
    token_index = jnp.arange(TOKENS_PER_BATCH, dtype=jnp.int32)
    allowed = (segment[:, :, None] == segment[:, None, :]) & (token_index[:, None] >= token_index[None, :])
    scores = jnp.where(allowed[:, None, None], scores, -1000000000.0)
    probs = reduced_copy(jax.nn.softmax(scores, axis=-1))
    mixed = jnp.einsum('bkgqs,bskd->bqkgd', probs, projected_value_rows, precision=highest).reshape(-1, QUERY_HEADS * HEAD_SIZE)
    mixed = reduced_copy_backward(reduced_copy(mixed))
    resid = act_rows + reduced_copy_backward(matrix_product(mixed, w_out))
    r_two = lax.rsqrt(lax.optimization_barrier(jnp.mean(resid * resid, axis=-1, keepdims=True)) + epsilon)
    normed_two = reduced_copy(resid * r_two * gain_two)
    logits = reduced_copy_backward(matrix_product(normed_two, w_router))
    chance = jax.nn.softmax(logits, axis=-1).reshape(count_of_blocks, TOKENS_PER_BATCH, E)
    picked = jnp.take_along_axis(chance, routes, axis=-1)
    gate_weights = picked / lax.optimization_barrier(jnp.sum(picked, axis=-1, keepdims=True))
    block_ids = jnp.arange(count_of_blocks, dtype=jnp.int32)[:, None, None]
    target = (block_ids * (E * CAP) + routes * CAP + slot_index).reshape(-1)
    source = jnp.broadcast_to(normed_two.reshape(count_of_blocks, TOKENS_PER_BATCH, 1, MODEL_WIDTH), (count_of_blocks, TOKENS_PER_BATCH, TOPK, MODEL_WIDTH)).reshape(-1, MODEL_WIDTH)
    buffer_rows = jnp.zeros((count_of_blocks * E * CAP, MODEL_WIDTH), jnp.float32).at[target].set(source)
    buffer_rows = reduced_copy_backward(buffer_rows.reshape(count_of_blocks, E, CAP, MODEL_WIDTH))
    gate_part = reduced_copy_backward(jnp.einsum('becd,edf->becf', buffer_rows, w_gate, precision=highest))
    up_part = reduced_copy_backward(jnp.einsum('becd,edf->becf', buffer_rows, w_up, precision=highest))
    active = reduced_copy(jax.nn.silu(gate_part) * up_part)
    result = reduced_copy_backward(reduced_copy(jnp.einsum('becf,efd->becd', active, w_down, precision=highest)))
    returned = result.reshape(-1, MODEL_WIDTH)[target].reshape(count_of_blocks, TOKENS_PER_BATCH, TOPK, MODEL_WIDTH)
    return resid.reshape(count_of_blocks, TOKENS_PER_BATCH, MODEL_WIDTH) + lax.optimization_barrier(jnp.sum(gate_weights[..., None] * returned, axis=2))

def reference(inputs, cotangent, lengths, routes, norm_gain_one, w_query, key_projection_weight, value_projection_weight, w_out, norm_gain_two, w_router, w_gate, w_up, w_down):
    blocks = MICRO * TOKENS // TOKENS_PER_BATCH
    group_size = 1
    while group_size * 2 * TOKENS_PER_BATCH <= 2048 and blocks % (group_size * 2) == 0:
        group_size = group_size * 2
    weights = tuple((weight.astype(jnp.float32) for weight in (norm_gain_one, w_query, key_projection_weight, value_projection_weight, w_out, norm_gain_two, w_router, w_gate, w_up, w_down)))
    input_blocks = inputs.astype(jnp.float32).reshape(blocks // group_size, group_size, TOKENS_PER_BATCH, MODEL_WIDTH)
    length_blocks = lengths.reshape(blocks // group_size, group_size, SEQS)
    route_blocks = routes.reshape(blocks // group_size, group_size, TOKENS_PER_BATCH, TOPK)

    def run_blocks(params, input_rows):
        block_step = jax.checkpoint(lambda block_item: block_forward(params, block_item))
        return lax.map(block_step, (input_rows, length_blocks, route_blocks))
    output, pullback = jax.vjp(run_blocks, weights, input_blocks)
    grad_weights, grad_rows = pullback(cotangent.astype(jnp.float32).reshape(output.shape))
    return (output.reshape(MICRO, TOKENS, MODEL_WIDTH).astype(jnp.bfloat16), grad_rows.reshape(MICRO, TOKENS, MODEL_WIDTH), grad_weights[0], grad_weights[1], grad_weights[2], grad_weights[3], grad_weights[4], grad_weights[5], grad_weights[6], grad_weights[7], grad_weights[8], grad_weights[9])
```

```python
import math

import jax
import jax.numpy as jnp
from jax import lax
from jax.sharding import Mesh, PartitionSpec as P

MODEL_WIDTH = 1536
QUERY_HEADS = 24
KEY_VALUE_HEADS = 8
HEAD_SIZE = 64
E = 40
TOPK = 8
SLICES = 4
LANES = 128

ALL = ("y", "c", "z", "x")
epsilon = 1e-05
F32 = jnp.float32
BF16 = jnp.bfloat16


def ring_step(array, axis):
    size = lax.axis_size(axis)
    return lax.ppermute(array, axis, [(i, (i + 1) % size) for i in range(size)])


def ring_gather(block, axis):
    blocks = [block]
    for _ in range(lax.axis_size(axis) - 1):
        blocks.append(ring_step(blocks[-1], axis))
    return blocks


def ring_sum(parts, axis, kind):
    total = parts[1]
    for part in parts[2:] + parts[:1]:
        total = (ring_step(total, axis).astype(F32) + part.astype(F32)).astype(kind)
    return total


def gather_group(block):
    chunks = []
    for own in ring_gather(block, "z"):
        rows = jnp.stack(ring_gather(own, "y"))
        chunks.append(jnp.concatenate(ring_gather(rows, "c")))
    return chunks


def sum_chunk(chunk, kind):
    halves = chunk.reshape((2, lax.axis_size("y")) + chunk.shape[1:])
    rows = ring_sum([halves[0], halves[1]], "c", kind)
    return ring_sum([rows[i] for i in range(rows.shape[0])], "y", kind)


def placed_gather(block, axis, position):
    size, index = lax.axis_size(axis), lax.axis_index(axis)
    whole = jnp.zeros(block.shape[:position] + (size,) + block.shape[position:], block.dtype)
    for step, part in enumerate(ring_gather(block, axis)):
        whole = lax.dynamic_update_index_in_dim(whole, part, (index - step) % size, position)
    return whole


def positions(lengths, count_of_tokens):
    seq_ends = jnp.cumsum(lengths, axis=-1)
    starts = seq_ends - lengths
    token_index = jnp.arange(count_of_tokens, dtype=jnp.int32)
    segment = jnp.sum((token_index[:, None] >= seq_ends[..., None, :]).astype(jnp.int32), axis=-1)
    choose = segment[..., None] == jnp.arange(lengths.shape[-1], dtype=jnp.int32)
    offset = jnp.sum(jnp.where(choose, starts[..., None, :], 0), axis=-1)
    return (segment, token_index - offset)


def rotary_embedding(values_in, token_position, direction):
    half_size = values_in.shape[-1] // 2
    frequency = jnp.exp(jnp.arange(half_size, dtype=F32) * (-math.log(10000.0) / half_size))
    angles = token_position.astype(F32)[..., None] * frequency
    cosine = jnp.cos(angles)[..., None, :]
    sine_part = jnp.sin(angles)[..., None, :]
    first_half = values_in[..., :half_size]
    second_half = values_in[..., half_size:]
    return jnp.concatenate(
        [
            first_half * cosine - direction * second_half * sine_part,
            second_half * cosine + direction * first_half * sine_part,
        ],
        axis=-1,
    )


def norm_back(grad_normed, values_in, inverse_root, gain):
    scaled = grad_normed * gain
    grad_gain = jnp.sum(grad_normed * values_in * inverse_root, axis=0)
    cubed = inverse_root * inverse_root * inverse_root
    grad_values = inverse_root * scaled - values_in * cubed * jnp.mean(
        scaled * values_in, axis=-1, keepdims=True
    )
    return (grad_values, grad_gain)


def dot(left, right, dims=((1,), (0,))):
    return lax.dot_general(left, right, (dims, ((), ())), preferred_element_type=F32)


def expert_chunk(rows_and_gates, grad_rows, w_in, w_back, local_count):
    count = rows_and_gates.shape[0]
    rows = rows_and_gates[:, :MODEL_WIDTH]
    high = rows_and_gates[:, MODEL_WIDTH : MODEL_WIDTH + E].astype(F32)
    low = rows_and_gates[:, MODEL_WIDTH + E : MODEL_WIDTH + 2 * E].astype(F32)
    group = lax.axis_index("y") * lax.axis_size("c") + lax.axis_index("c")
    gates = lax.dynamic_slice_in_dim(high + low, group * local_count, local_count, axis=1)
    gates = gates[..., None]
    hidden = dot(rows, w_in).reshape(count, local_count, 2, -1)
    gate_part, up_part = hidden[:, :, 0], hidden[:, :, 1]
    grad_plain = dot(grad_rows, w_back, ((1,), (1,))).reshape(gate_part.shape)
    sigmoid_gate = jax.nn.sigmoid(gate_part)
    active = gate_part * sigmoid_gate * up_part
    grad_gates = jnp.sum(active * grad_plain, axis=-1)
    weighted = (gates * active).astype(BF16).reshape(count, -1)
    grad_active = gates * grad_plain
    grad_gate = grad_active * up_part * sigmoid_gate * (1.0 + gate_part * (1.0 - sigmoid_gate))
    grad_up = grad_active * gate_part * sigmoid_gate
    grad_hidden = jnp.stack([grad_gate, grad_up], axis=2).astype(BF16).reshape(count, -1)
    result = dot(weighted, w_back).astype(BF16)
    grad_in = dot(grad_hidden, w_in, ((1,), (1,))).astype(BF16)
    return result, grad_in, grad_gates, weighted, grad_hidden


def body(
    inputs,
    cotangent,
    lengths,
    routes,
    norm_gain_one,
    w_query,
    key_projection_weight,
    value_projection_weight,
    w_out,
    norm_gain_two,
    w_router,
    w_gate,
    w_up,
    w_down,
):
    micro, block, _ = inputs.shape
    count = micro * block
    local_count = w_gate.shape[0]
    y_size, z_size, x_size = lax.axis_size("y"), lax.axis_size("z"), lax.axis_size("x")
    group = lax.axis_index("y") * lax.axis_size("c") + lax.axis_index("c")
    query_per_group = QUERY_HEADS // KEY_VALUE_HEADS
    kv_width = KEY_VALUE_HEADS * HEAD_SIZE
    score_scale = 1.0 / math.sqrt(HEAD_SIZE)

    small = jnp.concatenate([w_router, norm_gain_one[:, None], norm_gain_two[:, None]], axis=1)
    small = jnp.pad(small, ((0, 0), (0, LANES - small.shape[1])))
    mine = jnp.concatenate(
        [w_query, key_projection_weight, value_projection_weight, small], axis=1
    )
    whole = lax.all_gather(mine, ALL, axis=0, tiled=True)
    w_qkv = whole[:, : MODEL_WIDTH + 2 * kv_width]
    small = whole[:, MODEL_WIDTH + 2 * kv_width :]
    w_router = small[:, :E]
    gain_first = small[:, E].astype(F32)
    gain_second = small[:, E + 1].astype(F32)
    w_out = lax.all_gather(w_out, ALL, axis=0, tiled=True)

    w_in = jnp.stack([w_gate, w_up])
    own_rows = w_in.shape[2]
    w_in = w_in.reshape(2, local_count, own_rows, z_size, -1)
    hidden_slice = w_in.shape[-1]
    w_in = w_in.transpose(3, 2, 1, 0, 4).reshape(z_size, own_rows, -1)
    w_in = lax.all_to_all(w_in, "z", 0, 0, tiled=True)
    w_in = placed_gather(w_in, "x", 1).reshape(MODEL_WIDTH, -1)
    w_back = placed_gather(w_down, "x", 1).reshape(-1, MODEL_WIDTH)

    act_rows = inputs.reshape(count, MODEL_WIDTH).astype(F32)
    grad_final_low = cotangent.reshape(count, MODEL_WIDTH)
    grad_final = grad_final_low.astype(F32)
    grad_chunks = gather_group(grad_final_low)
    r_one = lax.rsqrt(jnp.mean(act_rows * act_rows, axis=-1, keepdims=True) + epsilon)
    normalized_input = (act_rows * r_one * gain_first).astype(BF16)
    qkv = dot(normalized_input, w_qkv)
    segment, token_position = positions(lengths[:, 0], block)
    query_pre = qkv[:, :MODEL_WIDTH].reshape(micro, block, QUERY_HEADS, HEAD_SIZE)
    key_pre = qkv[:, MODEL_WIDTH : MODEL_WIDTH + kv_width]
    key_pre = key_pre.reshape(micro, block, KEY_VALUE_HEADS, HEAD_SIZE)
    values = qkv[:, MODEL_WIDTH + kv_width :].astype(BF16)
    values = values.reshape(micro, block, KEY_VALUE_HEADS, HEAD_SIZE)
    query = rotary_embedding(query_pre, token_position, 1.0).astype(BF16)
    query = query.reshape(micro, block, KEY_VALUE_HEADS, query_per_group, HEAD_SIZE)
    keys = rotary_embedding(key_pre, token_position, 1.0).astype(BF16)
    token_index = jnp.arange(block, dtype=jnp.int32)
    allowed = (segment[:, :, None] == segment[:, None, :]) & (
        token_index[:, None] >= token_index[None, :]
    )
    scores = jnp.einsum("bqkgd,bskd->bkgqs", query, keys, preferred_element_type=F32)
    scores = jnp.where(allowed[:, None, None], scores * score_scale, -1000000000.0)
    probs = jax.nn.softmax(scores, axis=-1)
    probs_low = probs.astype(BF16)
    mixed = jnp.einsum("bkgqs,bskd->bqkgd", probs_low, values, preferred_element_type=F32)
    mixed = mixed.reshape(count, MODEL_WIDTH).astype(BF16)
    resid = act_rows + dot(mixed, w_out)

    r_two = lax.rsqrt(jnp.mean(resid * resid, axis=-1, keepdims=True) + epsilon)
    normed_two = (resid * r_two * gain_second).astype(BF16)
    chance = jax.nn.softmax(dot(normed_two, w_router), axis=-1)
    choice = routes.reshape(count, TOPK)
    chosen = jnp.any(choice[..., None] == jnp.arange(E, dtype=jnp.int32), axis=1).astype(F32)
    picked = chance * chosen
    picked_total = jnp.sum(picked, axis=-1, keepdims=True)
    gates = picked / picked_total

    high = lax.reduce_precision(gates, 8, 7)
    low = gates - high
    spare = jnp.zeros((count, LANES - 2 * E), BF16)
    sent = jnp.concatenate([normed_two, high.astype(BF16), low.astype(BF16), spare], axis=1)
    sent_chunks = gather_group(sent)
    results, grads_in, grads_gates, weighted, grad_hidden = [], [], [], [], []
    for sent_chunk, grad_chunk in zip(sent_chunks, grad_chunks):
        parts = expert_chunk(
            sent_chunk.reshape(-1, sent_chunk.shape[-1]),
            grad_chunk.reshape(-1, MODEL_WIDTH),
            w_in,
            w_back,
            local_count,
        )
        shape = (-1, count, MODEL_WIDTH)
        results.append(sum_chunk(parts[0].reshape(shape), BF16))
        grads_in.append(sum_chunk(parts[1].reshape(shape), BF16))
        spread = jnp.zeros((parts[2].shape[0], E), F32)
        spread = lax.dynamic_update_slice(spread, parts[2], (0, group * local_count))
        grads_gates.append(sum_chunk(spread.reshape(-1, count, E), F32))
        weighted.append(parts[3])
        grad_hidden.append(parts[4])
    outputs = resid + ring_sum(results, "z", F32)
    grad_experts = ring_sum(grads_in, "z", F32)
    grad_gates = ring_sum(grads_gates, "z", F32)

    all_rows = jnp.concatenate(sent_chunks).reshape(-1, sent.shape[1])[:, :MODEL_WIDTH]
    all_grads = jnp.concatenate(grad_chunks).reshape(-1, MODEL_WIDTH)
    grad_w_in = dot(all_rows, jnp.concatenate(grad_hidden), ((0,), (0,))).astype(BF16)
    grad_w_back = dot(jnp.concatenate(weighted), all_grads, ((0,), (0,))).astype(BF16)
    x_index = lax.axis_index("x")

    def sum_x(parts, position, kind):
        ordered = [
            lax.dynamic_index_in_dim(parts, (x_index - step) % x_size, position, keepdims=False)
            for step in range(x_size)
        ]
        return ring_sum(ordered, "x", kind)

    grad_w_in = sum_x(grad_w_in.reshape(z_size, x_size, own_rows, -1), 1, BF16)
    grad_w_in = lax.all_to_all(grad_w_in, "z", 0, 0, tiled=True)
    grad_w_in = grad_w_in.reshape(z_size, own_rows, local_count, 2, hidden_slice)
    grad_w_in = grad_w_in.transpose(3, 2, 1, 0, 4).reshape(2, local_count, own_rows, -1)
    grad_w_in = grad_w_in.astype(F32)
    grad_w_down = sum_x(grad_w_back.reshape(local_count, x_size, -1, MODEL_WIDTH), 1, F32)

    grad_picked = grad_gates * chosen
    grad_picked = grad_picked - chosen * jnp.sum(grad_gates * gates, axis=-1, keepdims=True)
    grad_chance = grad_picked / picked_total
    grad_logits = (
        chance * (grad_chance - jnp.sum(chance * grad_chance, axis=-1, keepdims=True))
    ).astype(BF16)
    grad_w_router = dot(normed_two, grad_logits, ((0,), (0,)))
    grad_normed_two = grad_experts + dot(grad_logits, w_router, ((1,), (1,)))
    grad_resid, grad_gain_two = norm_back(grad_normed_two, resid, r_two, gain_second)
    grad_resid = grad_final + grad_resid

    grad_att = grad_resid.astype(BF16)
    grad_w_out = dot(mixed, grad_att, ((0,), (0,))).astype(BF16)
    grad_w_out = lax.psum_scatter(grad_w_out, ALL, scatter_dimension=0, tiled=True)
    grad_mixed = dot(grad_att, w_out, ((1,), (1,))).astype(BF16).reshape(query.shape)
    grad_probs = jnp.einsum("bqkgd,bskd->bkgqs", grad_mixed, values, preferred_element_type=F32)
    grad_value_pre = jnp.einsum(
        "bkgqs,bqkgd->bskd", probs_low, grad_mixed, preferred_element_type=F32
    )
    grad_value_pre = grad_value_pre.reshape(count, kv_width).astype(BF16)
    grad_scores = (
        probs * (grad_probs - jnp.sum(probs * grad_probs, axis=-1, keepdims=True))
    ).astype(BF16)
    grad_query = jnp.einsum("bkgqs,bskd->bqkgd", grad_scores, keys, preferred_element_type=F32)
    grad_keys = jnp.einsum("bkgqs,bqkgd->bskd", grad_scores, query, preferred_element_type=F32)
    grad_query_pre = rotary_embedding(
        (grad_query * score_scale).reshape(query_pre.shape), token_position, -1.0
    )
    grad_key_pre = rotary_embedding(grad_keys * score_scale, token_position, -1.0)
    grad_qkv = jnp.concatenate(
        [
            grad_query_pre.reshape(count, MODEL_WIDTH).astype(BF16),
            grad_key_pre.reshape(count, kv_width).astype(BF16),
            grad_value_pre,
        ],
        axis=1,
    )
    grad_w_qkv = dot(normalized_input, grad_qkv, ((0,), (0,))).astype(BF16)
    grad_normed = dot(grad_qkv, w_qkv, ((1,), (1,)))
    grad_rows, grad_gain_one = norm_back(grad_normed, act_rows, r_one, gain_first)
    grad_rows = grad_resid + grad_rows

    grad_small = jnp.concatenate(
        [grad_w_router, grad_gain_one[:, None], grad_gain_two[:, None]], axis=1
    )
    grad_small = jnp.pad(grad_small, ((0, 0), (0, LANES - grad_small.shape[1])))
    grad_mine = jnp.concatenate([grad_w_qkv, grad_small.astype(BF16)], axis=1)
    grad_mine = lax.psum_scatter(grad_mine, ALL, scatter_dimension=0, tiled=True).astype(F32)
    grad_small = grad_mine[:, MODEL_WIDTH + 2 * kv_width :]
    return (
        outputs.astype(BF16).reshape(inputs.shape),
        grad_rows.reshape(inputs.shape),
        grad_small[:, E],
        grad_mine[:, :MODEL_WIDTH],
        grad_mine[:, MODEL_WIDTH : MODEL_WIDTH + kv_width],
        grad_mine[:, MODEL_WIDTH + kv_width : MODEL_WIDTH + 2 * kv_width],
        grad_w_out.astype(F32),
        grad_small[:, E + 1],
        grad_small[:, :E],
        grad_w_in[0],
        grad_w_in[1],
        grad_w_down,
    )


def solution(mesh):
    experts, shards = mesh.shape["expert"], mesh.shape["shard"]
    split = Mesh(
        mesh.devices.reshape(experts // 2, 2, SLICES, shards // SLICES), ("y", "c", "z", "x")
    )
    groups, within = ("y", "c"), ("z", "x")
    tokens = P(None, ALL, None)
    rows = P(ALL, None)
    expert = P(groups, within, None)
    return jax.shard_map(
        body,
        mesh=split,
        in_specs=(tokens,) * 4
        + (P(ALL), rows, rows, rows, rows, P(ALL), rows, expert, expert, expert),
        out_specs=(tokens, tokens, P(ALL), rows, rows, rows, rows, P(ALL), rows)
        + (expert, expert, expert),
        check_vma=False,
    )
```

```python
import functools
import itertools
import math

import jax
import jax.numpy as jnp
from jax import lax
from jax.experimental import pallas as pl
from jax.experimental.pallas import tpu as pltpu
from jax.sharding import Mesh, PartitionSpec as P

MODEL_WIDTH = 1536
QUERY_HEADS = 24
KEY_VALUE_HEADS = 8
HEAD_SIZE = 64
QUERY_PER_GROUP = QUERY_HEADS // KEY_VALUE_HEADS
E = 40
TOPK = 8
SLICES = 4
LANES = 128
VMEM_BYTES = 60 * 1024 * 1024

ALL = ("y", "c", "z", "x")
epsilon = 1e-05
F32 = jnp.float32
BF16 = jnp.bfloat16


def dot(left, right, dims=((1,), (0,))):
    return lax.dot_general(left, right, (dims, ((), ())), preferred_element_type=F32)


def sync(*values):
    return lax.optimization_barrier(values)


def ring_step(array, axis):
    size = lax.axis_size(axis)
    return lax.ppermute(array, axis, [(i, (i + 1) % size) for i in range(size)])


def ring_gather(block, axis):
    blocks = [block]
    for _ in range(lax.axis_size(axis) - 1):
        blocks.append(ring_step(blocks[-1], axis))
    return blocks


def ring_sum(parts, axis, kind):
    total = parts[1]
    for part in list(parts[2:]) + [parts[0]]:
        total = ring_step(total, axis).astype(F32) + part.astype(F32)
        total = total.astype(kind if part is parts[0] else part.dtype)
    return total


def index_at(axis, step):
    return (lax.axis_index(axis) - step) % lax.axis_size(axis)


def move_kernel(moves, count_in, count_out, place_ref, *refs):
    sources, targets = refs[:count_in], refs[count_in : count_in + count_out]
    held, sems = refs[count_in + count_out : -1], refs[-1]
    copies = [[] for _ in targets]
    for number, (source, from_index, target, to_index) in enumerate(moves):
        picked = [
            tuple(place_ref[i[0]] if isinstance(i, tuple) else i for i in index)
            for index in (from_index, to_index)
        ]
        copy = pltpu.make_async_copy(
            sources[source].at[picked[0]], held[target].at[picked[1]], sems.at[number]
        )
        copy.start()
        copies[target].append(copy)
    out = []
    for target, arriving in enumerate(copies):
        for copy in arriving:
            copy.wait()
        out.append(
            pltpu.make_async_copy(held[target], targets[target], sems.at[len(moves) + target])
        )
        out[-1].start()
    for copy in out:
        copy.wait()


def move(moves, places, sources, shapes, name):
    anywhere = pl.BlockSpec(memory_space=pl.ANY)
    total = sum(math.prod(s.shape) * s.dtype.itemsize for s in shapes)
    return pl.pallas_call(
        functools.partial(move_kernel, moves, len(sources), len(shapes)),
        in_specs=[pl.BlockSpec(memory_space=pltpu.SMEM)] + [anywhere] * len(sources),
        out_specs=[anywhere] * len(shapes),
        out_shape=shapes,
        scratch_shapes=[pltpu.VMEM(s.shape, s.dtype) for s in shapes]
        + [pltpu.SemaphoreType.DMA((len(moves) + len(shapes),))],
        compiler_params=pltpu.CompilerParams(vmem_limit_bytes=VMEM_BYTES // 3),
        cost_estimate=pl.CostEstimate(flops=0, bytes_accessed=2 * total, transcendentals=0),
        name=name,
    )(jnp.stack(places).astype(jnp.int32), *sources)


def places_of(axes):
    places, where = [], {}
    for axis in axes:
        for step in range(lax.axis_size(axis)):
            where[axis, step] = (len(places),)
            places.append(index_at(axis, step))
    return places, where


def place_weights(gathers):
    places, where = places_of(("y", "z", "x"))
    sizes = [lax.axis_size(axis) for axis in ("y", "z", "x")]
    moves, sources, shapes = [], [], []
    for number, blocks in enumerate(gathers):
        for (y_step, z_first, x_step), part in blocks.items():
            for i in range(part.shape[0]):
                spot = (where["y", y_step], slice(None), where["z", z_first + i], where["x", x_step])
                moves.append((len(sources), (i,), number, spot))
            sources.append(part)
        shape = (sizes[0], 2) + tuple(sizes[1:]) + sources[-1].shape[2:]
        shapes.append(jax.ShapeDtypeStruct(shape, sources[-1].dtype))
    whole = move(moves, places, sources, shapes, "place_weights")
    return [part.reshape(-1, part.shape[-1]) for part in whole]


def pick_weights(grad, first, second, with_core):
    sizes = {axis: lax.axis_size(axis) for axis in ("y", "z", "x")}
    core = (2,) if with_core else ()
    shape = (sizes["y"],) + core + (sizes["z"], sizes["x"], -1, grad.shape[-1])
    grad = grad.reshape(shape)
    places, where = places_of(("y", "z", "x"))
    moves = []
    for y_step, z_step, x_step in itertools.product(
        range(sizes["y"]), range(sizes["z"]), range(sizes["x"])
    ):
        spot = [where["y", y_step], where["z", z_step], where["x", x_step]]
        if with_core:
            spot.insert(1, slice(None))
        steps = {"y": y_step, "x": x_step}
        moves.append((0, tuple(spot), steps[second], (steps[first], z_step)))
    tail = core + grad.shape[-2:]
    shape = jax.ShapeDtypeStruct((sizes[first], sizes["z"]) + tail, grad.dtype)
    return move(moves, places, [grad], [shape] * sizes[second], "pick_weights")


def sum_along(parts, axis, kind=BF16):
    return ring_sum([parts[i] for i in range(parts.shape[0])], axis, kind)


def pack_kernel(gate_ref, up_ref, out_ref):
    width = out_ref.shape[-1] // 2
    for z in range(out_ref.shape[0]):
        out_ref[z, :, :width] = gate_ref[0, :, z * width : (z + 1) * width]
        out_ref[z, :, width:] = up_ref[0, :, z * width : (z + 1) * width]


def pack_experts(w_gate, w_up, first, last, slices):
    rows, hidden = w_gate.shape[1:]
    spec = pl.BlockSpec((1, rows, hidden), lambda e: (first + e, 0, 0))
    width = 2 * hidden // slices
    return pl.pallas_call(
        pack_kernel,
        grid=(last - first,),
        in_specs=[spec, spec],
        out_specs=pl.BlockSpec((slices, rows, width), lambda e: (0, 0, e)),
        out_shape=jax.ShapeDtypeStruct((slices, rows, (last - first) * width), w_gate.dtype),
        name="pack_experts",
    )(w_gate, w_up)


def unpack_kernel(counts, slices, place_ref, *refs):
    parts, (gate_ref, up_ref) = refs[:-2], refs[-2:]
    expert = pl.program_id(0)
    width = gate_ref.shape[-1] // slices
    first = 0
    for which, count in enumerate(counts):

        @pl.when((expert >= first) & (expert < first + count))
        def _(which=which, first=first):
            start = pl.multiple_of((expert - first) * 2 * width, 2 * width)
            for step in range(slices):
                both = parts[which * slices + step][:, pl.ds(start, 2 * width)].astype(F32)
                spot = pl.multiple_of(place_ref[step] * width, width)
                gate_ref[0, :, pl.ds(spot, width)] = both[:, :width]
                up_ref[0, :, pl.ds(spot, width)] = both[:, width:]

        first = first + count


def unpack_experts(parts, counts):
    places, _ = places_of(("z",))
    slices, local_count = len(parts[0]), sum(counts)
    rows, columns = parts[0][0].shape
    hidden = columns // (2 * counts[0]) * slices
    flat = [part for half in parts for part in half]
    spec = pl.BlockSpec((1, rows, hidden), lambda e: (e, 0, 0))
    whole = [pl.BlockSpec(part.shape, lambda e: (0, 0)) for part in flat]
    shape = jax.ShapeDtypeStruct((local_count, rows, hidden), F32)
    return pl.pallas_call(
        functools.partial(unpack_kernel, counts, slices),
        grid=(local_count,),
        in_specs=[pl.BlockSpec(memory_space=pltpu.SMEM)] + whole,
        out_specs=[spec, spec],
        out_shape=[shape, shape],
        compiler_params=pltpu.CompilerParams(vmem_limit_bytes=VMEM_BYTES),
        name="unpack_experts",
    )(jnp.stack(places).astype(jnp.int32), *flat)


def experts_kernel(counts, steps, x_size, place_ref, *refs):
    parts = len(counts)
    rows_in, grads_in, refs = refs[:steps], refs[steps : 2 * steps], refs[2 * steps :]
    w_in_parts, refs = [refs[i * x_size : (i + 1) * x_size] for i in range(parts)], refs[parts * x_size :]
    w_back_parts, refs = [refs[i * x_size : (i + 1) * x_size] for i in range(parts)], refs[parts * x_size :]
    results, grads, (active_ref, hidden_ref, gates_ref) = refs[:2], refs[2:4], refs[4:7]
    rows_buf, grads_buf = refs[7:9]
    w_in, w_back, sems = refs[9 : 9 + parts], refs[9 + parts], refs[10 + parts]
    step = pl.program_id(0)
    half = steps // 2
    weights, late = [], [[] for _ in range(steps)]
    number = 0

    def copy_of(source, target):
        nonlocal number
        number = number + 1
        return pltpu.make_async_copy(source, target, sems.at[number - 1])

    first = 0
    for part, count in enumerate(counts):
        for x_step in range(x_size):
            place = place_ref[1 + x_step]
            source = w_in_parts[part][x_step]
            size = source.shape[1]
            for z in range(source.shape[0]):
                start = pl.multiple_of((z * x_size + place) * size, size)
                weights.append(copy_of(source.at[z], w_in[part].at[pl.ds(start, size)]))
            source = w_back_parts[part][x_step]
            size = source.shape[1]
            for e in range(count):
                start = pl.multiple_of(((first + e) * x_size + place) * size, size)
                weights.append(copy_of(source.at[e], w_back.at[pl.ds(start, size)]))
        first = first + count
    for i in range(steps):
        late[i] = [copy_of(rows_in[i], rows_buf.at[i]), copy_of(grads_in[i], grads_buf.at[i])]

    @pl.when(step == 0)
    def _():
        for copy in late[0] + weights + [copy for some in late[1:] for copy in some]:
            copy.start()
        for copy in weights:
            copy.wait()

    for i in range(steps):

        @pl.when(step == i)
        def _(i=i):
            for copy in late[i]:
                copy.wait()

    local_count = sum(counts)
    width = w_back.shape[0] // local_count
    rows = rows_buf[step, :, :MODEL_WIDTH]
    grad_rows = grads_buf[step]
    first = place_ref[0] * local_count
    source = lax.broadcasted_iota(jnp.int32, (LANES, LANES), 0)
    wanted = lax.broadcasted_iota(jnp.int32, (LANES, LANES), 1) + first
    choose = ((source == wanted) | (source == wanted + E)).astype(F32).astype(BF16)
    gates = dot(rows_buf[step, :, MODEL_WIDTH:], choose)
    lane = lax.broadcasted_iota(jnp.int32, gates.shape, 1)
    grad_gates = jnp.zeros(gates.shape, F32)
    expert = 0
    for part, count in enumerate(counts):
        for i in range(count):
            here = slice(expert * width, (expert + 1) * width)
            hidden = dot(rows, w_in[part][:, 2 * width * i : 2 * width * (i + 1)])
            grad_plain = dot(grad_rows, w_back[here, :], ((1,), (1,)))
            gate_part, up_part = hidden[:, :width], hidden[:, width:]
            sigmoid_gate = 1.0 / (1.0 + jnp.exp(-gate_part))
            silu = gate_part * sigmoid_gate
            active = silu * up_part
            weight = gates[:, expert : expert + 1]
            total = jnp.sum(active * grad_plain, axis=1, keepdims=True)
            grad_gates = jnp.where(lane == expert, total, grad_gates)
            active_ref[:, here] = (weight * active).astype(BF16)
            grad_active = weight * grad_plain
            start = 2 * width * expert
            hidden_ref[:, start : start + width] = (
                grad_active * up_part * (sigmoid_gate + silu * (1.0 - sigmoid_gate))
            ).astype(BF16)
            hidden_ref[:, start + width : start + 2 * width] = (grad_active * silu).astype(BF16)
            expert = expert + 1
    gates_ref[...] = grad_gates
    result = dot(active_ref[...], w_back[...]).astype(BF16)
    grad_in = jnp.zeros(rows.shape, F32)
    start = 0
    for part, count in enumerate(counts):
        size = 2 * width * count
        grad_in += dot(hidden_ref[:, start : start + size], w_in[part][...], ((1,), (1,)))
        start = start + size
    grad_in = grad_in.astype(BF16)

    for side, now in enumerate((step < half, step >= half)):

        @pl.when(now)
        def _(side=side):
            results[side][0] = result
            grads[side][0] = grad_in


def run_experts(rows, grads, w_in_parts, w_back_parts, counts, group):
    count, wide = rows[0].shape
    steps = len(rows)
    half = steps // 2
    local_count = sum(counts)
    x_size = len(w_in_parts[0])
    z_size, own_rows, columns = w_in_parts[0][0].shape
    width = columns // (2 * counts[0])
    copies = 2 * steps + x_size * (len(counts) * z_size + local_count)
    places, _ = places_of(("x",))
    anywhere = pl.BlockSpec(memory_space=pl.ANY)
    own = pl.BlockSpec((1, count, MODEL_WIDTH), lambda i: (jnp.minimum(i, half - 1), 0, 0))
    other = pl.BlockSpec((1, count, MODEL_WIDTH), lambda i: (jnp.maximum(i - half, 0), 0, 0))

    def by_row(columns):
        return pl.BlockSpec((count, columns), lambda i: (i, 0))

    side = jax.ShapeDtypeStruct((half, count, MODEL_WIDTH), BF16)
    flops = 2 * steps * count * MODEL_WIDTH * 6 * local_count * width
    return pl.pallas_call(
        functools.partial(experts_kernel, counts, steps, x_size),
        grid=(steps,),
        in_specs=[pl.BlockSpec(memory_space=pltpu.SMEM)]
        + [anywhere] * (2 * steps + 2 * len(counts) * x_size),
        out_specs=[own, other, own, other]
        + [by_row(local_count * width), by_row(2 * local_count * width), by_row(LANES)],
        out_shape=[side] * 4
        + [
            jax.ShapeDtypeStruct((steps * count, local_count * width), BF16),
            jax.ShapeDtypeStruct((steps * count, 2 * local_count * width), BF16),
            jax.ShapeDtypeStruct((steps * count, LANES), F32),
        ],
        scratch_shapes=[
            pltpu.VMEM((steps, count, wide), BF16),
            pltpu.VMEM((steps, count, MODEL_WIDTH), BF16),
        ]
        + [pltpu.VMEM((MODEL_WIDTH, part[0].shape[-1]), BF16) for part in w_in_parts]
        + [
            pltpu.VMEM((local_count * width, MODEL_WIDTH), BF16),
            pltpu.SemaphoreType.DMA((copies,)),
        ],
        compiler_params=pltpu.CompilerParams(vmem_limit_bytes=VMEM_BYTES),
        cost_estimate=pl.CostEstimate(
            flops=flops, bytes_accessed=30 * 1024 * 1024, transcendentals=0
        ),
        name="experts",
    )(
        jnp.stack([group] + places).astype(jnp.int32),
        *rows,
        *grads,
        *[part for parts in w_in_parts for part in parts],
        *[part for parts in w_back_parts for part in parts],
    )


def expert_grads_kernel(count_left, count_right, back, place_ref, *refs):
    whole = refs[:count_left]
    columns = refs[count_left : count_left + count_right]
    outs, (buf, total, sems) = refs[count_left + count_right : -3], refs[-3:]
    rows_each = whole[0].shape[0]

    @pl.when(pl.program_id(0) == 0)
    def _():
        copies = [
            pltpu.make_async_copy(
                part.at[:, pl.ds(0, MODEL_WIDTH)],
                buf.at[pl.ds(number * rows_each, rows_each)],
                sems.at[number],
            )
            for number, part in enumerate(whole)
        ]
        for copy in copies:
            copy.start()
        for copy in copies:
            copy.wait()

    size = columns[0].shape[0]
    for i, part in enumerate(columns):
        rows = buf[i * size : (i + 1) * size, :]
        if back:
            term = dot(part[...], rows, ((0,), (0,)))
        else:
            term = dot(rows, part[...], ((0,), (0,)))
        if i == 0:
            total[...] = term
        else:
            total[...] += term
    blocks, own = outs[0].shape[0], outs[0].shape[1]
    for step, out in enumerate(outs):
        for i in range(blocks):
            block = i if back else place_ref[len(outs) + (blocks - i) % blocks]
            start = pl.multiple_of((block * len(outs) + place_ref[step]) * own, own)
            out[i] = total[pl.ds(start, own), :].astype(BF16)


def expert_grads(whole, columns, first, last, width, back):
    x_size = lax.axis_size("x")
    places, _ = places_of(("x",) if back else ("x", "z"))
    tokens = len(whole) * whole[0].shape[0]
    experts = last - first
    anywhere = pl.BlockSpec(memory_space=pl.ANY)
    column = pl.BlockSpec((columns[0].shape[0], width), lambda e: (0, first + e))
    if back:
        own = width // x_size
        block = (1, own, MODEL_WIDTH)
        shape = (experts, own, MODEL_WIDTH)
        out = pl.BlockSpec(block, lambda e: (e, 0, 0))
        total = (width, MODEL_WIDTH)
    else:
        z_size = lax.axis_size("z")
        own = MODEL_WIDTH // (z_size * x_size)
        shape = (z_size, own, experts * width)
        out = pl.BlockSpec((z_size, own, width), lambda e: (0, 0, e))
        total = (MODEL_WIDTH, width)
    return pl.pallas_call(
        functools.partial(expert_grads_kernel, len(whole), len(columns), back),
        grid=(experts,),
        in_specs=[pl.BlockSpec(memory_space=pltpu.SMEM)]
        + [anywhere] * len(whole)
        + [column] * len(columns),
        out_specs=[out] * x_size,
        out_shape=[jax.ShapeDtypeStruct(shape, BF16)] * x_size,
        scratch_shapes=[
            pltpu.VMEM((tokens, MODEL_WIDTH), BF16),
            pltpu.VMEM(total, F32),
            pltpu.SemaphoreType.DMA((len(whole),)),
        ],
        compiler_params=pltpu.CompilerParams(vmem_limit_bytes=VMEM_BYTES),
        cost_estimate=pl.CostEstimate(
            flops=2 * tokens * MODEL_WIDTH * width * experts,
            bytes_accessed=2 * tokens * (MODEL_WIDTH + width * experts),
            transcendentals=0,
        ),
        name="expert_grads",
    )(jnp.stack(places).astype(jnp.int32), *whole, *columns)


def positions(lengths, count_of_tokens):
    seq_ends = jnp.cumsum(lengths, axis=-1)
    starts = seq_ends - lengths
    token_index = jnp.arange(count_of_tokens, dtype=jnp.int32)
    segment = jnp.sum((token_index[:, None] >= seq_ends[..., None, :]).astype(jnp.int32), axis=-1)
    choose = segment[..., None] == jnp.arange(lengths.shape[-1], dtype=jnp.int32)
    offset = jnp.sum(jnp.where(choose, starts[..., None, :], 0), axis=-1)
    return (segment, token_index - offset)


def rotary_embedding(values_in, token_position, direction):
    half_size = values_in.shape[-1] // 2
    frequency = jnp.exp(jnp.arange(half_size, dtype=F32) * (-math.log(10000.0) / half_size))
    angles = token_position.astype(F32)[..., None] * frequency
    cosine = jnp.cos(angles)[..., None, :]
    sine_part = jnp.sin(angles)[..., None, :]
    first_half = values_in[..., :half_size]
    second_half = values_in[..., half_size:]
    return jnp.concatenate(
        [
            first_half * cosine - direction * second_half * sine_part,
            second_half * cosine + direction * first_half * sine_part,
        ],
        axis=-1,
    )


def norm_back(grad_normed, values_in, inverse_root, gain):
    scaled = grad_normed * gain
    grad_gain = jnp.sum(grad_normed * values_in * inverse_root, axis=0)
    cubed = inverse_root * inverse_root * inverse_root
    grad_values = inverse_root * scaled - values_in * cubed * jnp.mean(
        scaled * values_in, axis=-1, keepdims=True
    )
    return (grad_values, grad_gain)


def body(
    inputs,
    cotangent,
    lengths,
    routes,
    norm_gain_one,
    w_query,
    key_projection_weight,
    value_projection_weight,
    w_out,
    norm_gain_two,
    w_router,
    w_gate,
    w_up,
    w_down,
):
    micro, block, _ = inputs.shape
    count = micro * block
    local_count = w_gate.shape[0]
    y_size, z_size, x_size = lax.axis_size("y"), lax.axis_size("z"), lax.axis_size("x")
    core = lax.axis_index("c")
    group = lax.axis_index("y") * 2 + core
    score_scale = 1.0 / math.sqrt(HEAD_SIZE)
    own_rows = w_query.shape[0]
    q_width, kv_width = MODEL_WIDTH // 2, KEY_VALUE_HEADS * HEAD_SIZE // 2
    kv_heads = KEY_VALUE_HEADS // 2

    def columns_of(weight, which):
        split = weight.reshape(own_rows, y_size, 2, -1)
        return lax.dynamic_index_in_dim(split, which, 2, keepdims=False).reshape(own_rows, -1)

    small = jnp.concatenate([w_router, norm_gain_one[:, None], norm_gain_two[:, None]], axis=1)
    small = jnp.pad(small, ((0, 0), (0, LANES - small.shape[1])))

    def both_cores(arrays):
        mine = jnp.concatenate([columns_of(a, core) for a in arrays], axis=1)
        theirs = jnp.concatenate([columns_of(a, 1 - core) for a in arrays], axis=1)
        return mine, theirs

    mine, theirs = both_cores([w_query, key_projection_weight, value_projection_weight])
    got = ring_step(jnp.concatenate([theirs, small], axis=1), "c")
    mine = jnp.concatenate([mine, small], axis=1)
    both = jnp.where(core == 0, jnp.stack([mine, got]), jnp.stack([got, mine]))
    both = jnp.concatenate(
        [
            both[..., : q_width + kv_width],
            both[..., q_width + 2 * kv_width :],
            both[..., q_width + kv_width : q_width + 2 * kv_width],
            jnp.stack([w_out[:, :q_width], w_out[:, q_width:]]),
        ],
        axis=-1,
    )
    counts = [local_count // 2, local_count - local_count // 2]
    ranges = [(0, counts[0]), (counts[0], local_count)]
    packed = [pack_experts(w_gate, w_up, first, last, z_size) for first, last in ranges]
    grad_final_low = cotangent.reshape(count, MODEL_WIDTH)
    grads_z = [grad_final_low]
    down = [w_down[first:last] for first, last in ranges]
    both, grads_ahead, grads_first = sync(
        both, ring_step(grad_final_low, "z"), ring_gather(grad_final_low, "y")
    )
    grads_z.append(grads_ahead)
    grads_y = [grads_first]
    pair = z_size // 2
    first_width = q_width + kv_width + LANES
    first_blocks, second_blocks = {}, {}

    def first_hops(blocks):
        rows = jnp.stack(blocks)
        return ring_gather(rows[..., :first_width], "x"), ring_gather(rows[..., first_width:], "y")

    def second_hops(by_x, by_y, z_first):
        for x_step, one in enumerate(by_x):
            for y_step, two in enumerate(ring_gather(one, "y")):
                first_blocks[y_step, z_first, x_step] = two
        for y_step, one in enumerate(by_y):
            for x_step, two in enumerate(ring_gather(one, "x")):
                second_blocks[y_step, z_first, x_step] = two

    z_blocks = [both]
    for _ in range(pair - 1):
        z_blocks.append(ring_step(z_blocks[-1], "z"))
    others = [ring_step(inputs, "c"), ring_step(lengths, "c")]
    z_blocks, others, packed, grads_second, first_down = sync(
        z_blocks, others, packed, ring_gather(grads_z[1], "y"), ring_gather(down[0], "x")
    )
    other_inputs, other_lengths = others
    grads_y.append(grads_second)
    hops, ahead, grads_ahead, grads_other = sync(
        first_hops(z_blocks),
        ring_step(z_blocks[-1], "z"),
        ring_step(grads_z[1], "z"),
        [[ring_step(part, "c") for part in some] for some in grads_y],
    )
    grads_z.append(grads_ahead)
    second_hops(*hops, 0)
    z_blocks = [ahead]
    for _ in range(pair - 1):
        z_blocks.append(ring_step(z_blocks[-1], "z"))
    first_blocks, second_blocks, z_blocks, packed = sync(
        first_blocks, second_blocks, z_blocks, packed
    )
    swapped = lax.all_to_all(packed[0], "z", 0, 0, tiled=True)
    (hops,) = sync(first_hops(z_blocks))
    second_hops(*hops, pair)
    w_first, w_second = place_weights([first_blocks, second_blocks])
    w_qk = w_first[:, : q_width + kv_width]
    small = w_first[:, q_width + kv_width :]
    w_v = w_second[:, :kv_width]
    w_out = w_second[:, kv_width:].reshape(y_size, 2, -1, q_width).transpose(0, 2, 1, 3)
    w_out = w_out.reshape(q_width, MODEL_WIDTH)
    w_router = small[:, :E]
    gain_first = small[:, E].astype(F32)
    gain_second = small[:, E + 1].astype(F32)

    all_inputs = jnp.stack([inputs, other_inputs])
    all_lengths = jnp.concatenate([lengths[:, 0], other_lengths[:, 0]])
    act_rows = all_inputs.reshape(2 * count, MODEL_WIDTH).astype(F32)
    grad_final = grad_final_low.astype(F32)
    r_one = lax.rsqrt(jnp.mean(act_rows * act_rows, axis=-1) + epsilon)[:, None]
    normalized_input = (act_rows * r_one * gain_first).astype(BF16)
    segment, token_position = positions(all_lengths, block)
    blocks = 2 * micro
    qk_pre = dot(normalized_input, w_qk)
    values = dot(normalized_input, w_v).astype(BF16)
    qk_pre, values, swapped, packed, grads_z, down = sync(
        qk_pre, values, swapped, packed, grads_z, down
    )
    first_parts = ring_gather(swapped, "x")
    swapped = lax.all_to_all(packed[1], "z", 0, 0, tiled=True)
    grads_third = ring_gather(grads_z[2], "y")
    query_pre = qk_pre[:, :q_width]
    query_pre = query_pre.reshape(blocks, block, kv_heads * QUERY_PER_GROUP, HEAD_SIZE)
    key_pre = qk_pre[:, q_width:].reshape(blocks, block, kv_heads, HEAD_SIZE)
    values = values.reshape(blocks, block, kv_heads, HEAD_SIZE)
    query = rotary_embedding(query_pre, token_position, 1.0).astype(BF16)
    query = query.reshape(blocks, block, kv_heads, QUERY_PER_GROUP, HEAD_SIZE)
    keys = rotary_embedding(key_pre, token_position, 1.0).astype(BF16)
    token_index = jnp.arange(block, dtype=jnp.int32)
    allowed = (segment[:, :, None] == segment[:, None, :]) & (
        token_index[:, None] >= token_index[None, :]
    )
    scores = jnp.einsum("bqkgd,bskd->bkgqs", query, keys, preferred_element_type=F32)
    scores = jnp.where(allowed[:, None, None], scores * score_scale, -1000000000.0)
    probs = jax.nn.softmax(scores, axis=-1)
    probs_low = probs.astype(BF16)
    mixed = jnp.einsum("bkgqs,bskd->bqkgd", probs_low, values, preferred_element_type=F32)
    mixed = mixed.reshape(2 * count, q_width).astype(BF16)
    mixed, first_parts, swapped, grads_third = sync(mixed, first_parts, swapped, grads_third)
    grads_y.append(grads_third)
    second_parts = ring_gather(swapped, "x")
    grads_ahead = ring_step(grads_z[2], "z")
    projected = dot(mixed, w_out)
    own_act = act_rows[:count]
    resid = own_act + ring_sum([projected[:count], projected[count:]], "c", F32)

    r_two = lax.rsqrt(jnp.mean(resid * resid, axis=-1) + epsilon)[:, None]
    normed_two = (resid * r_two * gain_second).astype(BF16)
    chance = jax.nn.softmax(dot(normed_two, w_router), axis=-1)
    choice = routes.reshape(count, TOPK)
    chosen = jnp.any(choice[..., None] == jnp.arange(E, dtype=jnp.int32), axis=1).astype(F32)
    picked = chance * chosen
    picked_total = jnp.sum(picked, axis=-1, keepdims=True)
    gates = picked / picked_total

    high = lax.reduce_precision(gates, 8, 7)
    low = gates - high
    spare = jnp.zeros((count, LANES - 2 * E), BF16)
    sent = jnp.concatenate([normed_two, high.astype(BF16), low.astype(BF16), spare], axis=1)
    sent, grads_ahead, down = sync(sent, grads_ahead, down)
    grads_z.append(grads_ahead)
    rows, ahead, second_parts, second_down, others, grads_third = sync(
        ring_gather(sent, "y"),
        ring_step(sent, "z"),
        second_parts,
        ring_gather(down[1], "x"),
        ring_step(sent, "c"),
        [ring_step(part, "c") for part in grads_y[2]],
    )
    grads_other.append(grads_third)
    w_in_parts, w_back_parts = [first_parts, second_parts], [first_down, second_down]
    rows, others = sync(rows, [others] + [ring_step(part, "c") for part in rows[1:]])
    width = w_in_parts[0][0].shape[-1] // (2 * counts[0])

    def plus(first, second, kind=BF16):
        return (first.astype(F32) + second.astype(F32)).astype(kind)

    def plus_all(first, second):
        return [plus(first[i], second[i]) for i in range(y_size)]

    def hops_y(parts):
        return ring_step(parts[1], "y") if y_size == 2 else ring_sum(parts, "y", BF16)

    def end_y(parts, arrived):
        return plus(arrived, parts[0]) if y_size == 2 else arrived

    sent_chunks, grad_chunks, weighted, grad_hidden, grads_gates = [], [], [], [], []
    results_c, grads_c, results_sum, grads_sum = [], [], [], []
    for z_step in range(z_size):
        sent_chunks += rows + others
        grad_chunks += grads_y[z_step] + grads_other[z_step]
        parts = run_experts(
            rows + others,
            grads_y[z_step] + grads_other[z_step],
            w_in_parts,
            w_back_parts,
            counts,
            group,
        )
        moved = {}
        if z_step + 1 < z_size:
            moved["rows"] = ring_gather(ahead, "y")
            moved["others"] = ring_step(ahead, "c")
        if z_step + 2 < z_size:
            moved["ahead"] = ring_step(ahead, "z")
        if z_step == 0:
            moved["grads"] = ring_gather(grads_z[3], "y")
        if z_step == 1:
            moved["grads_other"] = [ring_step(part, "c") for part in grads_y[3]]
        if z_step >= 1:
            moved["grad"] = hops_y(grads_c[-1])
            moved["result"] = ring_step(last_results[1], "c")
        if z_step == 3:
            moved["step"] = ring_step(grads_sum[1], "z")
            moved["result_y"] = hops_y(results_c[0])
        parts, moved = sync(parts, moved)
        weighted.append(parts[4])
        grad_hidden.append(parts[5])
        grads_gates.append(parts[6][:, :local_count])
        if z_step == 0:
            grads_y.append(moved["grads"])
        if z_step == 1:
            grads_other.append(moved["grads_other"])
        arrived = ring_step(parts[3], "c")
        if z_step + 1 < z_size:
            ahead, rows = moved.get("ahead"), moved["rows"]
            others = [ring_step(part, "c") for part in rows[1:]]
        arrived, others, rows = sync(arrived, others, rows)
        others = [moved.get("others")] + others
        if z_step >= 1:
            grads_sum.append(end_y(grads_c[-1], moved["grad"]))
            results_c.append(plus_all(moved["result"], last_results[0]))
        grads_c.append(plus_all(arrived, parts[2]))
        last_results = parts[:2]

    total = plus(moved["step"], grads_sum[2])
    results_sum.append(end_y(results_c[0], moved["result_y"]))
    spread = jnp.stack(grads_gates)
    spread = lax.dynamic_update_slice(
        jnp.zeros(spread.shape[:2] + (E,), F32), spread, (0, 0, group * local_count)
    )
    spread = spread.reshape(z_size, 2, y_size, count, E)
    spread = ring_sum([spread[:, 0], spread[:, 1]], "c", F32)

    def in_grads(which):
        first, last = ranges[which]
        return expert_grads(sent_chunks, grad_hidden, first, last, 2 * width, False)

    def halves(part):
        middle = part.shape[0] // 2
        return part[:middle], part[middle:]

    grads_c, total, results_c, last_results, spread, grad_hidden = sync(
        grads_c, total, results_c, last_results, spread, grad_hidden
    )
    first_grads, last_grad, step, result_two, result_three, spread = sync(
        in_grads(0),
        hops_y(grads_c[3]),
        ring_step(total, "z"),
        hops_y(results_c[1]),
        ring_step(last_results[1], "c"),
        ring_sum([spread[:, i] for i in range(y_size)], "y", F32),
    )
    total = plus(step, end_y(grads_c[3], last_grad))
    results_sum.append(end_y(results_c[1], result_two))
    results_c.append(plus_all(result_three, last_results[0]))
    one, two = halves(first_grads[1])
    grad_hidden, total, results_sum, results_c, one, two = sync(
        grad_hidden, total, results_sum, results_c, one, two
    )
    second_grads, step, result_step, result_two, grad_gates, one = sync(
        in_grads(1),
        ring_step(total, "z"),
        ring_step(results_sum[1], "z"),
        hops_y(results_c[2]),
        ring_sum([spread[i] for i in range(z_size)], "z", F32),
        ring_step(one, "x"),
    )
    grad_experts = plus(step, grads_sum[0], F32)
    results_sum.append(end_y(results_c[2], result_two))
    result_total = plus(result_step, results_sum[2])
    result_total, grad_experts, two = sync(result_total, grad_experts, two)
    result_three = hops_y(results_c[3])
    two = ring_step(two, "x")

    def finish_x(parts, arrived, kind):
        rest = list(parts[2:]) + [parts[0]]
        total = plus(arrived, rest[0], kind)
        for part in rest[1:]:
            total = plus(ring_step(total, "x"), part, kind)
        return total

    def shift_pieces(total):
        pieces = [total[0]]
        for step in range(1, z_size):
            to = [(i, (i + step) % z_size) for i in range(z_size)]
            pieces.append(lax.ppermute(total[step], "z", to))
        return pieces

    grad_picked = chosen * (grad_gates - jnp.sum(grad_gates * gates, axis=-1, keepdims=True))
    grad_chance = grad_picked / picked_total
    grad_logits = (
        chance * (grad_chance - jnp.sum(chance * grad_chance, axis=-1, keepdims=True))
    ).astype(BF16)
    grad_w_router = dot(normed_two, grad_logits, ((0,), (0,)))
    grad_normed_two = grad_experts + dot(grad_logits, w_router, ((1,), (1,)))
    grad_resid, grad_gain_two = norm_back(grad_normed_two, resid, r_two, gain_second)
    grad_resid = grad_final + grad_resid

    grad_att = grad_resid.astype(BF16)
    grad_att = jnp.concatenate([grad_att, ring_step(grad_att, "c")])
    grad_w_out = dot(mixed, grad_att, ((0,), (0,))).astype(BF16)
    grad_mixed = dot(grad_att, w_out, ((1,), (1,))).astype(BF16).reshape(query.shape)
    grad_mixed, grad_w_out, two, result_step, result_three = sync(
        grad_mixed, grad_w_out, two, ring_step(result_total, "z"), result_three
    )
    first_x = jnp.concatenate([one, two])
    result_total = plus(result_step, end_y(results_c[3], result_three))
    out_parts = pick_weights(grad_w_out, "x", "y", False)
    one, two = halves(second_grads[1])
    first_sum, out_parts, grad_mixed, one, two, result_total = sync(
        finish_x(first_grads, first_x, BF16), out_parts, grad_mixed, one, two, result_total
    )
    first_pieces = shift_pieces(first_sum)
    one = ring_step(one, "x")
    result_step = ring_step(result_total, "z")
    out_sum = ring_sum(out_parts, "y", BF16)
    grad_probs = jnp.einsum("bqkgd,bskd->bkgqs", grad_mixed, values, preferred_element_type=F32)
    grad_value_pre = jnp.einsum(
        "bkgqs,bqkgd->bskd", probs_low, grad_mixed, preferred_element_type=F32
    )
    grad_value_pre = grad_value_pre.reshape(2 * count, kv_width).astype(BF16)
    grad_scores = (
        probs * (grad_probs - jnp.sum(probs * grad_probs, axis=-1, keepdims=True))
    ).astype(BF16)
    grad_query = jnp.einsum("bkgqs,bskd->bqkgd", grad_scores, keys, preferred_element_type=F32)
    grad_keys = jnp.einsum("bkgqs,bqkgd->bskd", grad_scores, query, preferred_element_type=F32)
    grad_query_pre = rotary_embedding(
        (grad_query * score_scale).reshape(query_pre.shape), token_position, -1.0
    )
    grad_query_pre = grad_query_pre.reshape(2 * count, q_width).astype(BF16)
    grad_key_pre = rotary_embedding(grad_keys * score_scale, token_position, -1.0)
    grad_key_pre = grad_key_pre.reshape(2 * count, kv_width).astype(BF16)
    grad_qk_pre = jnp.concatenate([grad_query_pre, grad_key_pre], axis=1)
    grad_qk_pre, grad_value_pre, out_sum, result_step, one, two = sync(
        grad_qk_pre, grad_value_pre, out_sum, result_step, one, two
    )
    outputs = resid + plus(result_step, results_sum[0], F32)
    two = ring_step(two, "x")
    out_sum = sum_along(out_sum, "x")
    grad_w_qk = dot(normalized_input, grad_qk_pre, ((0,), (0,))).astype(BF16)
    grad_w_v = dot(normalized_input, grad_value_pre, ((0,), (0,))).astype(BF16)
    grad_normed = dot(grad_qk_pre, w_qk, ((1,), (1,)))
    grad_normed = grad_normed + dot(grad_value_pre, w_v, ((1,), (1,)))
    grad_normed = ring_sum([grad_normed[:count], grad_normed[count:]], "c", F32)
    grad_rows, grad_gain_one = norm_back(grad_normed, own_act, r_one[:count], gain_first)
    grad_rows = grad_resid + grad_rows

    grad_small = jnp.concatenate(
        [grad_w_router, grad_gain_one[:, None], grad_gain_two[:, None]], axis=1
    )
    grad_small = jnp.pad(grad_small, ((0, 0), (0, LANES - grad_small.shape[1])))
    grad_vs = jnp.concatenate([grad_w_v, grad_small.astype(BF16)], axis=1)
    q_parts = pick_weights(grad_w_qk[:, :q_width], "x", "y", True)
    rest_parts = pick_weights(
        jnp.concatenate([grad_w_qk[:, q_width:], grad_vs], axis=1), "y", "x", True
    )
    q_parts, rest_parts, grad_rows, grad_chunks, first_pieces, out_sum, two = sync(
        q_parts, rest_parts, grad_rows, grad_chunks, first_pieces, out_sum, two
    )
    second_sum = finish_x(second_grads, jnp.concatenate([one, two]), BF16)
    second_sum, q_parts, rest_parts, grad_chunks = sync(
        second_sum, q_parts, rest_parts, grad_chunks
    )
    second_pieces = shift_pieces(second_sum)
    out_sum = sum_along(out_sum, "z", F32)
    grad_w_back, q_sum, rest_sum = sync(
        expert_grads(grad_chunks, weighted, 0, local_count, width, True),
        ring_sum(q_parts, "y", BF16),
        ring_sum(rest_parts, "x", BF16),
    )
    back_x = ring_step(grad_w_back[1], "x")
    q_sum, rest_sum, grad_w_out = sync(
        sum_along(q_sum, "x"), sum_along(rest_sum, "y"), out_sum
    )
    grad_first, grad_second, first_pieces, second_pieces = sync(
        sum_along(q_sum, "z", F32), sum_along(rest_sum, "z", F32), first_pieces, second_pieces
    )
    grad_w_gate, grad_w_up = unpack_experts([first_pieces, second_pieces], counts)
    grad_w_down = finish_x(grad_w_back, back_x, F32)
    grad_both = jnp.concatenate([grad_first, grad_second], axis=-1)
    mine = lax.dynamic_index_in_dim(grad_both, core, 0, keepdims=False)
    theirs = lax.dynamic_index_in_dim(grad_both, 1 - core, 0, keepdims=False)
    got = ring_step(theirs, "c")

    def whole_columns(start, columns):
        parts = [part[:, start : start + columns].reshape(own_rows, y_size, -1) for part in (mine, got)]
        ordered = jnp.where(core == 0, jnp.stack(parts, 2), jnp.stack(parts[::-1], 2))
        return ordered.reshape(own_rows, 2 * columns)

    grad_small = (mine + got)[:, q_width + 2 * kv_width :]
    return (
        outputs.astype(BF16).reshape(inputs.shape),
        grad_rows.reshape(inputs.shape),
        grad_small[:, E],
        whole_columns(0, q_width),
        whole_columns(q_width, kv_width),
        whole_columns(q_width + kv_width, kv_width),
        grad_w_out,
        grad_small[:, E + 1],
        grad_small[:, :E],
        grad_w_gate,
        grad_w_up,
        grad_w_down,
    )


def solution(mesh):
    experts, shards = mesh.shape["expert"], mesh.shape["shard"]
    split = Mesh(
        mesh.devices.reshape(experts // 2, 2, SLICES, shards // SLICES), ("y", "c", "z", "x")
    )
    groups, within = ("y", "c"), ("z", "x")
    tokens = P(None, ALL, None)
    rows = P(ALL, None)
    expert = P(groups, within, None)
    return jax.shard_map(
        body,
        mesh=split,
        in_specs=(tokens,) * 4
        + (P(ALL), rows, rows, rows, rows, P(ALL), rows, expert, expert, expert),
        out_specs=(tokens, tokens, P(ALL), rows, rows, rows, rows, P(ALL), rows)
        + (expert, expert, expert),
        check_vma=False,
    )
```

```python
import functools
import itertools
import math

import jax
import jax.numpy as jnp
from jax import lax
from jax.experimental import pallas as pl
from jax.experimental.pallas import tpu as pltpu
from jax.experimental.layout import Layout, with_layout_constraint
from jax.sharding import Mesh, PartitionSpec as P

MODEL_WIDTH = 1536
QUERY_HEADS = 24
KEY_VALUE_HEADS = 8
HEAD_SIZE = 64
QUERY_PER_GROUP = QUERY_HEADS // KEY_VALUE_HEADS
E = 40
TOPK = 8
SLICES = 4
LANES = 128
VMEM_BYTES = 60 * 1024 * 1024

ALL = ("y", "c", "z", "x")
epsilon = 1e-05
F32 = jnp.float32
BF16 = jnp.bfloat16


def dot(left, right, dims=((1,), (0,))):
    return lax.dot_general(left, right, (dims, ((), ())), preferred_element_type=F32)


def sync(*values):
    return lax.optimization_barrier(values)


def ring_step(array, axis):
    size = lax.axis_size(axis)
    return lax.ppermute(array, axis, [(i, (i + 1) % size) for i in range(size)])


def ring_gather(block, axis):
    blocks = [block]
    for _ in range(lax.axis_size(axis) - 1):
        blocks.append(ring_step(blocks[-1], axis))
    return blocks


def ring_sum(parts, axis, kind):
    total = parts[1]
    for part in list(parts[2:]) + [parts[0]]:
        total = ring_step(total, axis).astype(F32) + part.astype(F32)
        total = total.astype(kind if part is parts[0] else part.dtype)
    return total


def direct_sum(parts, axis, kind):
    size = lax.axis_size(axis)
    total = parts[0].astype(F32)
    for step in range(1, size):
        to = [(i, (i - step) % size) for i in range(size)]
        total = total + lax.ppermute(parts[step], axis, to).astype(F32)
    return total.astype(kind)


def index_at(axis, step):
    return (lax.axis_index(axis) - step) % lax.axis_size(axis)


def move_kernel(moves, count_in, count_out, place_ref, *refs):
    sources, targets = refs[:count_in], refs[count_in : count_in + count_out]
    held, sems = refs[count_in + count_out : -1], refs[-1]
    copies = [[] for _ in targets]
    for number, (source, from_index, target, to_index) in enumerate(moves):
        picked = [
            tuple(place_ref[i[0]] if isinstance(i, tuple) else i for i in index)
            for index in (from_index, to_index)
        ]
        copy = pltpu.make_async_copy(
            sources[source].at[picked[0]], held[target].at[picked[1]], sems.at[number]
        )
        copy.start()
        copies[target].append(copy)
    out = []
    for target, arriving in enumerate(copies):
        for copy in arriving:
            copy.wait()
        out.append(
            pltpu.make_async_copy(held[target], targets[target], sems.at[len(moves) + target])
        )
        out[-1].start()
    for copy in out:
        copy.wait()


def move(moves, places, sources, shapes, name):
    anywhere = pl.BlockSpec(memory_space=pl.ANY)
    total = sum(math.prod(s.shape) * s.dtype.itemsize for s in shapes)
    return pl.pallas_call(
        functools.partial(move_kernel, moves, len(sources), len(shapes)),
        in_specs=[pl.BlockSpec(memory_space=pltpu.SMEM)] + [anywhere] * len(sources),
        out_specs=[anywhere] * len(shapes),
        out_shape=shapes,
        scratch_shapes=[pltpu.VMEM(s.shape, s.dtype) for s in shapes]
        + [pltpu.SemaphoreType.DMA((len(moves) + len(shapes),))],
        compiler_params=pltpu.CompilerParams(vmem_limit_bytes=VMEM_BYTES),
        cost_estimate=pl.CostEstimate(flops=0, bytes_accessed=2 * total, transcendentals=0),
        name=name,
    )(jnp.stack(places).astype(jnp.int32), *sources)


def places_of(axes):
    places, where = [], {}
    for axis in axes:
        for step in range(lax.axis_size(axis)):
            where[axis, step] = (len(places),)
            places.append(index_at(axis, step))
    return places, where


def place_weights(gathers):
    places, where = places_of(("y", "z", "x"))
    sizes = [lax.axis_size(axis) for axis in ("y", "z", "x")]
    moves, sources, shapes = [], [], []
    for number, blocks in enumerate(gathers):
        for (y_step, z_first, x_step), part in blocks.items():
            for i in range(part.shape[0]):
                spot = (where["y", y_step], slice(None), where["z", z_first + i], where["x", x_step])
                moves.append((len(sources), (i,), number, spot))
            sources.append(part)
        shape = (sizes[0], 2) + tuple(sizes[1:]) + sources[-1].shape[2:]
        shapes.append(jax.ShapeDtypeStruct(shape, sources[-1].dtype))
    whole = move(moves, places, sources, shapes, "place_weights")
    return [part.reshape(-1, part.shape[-1]) for part in whole]


def pick_weights(grads, first, second, with_core):
    sizes = {axis: lax.axis_size(axis) for axis in ("y", "z", "x")}
    core = (2,) if with_core else ()
    places, where = places_of(("y", "z", "x"))
    moves, sources, start = [], [], 0
    for number, (grad, column, columns) in enumerate(grads):
        shape = (sizes["y"],) + core + (sizes["z"], sizes["x"], -1, grad.shape[-1])
        sources.append(grad.reshape(shape))
        rows = slice(None)
        for y_step, z_step, x_step in itertools.product(
            range(sizes["y"]), range(sizes["z"]), range(sizes["x"])
        ):
            spot = [where["y", y_step], where["z", z_step], where["x", x_step]]
            if with_core:
                spot.insert(1, rows)
            spot += [rows, pl.ds(column, columns)]
            steps = {"y": y_step, "x": x_step}
            to = (steps[first], z_step) + (rows,) * (1 + len(core)) + (pl.ds(start, columns),)
            moves.append((number, tuple(spot), steps[second], to))
        start = start + columns
    tail = core + (sources[0].shape[-2], start)
    shape = jax.ShapeDtypeStruct((sizes[first], sizes["z"]) + tail, sources[0].dtype)
    return move(moves, places, sources, [shape] * sizes[second], "pick_weights")


def sum_along(parts, axis, kind=BF16):
    return ring_sum([parts[i] for i in range(parts.shape[0])], axis, kind)


def pack_kernel(gate_ref, up_ref, out_ref):
    width = out_ref.shape[-1] // 2
    for z in range(out_ref.shape[0]):
        out_ref[z, :, :width] = gate_ref[0, :, z * width : (z + 1) * width]
        out_ref[z, :, width:] = up_ref[0, :, z * width : (z + 1) * width]


def pack_experts(w_gate, w_up, first, last, slices):
    rows, hidden = w_gate.shape[1:]
    spec = pl.BlockSpec((1, rows, hidden), lambda e: (first + e, 0, 0))
    width = 2 * hidden // slices
    return pl.pallas_call(
        pack_kernel,
        grid=(last - first,),
        in_specs=[spec, spec],
        out_specs=pl.BlockSpec((slices, rows, width), lambda e: (0, 0, e)),
        out_shape=jax.ShapeDtypeStruct((slices, rows, (last - first) * width), w_gate.dtype),
        name="pack_experts",
    )(w_gate, w_up)


def unpack_kernel(part_ref, *refs):
    gate_ref, up_ref = refs[-2:]
    slices = part_ref.shape[0]
    width = gate_ref.shape[-1] // slices
    for z in range(slices):
        both = part_ref[z].astype(F32)
        gate_ref[0, :, z * width : (z + 1) * width] = both[:, :width]
        up_ref[0, :, z * width : (z + 1) * width] = both[:, width:]


def unpack_experts(part, first, last, local_count, earlier):
    slices, rows, columns = part.shape
    width = columns // (last - first)
    spec = pl.BlockSpec((1, rows, width // 2 * slices), lambda e: (first + e, 0, 0))
    shape = jax.ShapeDtypeStruct((local_count, rows, width // 2 * slices), F32)
    anywhere = pl.BlockSpec(memory_space=pl.ANY)
    return pl.pallas_call(
        unpack_kernel,
        grid=(last - first,),
        in_specs=[pl.BlockSpec((slices, rows, width), lambda e: (0, 0, e))]
        + [anywhere] * len(earlier),
        out_specs=[spec, spec],
        out_shape=[shape, shape],
        input_output_aliases={1 + i: i for i in range(len(earlier))},
        name="unpack_experts",
    )(part, *earlier)


def experts_kernel(counts, steps, x_size, place_ref, *refs):
    parts = len(counts)
    rows_in, grads_in, refs = refs[:steps], refs[steps : 2 * steps], refs[2 * steps :]
    w_in_parts, refs = [refs[i * x_size : (i + 1) * x_size] for i in range(parts)], refs[parts * x_size :]
    w_back_parts, refs = refs[:x_size], refs[x_size:]
    results, grads, (active_ref, hidden_ref, gates_ref) = refs[:2], refs[2:4], refs[4:7]
    rows_buf, grads_buf = refs[7:9]
    w_in, w_back, sems = refs[9 : 9 + parts], refs[9 + parts], refs[10 + parts]
    step = pl.program_id(0)
    half = steps // 2
    weights, late = [[] for _ in counts], [[] for _ in range(steps)]
    number = 0

    def copy_of(source, target):
        nonlocal number
        number = number + 1
        return pltpu.make_async_copy(source, target, sems.at[number - 1])

    first = 0
    for part, count in enumerate(counts):
        for x_step in range(x_size):
            place = place_ref[1 + x_step]
            source = w_in_parts[part][x_step]
            size = source.shape[1]
            for z in range(source.shape[0]):
                start = pl.multiple_of((z * x_size + place) * size, size)
                weights[part].append(copy_of(source.at[z], w_in[part].at[pl.ds(start, size)]))
            source = w_back_parts[x_step]
            size = source.shape[1]
            for e in range(first, first + count):
                start = pl.multiple_of((e * x_size + place) * size, size)
                weights[part].append(copy_of(source.at[e], w_back.at[pl.ds(start, size)]))
        first = first + count
    for i in range(steps):
        late[i] = [copy_of(rows_in[i], rows_buf.at[i]), copy_of(grads_in[i], grads_buf.at[i])]

    @pl.when(step == 0)
    def _():
        for some in late[:1] + weights + late[1:]:
            for copy in some:
                copy.start()

    for i in range(steps):

        @pl.when(step == i)
        def _(i=i):
            for copy in late[i]:
                copy.wait()

    local_count = sum(counts)
    width = w_back.shape[0] // local_count
    rows = rows_buf[step, :, :MODEL_WIDTH]
    grad_rows = grads_buf[step]
    first = place_ref[0] * local_count
    source = lax.broadcasted_iota(jnp.int32, (LANES, LANES), 0)
    wanted = lax.broadcasted_iota(jnp.int32, (LANES, LANES), 1) + first
    choose = ((source == wanted) | (source == wanted + E)).astype(F32).astype(BF16)
    gates = dot(rows_buf[step, :, MODEL_WIDTH:], choose)
    lane = lax.broadcasted_iota(jnp.int32, gates.shape, 1)
    grad_gates = jnp.zeros(gates.shape, F32)
    expert = 0
    for part, count in enumerate(counts):

        @pl.when(step == 0)
        def _(part=part):
            for copy in weights[part]:
                copy.wait()

        for i in range(count):
            here = slice(expert * width, (expert + 1) * width)
            hidden = dot(rows, w_in[part][:, 2 * width * i : 2 * width * (i + 1)])
            grad_plain = dot(grad_rows, w_back[here, :], ((1,), (1,)))
            gate_part, up_part = hidden[:, :width], hidden[:, width:]
            sigmoid_gate = 1.0 / (1.0 + jnp.exp(-gate_part))
            silu = gate_part * sigmoid_gate
            active = silu * up_part
            weight = gates[:, expert : expert + 1]
            total = jnp.sum(active * grad_plain, axis=1, keepdims=True)
            grad_gates = jnp.where(lane == first + expert, total, grad_gates)
            active_ref[:, here] = (weight * active).astype(BF16)
            grad_active = weight * grad_plain
            start = 2 * width * expert
            hidden_ref[:, start : start + width] = (
                grad_active * up_part * (sigmoid_gate + silu * (1.0 - sigmoid_gate))
            ).astype(BF16)
            hidden_ref[:, start + width : start + 2 * width] = (grad_active * silu).astype(BF16)
            expert = expert + 1
    gates_ref[0] = grad_gates.T[:E]
    result = dot(active_ref[...], w_back[...]).astype(BF16)
    grad_in = jnp.zeros(rows.shape, F32)
    start = 0
    for part, count in enumerate(counts):
        size = 2 * width * count
        grad_in += dot(hidden_ref[:, start : start + size], w_in[part][...], ((1,), (1,)))
        start = start + size
    grad_in = grad_in.astype(BF16)

    for side, now in enumerate((step < half, step >= half)):

        @pl.when(now)
        def _(side=side):
            results[side][0] = result
            grads[side][0] = grad_in


def run_experts(rows, grads, w_in_parts, w_back_parts, counts, group):
    count, wide = rows[0].shape
    steps = len(rows)
    half = steps // 2
    local_count = sum(counts)
    x_size = len(w_in_parts[0])
    z_size, own_rows, columns = w_in_parts[0][0].shape
    width = columns // (2 * counts[0])
    copies = 2 * steps + x_size * (len(counts) * z_size + local_count)
    places, _ = places_of(("x",))
    anywhere = pl.BlockSpec(memory_space=pl.ANY)
    own = pl.BlockSpec((1, count, MODEL_WIDTH), lambda i: (jnp.minimum(i, half - 1), 0, 0))
    other = pl.BlockSpec((1, count, MODEL_WIDTH), lambda i: (jnp.maximum(i - half, 0), 0, 0))

    def by_row(columns):
        return pl.BlockSpec((count, columns), lambda i: (i, 0))

    side = jax.ShapeDtypeStruct((half, count, MODEL_WIDTH), BF16)
    flops = 2 * steps * count * MODEL_WIDTH * 6 * local_count * width
    return pl.pallas_call(
        functools.partial(experts_kernel, counts, steps, x_size),
        grid=(steps,),
        in_specs=[pl.BlockSpec(memory_space=pltpu.SMEM)]
        + [anywhere] * (2 * steps + (len(counts) + 1) * x_size),
        out_specs=[own, other, own, other]
        + [by_row(local_count * width), by_row(2 * local_count * width)]
        + [pl.BlockSpec((1, E, count), lambda i: (i, 0, 0))],
        out_shape=[side] * 4
        + [
            jax.ShapeDtypeStruct((steps * count, local_count * width), BF16),
            jax.ShapeDtypeStruct((steps * count, 2 * local_count * width), BF16),
            jax.ShapeDtypeStruct((steps, E, count), F32),
        ],
        scratch_shapes=[
            pltpu.VMEM((steps, count, wide), BF16),
            pltpu.VMEM((steps, count, MODEL_WIDTH), BF16),
        ]
        + [pltpu.VMEM((MODEL_WIDTH, part[0].shape[-1]), BF16) for part in w_in_parts]
        + [
            pltpu.VMEM((local_count * width, MODEL_WIDTH), BF16),
            pltpu.SemaphoreType.DMA((copies,)),
        ],
        compiler_params=pltpu.CompilerParams(vmem_limit_bytes=VMEM_BYTES),
        cost_estimate=pl.CostEstimate(
            flops=flops, bytes_accessed=30 * 1024 * 1024, transcendentals=0
        ),
        name="experts",
    )(
        jnp.stack([group] + places).astype(jnp.int32),
        *rows,
        *grads,
        *[part for parts in w_in_parts for part in parts],
        *w_back_parts,
    )


def expert_grads_kernel(count_left, count_right, back, place_ref, *refs):
    whole = refs[:count_left]
    columns = refs[count_left : count_left + count_right]
    outs, (buf, total, sems) = refs[count_left + count_right : -3], refs[-3:]
    rows_each = whole[0].shape[0]

    @pl.when(pl.program_id(0) == 0)
    def _():
        copies = [
            pltpu.make_async_copy(
                part.at[:, pl.ds(0, MODEL_WIDTH)],
                buf.at[pl.ds(number * rows_each, rows_each)],
                sems.at[number],
            )
            for number, part in enumerate(whole)
        ]
        for copy in copies:
            copy.start()
        for copy in copies:
            copy.wait()

    size = columns[0].shape[0]
    for i, part in enumerate(columns):
        rows = buf[i * size : (i + 1) * size, :]
        if back:
            term = dot(part[...], rows, ((0,), (0,)))
        else:
            term = dot(rows, part[...], ((0,), (0,)))
        if i == 0:
            total[...] = term
        else:
            total[...] += term
    blocks, own = outs[0].shape[0], outs[0].shape[1]
    devices = len(outs) if back else len(outs) // 2
    for number, out in enumerate(outs):
        step, half = (number, 0) if back else (number // 2, number % 2)
        for i in range(blocks):
            block = half * blocks + i
            start = pl.multiple_of((block * devices + place_ref[step]) * own, own)
            out[i] = total[pl.ds(start, own), :].astype(BF16)


def expert_grads(whole, columns, first, last, width, back):
    x_size = lax.axis_size("x")
    places, _ = places_of(("x",))
    tokens = len(whole) * whole[0].shape[0]
    experts = last - first
    anywhere = pl.BlockSpec(memory_space=pl.ANY)
    column = pl.BlockSpec((columns[0].shape[0], width), lambda e: (0, first + e))
    outs = x_size if back else 2 * x_size
    if back:
        own = width // x_size
        block = (1, own, MODEL_WIDTH)
        shape = (experts, own, MODEL_WIDTH)
        out = pl.BlockSpec(block, lambda e: (e, 0, 0))
        total = (width, MODEL_WIDTH)
    else:
        z_size = lax.axis_size("z")
        own = MODEL_WIDTH // (z_size * x_size)
        shape = (z_size // 2, own, experts * width)
        out = pl.BlockSpec((z_size // 2, own, width), lambda e: (0, 0, e))
        total = (MODEL_WIDTH, width)
    return pl.pallas_call(
        functools.partial(expert_grads_kernel, len(whole), len(columns), back),
        grid=(experts,),
        in_specs=[pl.BlockSpec(memory_space=pltpu.SMEM)]
        + [anywhere] * len(whole)
        + [column] * len(columns),
        out_specs=[out] * outs,
        out_shape=[jax.ShapeDtypeStruct(shape, BF16)] * outs,
        scratch_shapes=[
            pltpu.VMEM((tokens, MODEL_WIDTH), BF16),
            pltpu.VMEM(total, F32),
            pltpu.SemaphoreType.DMA((len(whole),)),
        ],
        compiler_params=pltpu.CompilerParams(vmem_limit_bytes=VMEM_BYTES),
        cost_estimate=pl.CostEstimate(
            flops=2 * tokens * MODEL_WIDTH * width * experts,
            bytes_accessed=2 * tokens * (MODEL_WIDTH + width * experts),
            transcendentals=0,
        ),
        name="expert_grads",
    )(jnp.stack(places).astype(jnp.int32), *whole, *columns)


def positions(lengths, count_of_tokens):
    seq_ends = jnp.cumsum(lengths, axis=-1)
    starts = seq_ends - lengths
    token_index = jnp.arange(count_of_tokens, dtype=jnp.int32)
    segment = jnp.sum((token_index[:, None] >= seq_ends[..., None, :]).astype(jnp.int32), axis=-1)
    choose = segment[..., None] == jnp.arange(lengths.shape[-1], dtype=jnp.int32)
    offset = jnp.sum(jnp.where(choose, starts[..., None, :], 0), axis=-1)
    return (segment, token_index - offset)


def rotary_embedding(values_in, token_position, direction):
    half_size = values_in.shape[-1] // 2
    frequency = jnp.exp(jnp.arange(half_size, dtype=F32) * (-math.log(10000.0) / half_size))
    angles = token_position.astype(F32)[..., None] * frequency
    cosine = jnp.cos(angles)[..., None, :]
    sine_part = jnp.sin(angles)[..., None, :]
    first_half = values_in[..., :half_size]
    second_half = values_in[..., half_size:]
    return jnp.concatenate(
        [
            first_half * cosine - direction * second_half * sine_part,
            second_half * cosine + direction * first_half * sine_part,
        ],
        axis=-1,
    )


def norm_back(grad_normed, values_in, inverse_root, gain):
    scaled = grad_normed * gain
    grad_gain = jnp.sum(grad_normed * values_in * inverse_root, axis=0)
    cubed = inverse_root * inverse_root * inverse_root
    grad_values = inverse_root * scaled - values_in * cubed * jnp.mean(
        scaled * values_in, axis=-1, keepdims=True
    )
    return (grad_values, grad_gain)


def body(
    inputs,
    cotangent,
    lengths,
    routes,
    norm_gain_one,
    w_query,
    key_projection_weight,
    value_projection_weight,
    w_out,
    norm_gain_two,
    w_router,
    w_gate,
    w_up,
    w_down,
):
    micro, block, _ = inputs.shape
    count = micro * block
    local_count = w_gate.shape[0]
    y_size, z_size, x_size = lax.axis_size("y"), lax.axis_size("z"), lax.axis_size("x")
    core = lax.axis_index("c")
    group = lax.axis_index("y") * 2 + core
    score_scale = 1.0 / math.sqrt(HEAD_SIZE)
    own_rows = w_query.shape[0]
    q_width, kv_width = MODEL_WIDTH // 2, KEY_VALUE_HEADS * HEAD_SIZE // 2
    kv_heads = KEY_VALUE_HEADS // 2

    def columns_of(weight, which):
        split = weight.reshape(own_rows, y_size, 2, -1)
        return lax.dynamic_index_in_dim(split, which, 2, keepdims=False).reshape(own_rows, -1)

    small = jnp.concatenate([w_router, norm_gain_one[:, None], norm_gain_two[:, None]], axis=1)
    small = jnp.pad(small, ((0, 0), (0, LANES - small.shape[1])))

    def both_cores(arrays):
        mine = jnp.concatenate([columns_of(a, core) for a in arrays], axis=1)
        theirs = jnp.concatenate([columns_of(a, 1 - core) for a in arrays], axis=1)
        return mine, theirs

    mine, theirs = both_cores([w_query, key_projection_weight, value_projection_weight])
    got, other_lengths = sync(
        ring_step(jnp.concatenate([theirs, small], axis=1), "c"), ring_step(lengths, "c")
    )
    mine = jnp.concatenate([mine, small], axis=1)
    both = jnp.where(core == 0, jnp.stack([mine, got]), jnp.stack([got, mine]))
    both = jnp.concatenate(
        [
            both[..., : q_width + kv_width],
            both[..., q_width + 2 * kv_width :],
            both[..., q_width + kv_width : q_width + 2 * kv_width],
            jnp.stack([w_out[:, :q_width], w_out[:, q_width:]]),
        ],
        axis=-1,
    )
    counts = [local_count // 2, local_count - local_count // 2]
    ranges = [(0, counts[0]), (counts[0], local_count)]
    grad_final_low = cotangent.reshape(count, MODEL_WIDTH)
    grads_z = [grad_final_low]
    grads_ahead = ring_step(grad_final_low, "z")
    grads_y = [ring_gather(grad_final_low, "y")]
    down_parts = ring_gather(w_down, "x")
    pair = z_size // 2
    first_width = q_width + kv_width + LANES
    first_blocks, second_blocks = {}, {}

    def first_hops(blocks):
        rows = jnp.stack(blocks)
        return ring_gather(rows[..., :first_width], "x"), ring_gather(rows[..., first_width:], "y")

    def second_hops(by_x, by_y, z_first):
        for x_step, one in enumerate(by_x):
            for y_step, two in enumerate(ring_gather(one, "y")):
                first_blocks[y_step, z_first, x_step] = two
        for y_step, one in enumerate(by_y):
            for x_step, two in enumerate(ring_gather(one, "x")):
                second_blocks[y_step, z_first, x_step] = two

    z_blocks = [both]
    for _ in range(pair - 1):
        z_blocks.append(ring_step(z_blocks[-1], "z"))
    others = ring_step(inputs, "c")
    packed = [pack_experts(w_gate, w_up, first, last, z_size) for first, last in ranges]
    z_blocks, others, grads_ahead, grads_y, packed = sync(
        z_blocks, others, grads_ahead, grads_y, packed
    )
    other_inputs = others
    grads_z.append(grads_ahead)
    ahead = []
    for _ in range(pair):
        ahead.append(ring_step((z_blocks + ahead)[-1], "z"))
    hops, ahead, down_parts, packed = sync(first_hops(z_blocks), ahead, down_parts, packed)
    swapped = lax.all_to_all(packed[0], "z", 0, 0, tiled=True)
    second_hops(*hops, 0)
    first_blocks, second_blocks, ahead = sync(first_blocks, second_blocks, ahead)
    hops, grads_z = sync(first_hops(ahead), grads_z)
    second_hops(*hops, pair)
    first_blocks, second_blocks, swapped, packed, grads_z = sync(
        first_blocks, second_blocks, swapped, packed, grads_z
    )
    grads_y.append(ring_gather(grads_z[1], "y"))
    first_parts = ring_gather(swapped, "x")
    swapped = lax.all_to_all(packed[1], "z", 0, 0, tiled=True)
    w_first, w_second = place_weights([first_blocks, second_blocks])
    w_qk = w_first[:, : q_width + kv_width]
    small = w_first[:, q_width + kv_width :]
    w_v = w_second[:, :kv_width]
    w_out = w_second[:, kv_width:].reshape(y_size, 2, -1, q_width).transpose(0, 2, 1, 3)
    w_out = w_out.reshape(q_width, MODEL_WIDTH)
    w_router = small[:, :E]
    gain_first = small[:, E].astype(F32)
    gain_second = small[:, E + 1].astype(F32)

    all_inputs = jnp.stack([inputs, other_inputs])
    all_lengths = jnp.concatenate([lengths[:, 0], other_lengths[:, 0]])
    act_rows = all_inputs.reshape(2 * count, MODEL_WIDTH).astype(F32)
    grad_final = grad_final_low.astype(F32)
    r_one = lax.rsqrt(jnp.mean(act_rows * act_rows, axis=-1) + epsilon)[:, None]
    normalized_input = (act_rows * r_one * gain_first).astype(BF16)
    segment, token_position = positions(all_lengths, block)
    blocks = 2 * micro
    qk_pre = dot(normalized_input, w_qk)
    values = dot(normalized_input, w_v).astype(BF16)
    qk_pre, values, grads_y = sync(qk_pre, values, grads_y)
    query_pre = qk_pre[:, :q_width]
    query_pre = query_pre.reshape(blocks, block, kv_heads * QUERY_PER_GROUP, HEAD_SIZE)
    key_pre = qk_pre[:, q_width:].reshape(blocks, block, kv_heads, HEAD_SIZE)
    values = values.reshape(blocks, block, kv_heads, HEAD_SIZE)
    query = rotary_embedding(query_pre, token_position, 1.0).astype(BF16)
    query = query.reshape(blocks, block, kv_heads, QUERY_PER_GROUP, HEAD_SIZE)
    keys = rotary_embedding(key_pre, token_position, 1.0).astype(BF16)
    token_index = jnp.arange(block, dtype=jnp.int32)
    allowed = (segment[:, :, None] == segment[:, None, :]) & (
        token_index[:, None] >= token_index[None, :]
    )
    query, keys, first_parts, swapped, grads_z = sync(query, keys, first_parts, swapped, grads_z)
    second_parts = ring_gather(swapped, "x")
    grads_ahead = ring_step(grads_z[1], "z")
    scores = jnp.einsum("bqkgd,bskd->bkgqs", query, keys, preferred_element_type=F32)
    scores = jnp.where(allowed[:, None, None], scores * score_scale, -1000000000.0)
    probs = jax.nn.softmax(scores, axis=-1)
    probs_low = probs.astype(BF16)
    mixed = jnp.einsum("bkgqs,bskd->bqkgd", probs_low, values, preferred_element_type=F32)
    mixed = mixed.reshape(2 * count, q_width).astype(BF16)
    grads_other = [[ring_step(part, "c") for part in some] for some in grads_y]
    mixed, grads_other = sync(mixed, grads_other)
    projected = dot(mixed, w_out)
    own_act = act_rows[:count]
    resid = own_act + ring_sum([projected[:count], projected[count:]], "c", F32)

    r_two = lax.rsqrt(jnp.mean(resid * resid, axis=-1) + epsilon)[:, None]
    normed_two = (resid * r_two * gain_second).astype(BF16)
    chance = jax.nn.softmax(dot(normed_two, w_router), axis=-1)
    choice = routes.reshape(count, TOPK)
    chosen = jnp.any(choice[..., None] == jnp.arange(E, dtype=jnp.int32), axis=1).astype(F32)
    picked = chance * chosen
    picked_total = jnp.sum(picked, axis=-1, keepdims=True)
    gates = picked / picked_total

    high = lax.reduce_precision(gates, 8, 7)
    low = gates - high
    spare = jnp.zeros((count, LANES - 2 * E), BF16)
    sent = jnp.concatenate([normed_two, high.astype(BF16), low.astype(BF16), spare], axis=1)
    sent, grads_ahead = sync(sent, grads_ahead)
    grads_z.append(grads_ahead)
    rows, ahead, second_parts, others, grads_third = sync(
        ring_gather(sent, "y"),
        ring_step(sent, "z"),
        second_parts,
        ring_step(sent, "c"),
        ring_step(grads_z[2], "c"),
    )
    grads_other.append([grads_third])
    w_in_parts, w_back_parts = [first_parts, second_parts], down_parts
    rows, others = sync(rows, [others] + [ring_step(part, "c") for part in rows[1:]])
    width = w_in_parts[0][0].shape[-1] // (2 * counts[0])

    def plus(first, second, kind=BF16):
        return (first.astype(F32) + second.astype(F32)).astype(kind)

    def plus_all(first, second):
        return [plus(first[i], second[i]) for i in range(y_size)]

    def hops_y(parts):
        return ring_step(parts[1], "y") if y_size == 2 else ring_sum(parts, "y", BF16)

    def end_y(parts, arrived):
        return plus(arrived, parts[0]) if y_size == 2 else arrived

    sent_chunks, grad_chunks, weighted, grad_hidden, grads_gates = [], [], [], [], []
    results_c, grads_c, results_sum, grads_sum = [], [], {}, {}
    for z_step in range(z_size):
        sent_chunks += rows + others
        grad_chunks += grads_y[z_step] + grads_other[z_step]
        parts = run_experts(
            rows + others,
            grads_y[z_step] + grads_other[z_step],
            w_in_parts,
            w_back_parts,
            counts,
            group,
        )
        moved = {}
        if z_step + 1 < z_size:
            moved["rows"] = ring_gather(ahead, "y")
        if z_step + 2 < z_size:
            moved["ahead"] = ring_step(ahead, "z")
        if z_step <= 1:
            moved["grads"] = ring_gather(grads_z[2 + z_step], "y")
        if z_step == 0:
            moved["grads_z"] = ring_step(grads_z[2], "z")
        if z_step == 1:
            moved["grads_other"] = [ring_step(part, "c") for part in grads_y[2][1:]]
        if z_step == 2:
            moved["grads_other"] = [ring_step(part, "c") for part in grads_y[3]]
        if z_step >= 2:
            moved["grad"] = hops_y(grads_c[z_step - 1])
        if z_step >= 1:
            moved["result"] = ring_step(last_results[1], "c")
        if z_step == 3:
            moved["step"] = ring_step(grads_sum[1], "z")
            moved["grad_zero"] = hops_y(grads_c[0])
            moved["result_one"] = hops_y(results_c[1])
        parts, moved = sync(parts, moved)
        weighted.append(parts[4])
        grad_hidden.append(parts[5])
        grads_gates.append(parts[6])
        if z_step <= 1:
            grads_y.append(moved["grads"])
        if z_step == 0:
            grads_z.append(moved["grads_z"])
        if z_step == 1:
            grads_other[2] += moved["grads_other"]
        if z_step == 2:
            grads_other.append(moved["grads_other"])
        arrived = ring_step(parts[3], "c")
        if z_step + 1 < z_size:
            ahead, rows = moved.get("ahead"), moved["rows"]
            others = [ring_step(part, "c") for part in rows]
        arrived, others, rows = sync(arrived, others, rows)
        if z_step >= 1:
            results_c.append(plus_all(moved["result"], last_results[0]))
        if z_step >= 2:
            grads_sum[z_step - 1] = end_y(grads_c[z_step - 1], moved["grad"])
        grads_c.append(plus_all(arrived, parts[2]))
        last_results = parts[:2]

    total = plus(moved["step"], grads_sum[2])
    grads_sum[0] = end_y(grads_c[0], moved["grad_zero"])
    results_sum[1] = end_y(results_c[1], moved["result_one"])
    spread = jnp.stack(grads_gates).reshape(z_size, 2, y_size, E, count)
    spread = ring_sum([spread[:, 0], spread[:, 1]], "c", F32)

    def in_grads(which):
        first, last = ranges[which]
        return expert_grads(sent_chunks, grad_hidden, first, last, 2 * width, False)

    def halves(part):
        middle = part.shape[0] // 2
        return part[:middle], part[middle:]

    grads_c, total, results_c, results_sum, last_results, spread, grad_hidden = sync(
        grads_c, total, results_c, results_sum, last_results, spread, grad_hidden
    )
    first_grads, last_grad, step, result_three, spread = sync(
        in_grads(0),
        hops_y(grads_c[3]),
        ring_step(total, "z"),
        ring_step(last_results[1], "c"),
        ring_sum([spread[:, i] for i in range(y_size)], "y", F32),
    )
    total = plus(step, end_y(grads_c[3], last_grad))
    grad_hidden, total, results_sum, results_c, first_grads, result_three = sync(
        grad_hidden, total, results_sum, results_c, first_grads, result_three
    )
    second_grads, step, result_two, grad_gates, one = sync(
        in_grads(1),
        ring_step(total, "z"),
        hops_y(results_c[2]),
        ring_sum([spread[i] for i in range(z_size)], "z", F32),
        ring_step(first_grads[2], "x"),
    )
    grad_gates = with_layout_constraint(grad_gates, Layout((0, 1))).T
    grad_experts = plus(step, grads_sum[0], F32)
    grad_experts, first_grads, second_grads, results_c, results_sum, result_two, result_three = sync(
        grad_experts, first_grads, second_grads, results_c, results_sum, result_two, result_three
    )
    two = ring_step(first_grads[3], "x")
    second_one = ring_step(second_grads[2], "x")
    result_step = ring_step(results_sum[1], "z")
    results_sum[2] = end_y(results_c[2], result_two)
    results_c.append(plus_all(result_three, last_results[0]))
    result_three = hops_y(results_c[3])

    def finish_x(parts, arrived, kind):
        rest = list(parts[2:]) + [parts[0]]
        total = plus(arrived, rest[0], kind)
        for part in rest[1:]:
            total = plus(ring_step(total, "x"), part, kind)
        return total

    def finish_in(parts, one, two):
        return jnp.concatenate([finish_x(parts[0::2], one, BF16), finish_x(parts[1::2], two, BF16)])

    grad_picked = chosen * (grad_gates - jnp.sum(grad_gates * gates, axis=-1, keepdims=True))
    grad_chance = grad_picked / picked_total
    grad_logits = (
        chance * (grad_chance - jnp.sum(chance * grad_chance, axis=-1, keepdims=True))
    ).astype(BF16)
    grad_w_router = dot(normed_two, grad_logits, ((0,), (0,)))
    grad_normed_two = grad_experts + dot(grad_logits, w_router, ((1,), (1,)))
    grad_resid, grad_gain_two = norm_back(grad_normed_two, resid, r_two, gain_second)
    grad_resid = grad_final + grad_resid

    grad_att = grad_resid.astype(BF16)
    grad_att = jnp.concatenate([grad_att, ring_step(grad_att, "c")])
    grad_w_out = dot(mixed, grad_att, ((0,), (0,))).astype(BF16)
    grad_mixed = dot(grad_att, w_out, ((1,), (1,))).astype(BF16).reshape(query.shape)
    grad_mixed, grad_w_out, two, result_step, result_three, second_grads, results_c = sync(
        grad_mixed, grad_w_out, two, result_step, result_three, second_grads, results_c
    )
    first_sum = finish_in(first_grads, one, two)
    result_total = plus(result_step, results_sum[2])
    results_sum[3] = end_y(results_c[3], result_three)
    out_parts = pick_weights([(grad_w_out, 0, MODEL_WIDTH)], "x", "y", False)
    first_sum, out_parts, grad_mixed, result_total, second_grads = sync(
        first_sum, out_parts, grad_mixed, result_total, second_grads
    )
    first_pieces = lax.all_to_all(first_sum, "z", 0, 0, tiled=True)
    second_two = ring_step(second_grads[3], "x")
    out_sum = ring_sum(out_parts, "y", BF16)
    result_step = ring_step(result_total, "z")
    result_zero = hops_y(results_c[0])
    grad_probs = jnp.einsum("bqkgd,bskd->bkgqs", grad_mixed, values, preferred_element_type=F32)
    grad_value_pre = jnp.einsum(
        "bkgqs,bqkgd->bskd", probs_low, grad_mixed, preferred_element_type=F32
    )
    grad_value_pre = grad_value_pre.reshape(2 * count, kv_width).astype(BF16)
    grad_scores = (
        probs * (grad_probs - jnp.sum(probs * grad_probs, axis=-1, keepdims=True))
    ).astype(BF16)
    grad_query = jnp.einsum("bkgqs,bskd->bqkgd", grad_scores, keys, preferred_element_type=F32)
    grad_keys = jnp.einsum("bkgqs,bqkgd->bskd", grad_scores, query, preferred_element_type=F32)
    grad_query_pre = rotary_embedding(
        (grad_query * score_scale).reshape(query_pre.shape), token_position, -1.0
    )
    grad_query_pre = grad_query_pre.reshape(2 * count, q_width).astype(BF16)
    grad_key_pre = rotary_embedding(grad_keys * score_scale, token_position, -1.0)
    grad_key_pre = grad_key_pre.reshape(2 * count, kv_width).astype(BF16)
    grad_qk_pre = jnp.concatenate([grad_query_pre, grad_key_pre], axis=1)
    grad_qk_pre, grad_value_pre, second_one, out_sum = sync(
        grad_qk_pre, grad_value_pre, second_one, out_sum
    )
    out_sum = sum_along(out_sum, "x")
    grad_w_qk = dot(normalized_input, grad_qk_pre, ((0,), (0,))).astype(BF16)
    grad_w_v = dot(normalized_input, grad_value_pre, ((0,), (0,))).astype(BF16)
    grad_normed = dot(grad_qk_pre, w_qk, ((1,), (1,)))
    grad_normed = grad_normed + dot(grad_value_pre, w_v, ((1,), (1,)))
    grad_normed, other_normed, second_two, grad_w_qk, grad_w_v, result_step = sync(
        grad_normed[:count],
        ring_step(grad_normed[count:], "c"),
        second_two,
        grad_w_qk,
        grad_w_v,
        result_step,
    )
    result_step = ring_step(plus(result_step, results_sum[3]), "z")
    second_sum = finish_in(second_grads, second_one, second_two)
    grad_normed = grad_normed + other_normed
    grad_rows, grad_gain_one = norm_back(grad_normed, own_act, r_one[:count], gain_first)
    grad_rows = grad_resid + grad_rows

    grad_small = jnp.concatenate(
        [grad_w_router, grad_gain_one[:, None], grad_gain_two[:, None]], axis=1
    )
    grad_small = jnp.pad(grad_small, ((0, 0), (0, LANES - grad_small.shape[1])))
    q_parts = pick_weights([(grad_w_qk, 0, q_width)], "x", "y", True)
    rest = [
        (grad_w_qk, q_width, kv_width),
        (grad_w_v, 0, kv_width),
        (grad_small.astype(BF16), 0, LANES),
    ]
    rest_parts = pick_weights(rest, "y", "x", True)
    q_parts, rest_parts, grad_rows, grad_chunks, out_sum, result_zero, first_pieces, second_sum = sync(
        q_parts, rest_parts, grad_rows, grad_chunks, out_sum, result_zero, first_pieces, second_sum
    )
    second_pieces = lax.all_to_all(second_sum, "z", 0, 0, tiled=True)
    grad_w_back, q_sum, rest_sum = sync(
        expert_grads(grad_chunks, weighted, 0, local_count, width, True),
        ring_sum(q_parts, "y", BF16),
        ring_sum(rest_parts, "x", BF16),
    )
    back_x = ring_step(grad_w_back[1], "x")
    q_sum, rest_sum, out_sum, first_pieces, second_pieces, result_step = sync(
        sum_along(q_sum, "x"),
        sum_along(rest_sum, "y"),
        out_sum,
        first_pieces,
        second_pieces,
        result_step,
    )
    grad_gate_up = unpack_experts(first_pieces, *ranges[0], local_count, [])
    outputs = resid + plus(result_step, end_y(results_c[0], result_zero), F32)
    grad_first, grad_second, grad_w_out, grad_gate_up, outputs = sync(
        *[sum_along(part, "z", F32) for part in (q_sum, rest_sum, out_sum)],
        grad_gate_up,
        outputs,
    )
    grad_w_gate, grad_w_up = unpack_experts(
        second_pieces, *ranges[1], local_count, list(grad_gate_up)
    )
    grad_w_down = finish_x(grad_w_back, back_x, F32)
    grad_both = jnp.concatenate([grad_first, grad_second], axis=-1)
    mine = lax.dynamic_index_in_dim(grad_both, core, 0, keepdims=False)
    theirs = lax.dynamic_index_in_dim(grad_both, 1 - core, 0, keepdims=False)
    got = ring_step(theirs, "c")

    def whole_columns(start, columns):
        parts = [part[:, start : start + columns].reshape(own_rows, y_size, -1) for part in (mine, got)]
        ordered = jnp.where(core == 0, jnp.stack(parts, 2), jnp.stack(parts[::-1], 2))
        return ordered.reshape(own_rows, 2 * columns)

    grad_small = (mine + got)[:, q_width + 2 * kv_width :]
    return (
        outputs.astype(BF16).reshape(inputs.shape),
        grad_rows.reshape(inputs.shape),
        grad_small[:, E],
        whole_columns(0, q_width),
        whole_columns(q_width, kv_width),
        whole_columns(q_width + kv_width, kv_width),
        grad_w_out,
        grad_small[:, E + 1],
        grad_small[:, :E],
        grad_w_gate,
        grad_w_up,
        grad_w_down,
    )


def solution(mesh):
    experts, shards = mesh.shape["expert"], mesh.shape["shard"]
    split = Mesh(
        mesh.devices.reshape(experts // 2, 2, SLICES, shards // SLICES), ("y", "c", "z", "x")
    )
    groups, within = ("y", "c"), ("z", "x")
    tokens = P(None, ALL, None)
    rows = P(ALL, None)
    expert = P(groups, within, None)
    return jax.shard_map(
        body,
        mesh=split,
        in_specs=(tokens,) * 4
        + (P(ALL), rows, rows, rows, rows, P(ALL), rows, expert, expert, expert),
        out_specs=(tokens, tokens, P(ALL), rows, rows, rows, rows, P(ALL), rows)
        + (expert, expert, expert),
        check_vma=False,
    )
```

```python
import functools
import itertools
import math

import jax
import jax.numpy as jnp
from jax import lax
from jax.experimental import pallas as pl
from jax.experimental.pallas import tpu as pltpu
from jax.experimental.layout import Layout, with_layout_constraint
from jax.sharding import Mesh, PartitionSpec as P

MODEL_WIDTH = 1536
QUERY_HEADS = 24
KEY_VALUE_HEADS = 8
HEAD_SIZE = 64
QUERY_PER_GROUP = QUERY_HEADS // KEY_VALUE_HEADS
E = 40
TOPK = 8
SLICES = 4
LANES = 128
VMEM_BYTES = 60 * 1024 * 1024

ALL = ("y", "c", "z", "x")
epsilon = 1e-05
F32 = jnp.float32
BF16 = jnp.bfloat16


def dot(left, right, dims=((1,), (0,))):
    return lax.dot_general(left, right, (dims, ((), ())), preferred_element_type=F32)


def sync(*values):
    return lax.optimization_barrier(values)


def ring_step(array, axis):
    size = lax.axis_size(axis)
    return lax.ppermute(array, axis, [(i, (i + 1) % size) for i in range(size)])


def ring_gather(block, axis):
    blocks = [block]
    for _ in range(lax.axis_size(axis) - 1):
        blocks.append(ring_step(blocks[-1], axis))
    return blocks


def ring_sum(parts, axis, kind):
    total = parts[1]
    for part in list(parts[2:]) + [parts[0]]:
        total = ring_step(total, axis).astype(F32) + part.astype(F32)
        total = total.astype(kind if part is parts[0] else part.dtype)
    return total


def direct_sum(parts, axis, kind):
    size = lax.axis_size(axis)
    total = parts[0].astype(F32)
    for step in range(1, size):
        to = [(i, (i - step) % size) for i in range(size)]
        total = total + lax.ppermute(parts[step], axis, to).astype(F32)
    return total.astype(kind)


def index_at(axis, step):
    return (lax.axis_index(axis) - step) % lax.axis_size(axis)


def move_kernel(moves, count_in, count_out, place_ref, *refs):
    sources, targets = refs[:count_in], refs[count_in : count_in + count_out]
    held, sems = refs[count_in + count_out : -1], refs[-1]
    copies = [[] for _ in targets]
    for number, (source, from_index, target, to_index) in enumerate(moves):
        picked = [
            tuple(place_ref[i[0]] if isinstance(i, tuple) else i for i in index)
            for index in (from_index, to_index)
        ]
        copy = pltpu.make_async_copy(
            sources[source].at[picked[0]], held[target].at[picked[1]], sems.at[number]
        )
        copy.start()
        copies[target].append(copy)
    out = []
    for target, arriving in enumerate(copies):
        for copy in arriving:
            copy.wait()
        out.append(
            pltpu.make_async_copy(held[target], targets[target], sems.at[len(moves) + target])
        )
        out[-1].start()
    for copy in out:
        copy.wait()


def move(moves, places, sources, shapes, name):
    anywhere = pl.BlockSpec(memory_space=pl.ANY)
    total = sum(math.prod(s.shape) * s.dtype.itemsize for s in shapes)
    return pl.pallas_call(
        functools.partial(move_kernel, moves, len(sources), len(shapes)),
        in_specs=[pl.BlockSpec(memory_space=pltpu.SMEM)] + [anywhere] * len(sources),
        out_specs=[anywhere] * len(shapes),
        out_shape=shapes,
        scratch_shapes=[pltpu.VMEM(s.shape, s.dtype) for s in shapes]
        + [pltpu.SemaphoreType.DMA((len(moves) + len(shapes),))],
        compiler_params=pltpu.CompilerParams(vmem_limit_bytes=VMEM_BYTES),
        cost_estimate=pl.CostEstimate(flops=0, bytes_accessed=2 * total, transcendentals=0),
        name=name,
    )(jnp.stack(places).astype(jnp.int32), *sources)


def places_of(axes):
    places, where = [], {}
    for axis in axes:
        for step in range(lax.axis_size(axis)):
            where[axis, step] = (len(places),)
            places.append(index_at(axis, step))
    return places, where


def place_weights(gathers):
    places, where = places_of(("y", "z", "x"))
    sizes = [lax.axis_size(axis) for axis in ("y", "z", "x")]
    moves, sources, shapes = [], [], []
    for number, blocks in enumerate(gathers):
        for (y_step, z_first, x_step), part in blocks.items():
            for i in range(part.shape[0]):
                spot = (where["y", y_step], slice(None), where["z", z_first + i], where["x", x_step])
                moves.append((len(sources), (i,), number, spot))
            sources.append(part)
        shape = (sizes[0], 2) + tuple(sizes[1:]) + sources[-1].shape[2:]
        shapes.append(jax.ShapeDtypeStruct(shape, sources[-1].dtype))
    whole = move(moves, places, sources, shapes, "place_weights")
    return [part.reshape(-1, part.shape[-1]) for part in whole]


def pick_weights(grads, first, second, with_core):
    sizes = {axis: lax.axis_size(axis) for axis in ("y", "z", "x")}
    core = (2,) if with_core else ()
    places, where = places_of(("y", "z", "x"))
    moves, sources, start = [], [], 0
    for number, (grad, column, columns) in enumerate(grads):
        shape = (sizes["y"],) + core + (sizes["z"], sizes["x"], -1, grad.shape[-1])
        sources.append(grad.reshape(shape))
        rows = slice(None)
        for y_step, z_step, x_step in itertools.product(
            range(sizes["y"]), range(sizes["z"]), range(sizes["x"])
        ):
            spot = [where["y", y_step], where["z", z_step], where["x", x_step]]
            if with_core:
                spot.insert(1, rows)
            spot += [rows, pl.ds(column, columns)]
            steps = {"y": y_step, "x": x_step}
            to = (steps[first], z_step) + (rows,) * (1 + len(core)) + (pl.ds(start, columns),)
            moves.append((number, tuple(spot), steps[second], to))
        start = start + columns
    tail = core + (sources[0].shape[-2], start)
    shape = jax.ShapeDtypeStruct((sizes[first], sizes["z"]) + tail, sources[0].dtype)
    return move(moves, places, sources, [shape] * sizes[second], "pick_weights")


def sum_along(parts, axis, kind=BF16):
    return ring_sum([parts[i] for i in range(parts.shape[0])], axis, kind)


def pack_kernel(gate_ref, up_ref, out_ref):
    width = out_ref.shape[-1] // 2
    for z in range(out_ref.shape[0]):
        out_ref[z, :, :width] = gate_ref[0, :, z * width : (z + 1) * width]
        out_ref[z, :, width:] = up_ref[0, :, z * width : (z + 1) * width]


def pack_experts(w_gate, w_up, first, last, slices):
    rows, hidden = w_gate.shape[1:]
    spec = pl.BlockSpec((1, rows, hidden), lambda e: (first + e, 0, 0))
    width = 2 * hidden // slices
    return pl.pallas_call(
        pack_kernel,
        grid=(last - first,),
        in_specs=[spec, spec],
        out_specs=pl.BlockSpec((slices, rows, width), lambda e: (0, 0, e)),
        out_shape=jax.ShapeDtypeStruct((slices, rows, (last - first) * width), w_gate.dtype),
        name="pack_experts",
    )(w_gate, w_up)


def unpack_kernel(part_ref, *refs):
    gate_ref, up_ref = refs[-2:]
    slices = part_ref.shape[0]
    width = gate_ref.shape[-1] // slices
    for z in range(slices):
        both = part_ref[z].astype(F32)
        gate_ref[0, :, z * width : (z + 1) * width] = both[:, :width]
        up_ref[0, :, z * width : (z + 1) * width] = both[:, width:]


def unpack_experts(part, first, last, local_count, earlier):
    slices, rows, columns = part.shape
    width = columns // (last - first)
    spec = pl.BlockSpec((1, rows, width // 2 * slices), lambda e: (first + e, 0, 0))
    shape = jax.ShapeDtypeStruct((local_count, rows, width // 2 * slices), F32)
    anywhere = pl.BlockSpec(memory_space=pl.ANY)
    return pl.pallas_call(
        unpack_kernel,
        grid=(last - first,),
        in_specs=[pl.BlockSpec((slices, rows, width), lambda e: (0, 0, e))]
        + [anywhere] * len(earlier),
        out_specs=[spec, spec],
        out_shape=[shape, shape],
        input_output_aliases={1 + i: i for i in range(len(earlier))},
        name="unpack_experts",
    )(part, *earlier)


def experts_kernel(counts, steps, x_size, place_ref, *refs):
    parts = len(counts)
    rows_in, grads_in, refs = refs[:steps], refs[steps : 2 * steps], refs[2 * steps :]
    w_in_parts, refs = [refs[i * x_size : (i + 1) * x_size] for i in range(parts)], refs[parts * x_size :]
    w_back_parts, refs = refs[:x_size], refs[x_size:]
    results, grads, (active_ref, hidden_ref, gates_ref) = refs[:2], refs[2:4], refs[4:7]
    rows_buf, grads_buf = refs[7:9]
    w_in, w_back, sems = refs[9 : 9 + parts], refs[9 + parts], refs[10 + parts]
    step = pl.program_id(0)
    half = steps // 2
    weights, late = [[] for _ in counts], [[] for _ in range(steps)]
    number = 0

    def copy_of(source, target):
        nonlocal number
        number = number + 1
        return pltpu.make_async_copy(source, target, sems.at[number - 1])

    first = 0
    for part, count in enumerate(counts):
        for x_step in range(x_size):
            place = place_ref[1 + x_step]
            source = w_in_parts[part][x_step]
            size = source.shape[1]
            for z in range(source.shape[0]):
                start = pl.multiple_of((z * x_size + place) * size, size)
                weights[part].append(copy_of(source.at[z], w_in[part].at[pl.ds(start, size)]))
            source = w_back_parts[x_step]
            size = source.shape[1]
            for e in range(first, first + count):
                start = pl.multiple_of((e * x_size + place) * size, size)
                weights[part].append(copy_of(source.at[e], w_back.at[pl.ds(start, size)]))
        first = first + count
    for i in range(steps):
        late[i] = [copy_of(rows_in[i], rows_buf.at[i]), copy_of(grads_in[i], grads_buf.at[i])]

    @pl.when(step == 0)
    def _():
        for some in late[:1] + weights + late[1:]:
            for copy in some:
                copy.start()

    for i in range(steps):

        @pl.when(step == i)
        def _(i=i):
            for copy in late[i]:
                copy.wait()

    local_count = sum(counts)
    width = w_back.shape[0] // local_count
    rows = rows_buf[step, :, :MODEL_WIDTH]
    grad_rows = grads_buf[step]
    first = place_ref[0] * local_count
    source = lax.broadcasted_iota(jnp.int32, (LANES, LANES), 0)
    wanted = lax.broadcasted_iota(jnp.int32, (LANES, LANES), 1) + first
    choose = ((source == wanted) | (source == wanted + E)).astype(F32).astype(BF16)
    gates = dot(rows_buf[step, :, MODEL_WIDTH:], choose)
    lane = lax.broadcasted_iota(jnp.int32, gates.shape, 1)
    grad_gates = jnp.zeros(gates.shape, F32)
    expert = 0
    for part, count in enumerate(counts):

        @pl.when(step == 0)
        def _(part=part):
            for copy in weights[part]:
                copy.wait()

        all_hidden = dot(rows, w_in[part][...])
        all_plain = dot(
            grad_rows, w_back[expert * width : (expert + count) * width, :], ((1,), (1,))
        )
        for i in range(count):
            here = slice(expert * width, (expert + 1) * width)
            hidden = all_hidden[:, 2 * width * i : 2 * width * (i + 1)]
            grad_plain = all_plain[:, width * i : width * (i + 1)]
            gate_part, up_part = hidden[:, :width], hidden[:, width:]
            sigmoid_gate = 1.0 / (1.0 + jnp.exp(-gate_part))
            silu = gate_part * sigmoid_gate
            active = silu * up_part
            weight = gates[:, expert : expert + 1]
            total = jnp.sum(active * grad_plain, axis=1, keepdims=True)
            grad_gates = jnp.where(lane == first + expert, total, grad_gates)
            active_ref[:, here] = (weight * active).astype(BF16)
            grad_active = weight * grad_plain
            start = 2 * width * expert
            hidden_ref[:, start : start + width] = (
                grad_active * up_part * (sigmoid_gate + silu * (1.0 - sigmoid_gate))
            ).astype(BF16)
            hidden_ref[:, start + width : start + 2 * width] = (grad_active * silu).astype(BF16)
            expert = expert + 1
    gates_ref[0] = grad_gates.T[:E]
    result = dot(active_ref[...], w_back[...]).astype(BF16)
    grad_in = jnp.zeros(rows.shape, F32)
    start = 0
    for part, count in enumerate(counts):
        size = 2 * width * count
        grad_in += dot(hidden_ref[:, start : start + size], w_in[part][...], ((1,), (1,)))
        start = start + size
    grad_in = grad_in.astype(BF16)

    for side, now in enumerate((step < half, step >= half)):

        @pl.when(now)
        def _(side=side):
            results[side][0] = result
            grads[side][0] = grad_in


def run_experts(rows, grads, w_in_parts, w_back_parts, counts, group):
    count, wide = rows[0].shape
    steps = len(rows)
    half = steps // 2
    local_count = sum(counts)
    x_size = len(w_in_parts[0])
    z_size, own_rows, columns = w_in_parts[0][0].shape
    width = columns // (2 * counts[0])
    copies = 2 * steps + x_size * (len(counts) * z_size + local_count)
    places, _ = places_of(("x",))
    anywhere = pl.BlockSpec(memory_space=pl.ANY)
    own = pl.BlockSpec((1, count, MODEL_WIDTH), lambda i: (jnp.minimum(i, half - 1), 0, 0))
    other = pl.BlockSpec((1, count, MODEL_WIDTH), lambda i: (jnp.maximum(i - half, 0), 0, 0))

    def by_row(columns):
        return pl.BlockSpec((count, columns), lambda i: (i, 0))

    side = jax.ShapeDtypeStruct((half, count, MODEL_WIDTH), BF16)
    flops = 2 * steps * count * MODEL_WIDTH * 6 * local_count * width
    return pl.pallas_call(
        functools.partial(experts_kernel, counts, steps, x_size),
        grid=(steps,),
        in_specs=[pl.BlockSpec(memory_space=pltpu.SMEM)]
        + [anywhere] * (2 * steps + (len(counts) + 1) * x_size),
        out_specs=[own, other, own, other]
        + [by_row(local_count * width), by_row(2 * local_count * width)]
        + [pl.BlockSpec((1, E, count), lambda i: (i, 0, 0))],
        out_shape=[side] * 4
        + [
            jax.ShapeDtypeStruct((steps * count, local_count * width), BF16),
            jax.ShapeDtypeStruct((steps * count, 2 * local_count * width), BF16),
            jax.ShapeDtypeStruct((steps, E, count), F32),
        ],
        scratch_shapes=[
            pltpu.VMEM((steps, count, wide), BF16),
            pltpu.VMEM((steps, count, MODEL_WIDTH), BF16),
        ]
        + [pltpu.VMEM((MODEL_WIDTH, part[0].shape[-1]), BF16) for part in w_in_parts]
        + [
            pltpu.VMEM((local_count * width, MODEL_WIDTH), BF16),
            pltpu.SemaphoreType.DMA((copies,)),
        ],
        compiler_params=pltpu.CompilerParams(vmem_limit_bytes=VMEM_BYTES),
        cost_estimate=pl.CostEstimate(
            flops=flops, bytes_accessed=30 * 1024 * 1024, transcendentals=0
        ),
        name="experts",
    )(
        jnp.stack([group] + places).astype(jnp.int32),
        *rows,
        *grads,
        *[part for parts in w_in_parts for part in parts],
        *w_back_parts,
    )


def expert_grads_kernel(count_left, count_right, back, place_ref, *refs):
    whole = refs[:count_left]
    columns = refs[count_left : count_left + count_right]
    outs, (buf, total, sems) = refs[count_left + count_right : -3], refs[-3:]
    rows_each = whole[0].shape[0]

    @pl.when(pl.program_id(0) == 0)
    def _():
        copies = [
            pltpu.make_async_copy(
                part.at[:, pl.ds(0, MODEL_WIDTH)],
                buf.at[pl.ds(number * rows_each, rows_each)],
                sems.at[number],
            )
            for number, part in enumerate(whole)
        ]
        for copy in copies:
            copy.start()
        for copy in copies:
            copy.wait()

    size = columns[0].shape[0]
    for i, part in enumerate(columns):
        rows = buf[i * size : (i + 1) * size, :]
        if back:
            term = dot(part[...], rows, ((0,), (0,)))
        else:
            term = dot(rows, part[...], ((0,), (0,)))
        if i == 0:
            total[...] = term
        else:
            total[...] += term
    blocks, own = outs[0].shape[0], outs[0].shape[1]
    devices = len(outs) if back else len(outs) // 2
    for number, out in enumerate(outs):
        step, half = (number, 0) if back else (number // 2, number % 2)
        for i in range(blocks):
            block = half * blocks + i
            start = pl.multiple_of((block * devices + place_ref[step]) * own, own)
            out[i] = total[pl.ds(start, own), :].astype(BF16)


def expert_grads(whole, columns, first, last, width, back):
    x_size = lax.axis_size("x")
    places, _ = places_of(("x",))
    tokens = len(whole) * whole[0].shape[0]
    experts = last - first
    anywhere = pl.BlockSpec(memory_space=pl.ANY)
    column = pl.BlockSpec((columns[0].shape[0], width), lambda e: (0, first + e))
    outs = x_size if back else 2 * x_size
    if back:
        own = width // x_size
        block = (1, own, MODEL_WIDTH)
        shape = (experts, own, MODEL_WIDTH)
        out = pl.BlockSpec(block, lambda e: (e, 0, 0))
        total = (width, MODEL_WIDTH)
    else:
        z_size = lax.axis_size("z")
        own = MODEL_WIDTH // (z_size * x_size)
        shape = (z_size // 2, own, experts * width)
        out = pl.BlockSpec((z_size // 2, own, width), lambda e: (0, 0, e))
        total = (MODEL_WIDTH, width)
    return pl.pallas_call(
        functools.partial(expert_grads_kernel, len(whole), len(columns), back),
        grid=(experts,),
        in_specs=[pl.BlockSpec(memory_space=pltpu.SMEM)]
        + [anywhere] * len(whole)
        + [column] * len(columns),
        out_specs=[out] * outs,
        out_shape=[jax.ShapeDtypeStruct(shape, BF16)] * outs,
        scratch_shapes=[
            pltpu.VMEM((tokens, MODEL_WIDTH), BF16),
            pltpu.VMEM(total, F32),
            pltpu.SemaphoreType.DMA((len(whole),)),
        ],
        compiler_params=pltpu.CompilerParams(vmem_limit_bytes=VMEM_BYTES),
        cost_estimate=pl.CostEstimate(
            flops=2 * tokens * MODEL_WIDTH * width * experts,
            bytes_accessed=2 * tokens * (MODEL_WIDTH + width * experts),
            transcendentals=0,
        ),
        name="expert_grads",
    )(jnp.stack(places).astype(jnp.int32), *whole, *columns)


def positions(lengths, count_of_tokens):
    seq_ends = jnp.cumsum(lengths, axis=-1)
    starts = seq_ends - lengths
    token_index = jnp.arange(count_of_tokens, dtype=jnp.int32)
    segment = jnp.sum((token_index[:, None] >= seq_ends[..., None, :]).astype(jnp.int32), axis=-1)
    choose = segment[..., None] == jnp.arange(lengths.shape[-1], dtype=jnp.int32)
    offset = jnp.sum(jnp.where(choose, starts[..., None, :], 0), axis=-1)
    return (segment, token_index - offset)


def rotary_tables(token_position):
    half_size = HEAD_SIZE // 2
    frequency = jnp.exp(jnp.arange(half_size, dtype=F32) * (-math.log(10000.0) / half_size))
    angles = token_position.astype(F32)[:, None] * frequency
    cosine, sine_part = jnp.cos(angles), jnp.sin(angles)
    repeat = LANES // HEAD_SIZE
    return (
        jnp.concatenate([cosine, cosine] * repeat, axis=1),
        jnp.concatenate([-sine_part, sine_part] * repeat, axis=1),
    )


def rotate(values, cosine, sine_part, direction):
    lane = lax.broadcasted_iota(jnp.int32, (values.shape[0], LANES), 1)
    first = lane % HEAD_SIZE < HEAD_SIZE // 2
    tiles = []
    for start in range(0, values.shape[1], LANES):
        tile = values[:, start : start + LANES]
        after = pltpu.roll(tile, LANES - HEAD_SIZE // 2, 1)
        before = pltpu.roll(tile, HEAD_SIZE // 2, 1)
        swapped = jnp.where(first, after, before)
        tiles.append(tile * cosine + direction * swapped * sine_part)
    return jnp.concatenate(tiles, axis=1)


def allowed_pairs(column_ref, row_ref):
    shape = column_ref.shape
    same = column_ref[...] == row_ref[0, :1, :]
    earlier = lax.broadcasted_iota(jnp.int32, shape, 0) >= lax.broadcasted_iota(jnp.int32, shape, 1)
    return jnp.concatenate([same & earlier] * QUERY_PER_GROUP, axis=0)


def group_rows(rows, group):
    heads = [group * QUERY_PER_GROUP + i for i in range(QUERY_PER_GROUP)]
    return jnp.concatenate([rows[:, HEAD_SIZE * h : HEAD_SIZE * (h + 1)] for h in heads], axis=0)


def probabilities(query, keys, allowed):
    scores = dot(query, keys, ((1,), (1,))) * (1.0 / math.sqrt(HEAD_SIZE))
    scores = jnp.where(allowed, scores, -1000000000.0)
    shifted = jnp.exp(scores - jnp.max(scores, axis=-1, keepdims=True))
    return shifted / jnp.sum(shifted, axis=-1, keepdims=True)


def attention_kernel(
    qk_ref, value_ref, cos_ref, sin_ref, column_ref, row_ref, query_ref, key_ref, mixed_ref
):
    width = query_ref.shape[1]
    block = query_ref.shape[0]
    rotated = rotate(qk_ref[...], cos_ref[...], sin_ref[...], 1.0).astype(BF16)
    query_ref[...] = rotated[:, :width]
    key_ref[...] = rotated[:, width:]
    allowed = allowed_pairs(column_ref, row_ref)
    for group in range(key_ref.shape[1] // HEAD_SIZE):
        here = slice(HEAD_SIZE * group, HEAD_SIZE * (group + 1))
        query = group_rows(query_ref[...], group)
        probs = probabilities(query, key_ref[:, here], allowed)
        mixed = dot(probs.astype(BF16), value_ref[:, here]).astype(BF16)
        for i in range(QUERY_PER_GROUP):
            start = HEAD_SIZE * (group * QUERY_PER_GROUP + i)
            mixed_ref[:, start : start + HEAD_SIZE] = mixed[block * i : block * (i + 1)]


def attention_back_kernel(
    query_ref,
    key_ref,
    value_ref,
    grad_ref,
    cos_ref,
    sin_ref,
    column_ref,
    row_ref,
    grad_qk_ref,
    grad_value_ref,
    total,
):
    width = query_ref.shape[1]
    block = query_ref.shape[0]
    scale = 1.0 / math.sqrt(HEAD_SIZE)
    allowed = allowed_pairs(column_ref, row_ref)
    for group in range(key_ref.shape[1] // HEAD_SIZE):
        here = slice(HEAD_SIZE * group, HEAD_SIZE * (group + 1))
        query = group_rows(query_ref[...], group)
        grad_mixed = group_rows(grad_ref[...], group)
        probs = probabilities(query, key_ref[:, here], allowed)
        grad_probs = dot(grad_mixed, value_ref[:, here], ((1,), (1,)))
        grad_value_ref[:, here] = dot(probs.astype(BF16), grad_mixed, ((0,), (0,))).astype(BF16)
        spread = jnp.sum(probs * grad_probs, axis=-1, keepdims=True)
        grad_scores = (probs * (grad_probs - spread)).astype(BF16)
        grad_query = dot(grad_scores, key_ref[:, here]) * scale
        for i in range(QUERY_PER_GROUP):
            start = HEAD_SIZE * (group * QUERY_PER_GROUP + i)
            total[:, start : start + HEAD_SIZE] = grad_query[block * i : block * (i + 1)]
        start = width + HEAD_SIZE * group
        total[:, start : start + HEAD_SIZE] = dot(grad_scores, query, ((0,), (0,))) * scale
    grad_qk_ref[...] = rotate(total[...], cos_ref[...], sin_ref[...], -1.0).astype(BF16)


def attention_call(kernel, arrays, widths, tables, block, scratch, name):
    rows = arrays[0].shape[0]

    def by_row(columns):
        return pl.BlockSpec((block, columns), lambda i: (i, 0))

    return pl.pallas_call(
        kernel,
        grid=(rows // block,),
        in_specs=[by_row(a.shape[1]) for a in list(arrays) + list(tables[:3])]
        + [pl.BlockSpec((1,) + tables[3].shape[1:], lambda i: (i, 0, 0))],
        out_specs=[by_row(width) for width in widths],
        out_shape=[jax.ShapeDtypeStruct((rows, width), BF16) for width in widths],
        scratch_shapes=scratch,
        compiler_params=pltpu.CompilerParams(vmem_limit_bytes=VMEM_BYTES // 2),
        cost_estimate=pl.CostEstimate(
            flops=2 * rows * block * 4 * MODEL_WIDTH, bytes_accessed=8 << 20, transcendentals=0
        ),
        name=name,
    )(*arrays, *tables)


def norm_back(grad_normed, values_in, inverse_root, gain):
    scaled = grad_normed * gain
    grad_gain = jnp.sum(grad_normed * values_in * inverse_root, axis=0)
    cubed = inverse_root * inverse_root * inverse_root
    grad_values = inverse_root * scaled - values_in * cubed * jnp.mean(
        scaled * values_in, axis=-1, keepdims=True
    )
    return (grad_values, grad_gain)


def body(
    inputs,
    cotangent,
    lengths,
    routes,
    norm_gain_one,
    w_query,
    key_projection_weight,
    value_projection_weight,
    w_out,
    norm_gain_two,
    w_router,
    w_gate,
    w_up,
    w_down,
):
    micro, block, _ = inputs.shape
    count = micro * block
    local_count = w_gate.shape[0]
    y_size, z_size, x_size = lax.axis_size("y"), lax.axis_size("z"), lax.axis_size("x")
    core = lax.axis_index("c")
    group = lax.axis_index("y") * 2 + core
    own_rows = w_query.shape[0]
    q_width, kv_width = MODEL_WIDTH // 2, KEY_VALUE_HEADS * HEAD_SIZE // 2
    kv_heads = KEY_VALUE_HEADS // 2

    def columns_of(weight, which):
        split = weight.reshape(own_rows, y_size, 2, -1)
        return lax.dynamic_index_in_dim(split, which, 2, keepdims=False).reshape(own_rows, -1)

    small = jnp.concatenate([w_router, norm_gain_one[:, None], norm_gain_two[:, None]], axis=1)
    small = jnp.pad(small, ((0, 0), (0, LANES - small.shape[1])))

    def both_cores(arrays):
        mine = jnp.concatenate([columns_of(a, core) for a in arrays], axis=1)
        theirs = jnp.concatenate([columns_of(a, 1 - core) for a in arrays], axis=1)
        return mine, theirs

    mine, theirs = both_cores([w_query, key_projection_weight, value_projection_weight])
    got, other_lengths = sync(
        ring_step(jnp.concatenate([theirs, small], axis=1), "c"), ring_step(lengths, "c")
    )
    mine = jnp.concatenate([mine, small], axis=1)
    both = jnp.where(core == 0, jnp.stack([mine, got]), jnp.stack([got, mine]))
    both = jnp.concatenate(
        [
            both[..., : q_width + kv_width],
            both[..., q_width + 2 * kv_width :],
            both[..., q_width + kv_width : q_width + 2 * kv_width],
            jnp.stack([w_out[:, :q_width], w_out[:, q_width:]]),
        ],
        axis=-1,
    )
    counts = [local_count // 2, local_count - local_count // 2]
    ranges = [(0, counts[0]), (counts[0], local_count)]
    grad_final_low = cotangent.reshape(count, MODEL_WIDTH)
    grads_z = [grad_final_low]
    grads_ahead = ring_step(grad_final_low, "z")
    grads_y = [ring_gather(grad_final_low, "y")]
    down_parts = ring_gather(w_down, "x")
    pair = z_size // 2
    first_width = q_width + kv_width + LANES
    first_blocks, second_blocks = {}, {}

    def first_hops(blocks):
        rows = jnp.stack(blocks)
        return ring_gather(rows[..., :first_width], "x"), ring_gather(rows[..., first_width:], "y")

    def second_hops(by_x, by_y, z_first):
        for x_step, one in enumerate(by_x):
            for y_step, two in enumerate(ring_gather(one, "y")):
                first_blocks[y_step, z_first, x_step] = two
        for y_step, one in enumerate(by_y):
            for x_step, two in enumerate(ring_gather(one, "x")):
                second_blocks[y_step, z_first, x_step] = two

    z_blocks = [both]
    for _ in range(pair - 1):
        z_blocks.append(ring_step(z_blocks[-1], "z"))
    others = ring_step(inputs, "c")
    packed = [pack_experts(w_gate, w_up, first, last, z_size) for first, last in ranges]
    z_blocks, others, grads_ahead, grads_y, packed = sync(
        z_blocks, others, grads_ahead, grads_y, packed
    )
    other_inputs = others
    grads_z.append(grads_ahead)
    ahead = []
    for _ in range(pair):
        ahead.append(ring_step((z_blocks + ahead)[-1], "z"))
    hops, ahead, down_parts, packed = sync(first_hops(z_blocks), ahead, down_parts, packed)
    swapped = lax.all_to_all(packed[0], "z", 0, 0, tiled=True)
    second_hops(*hops, 0)
    first_blocks, second_blocks, ahead = sync(first_blocks, second_blocks, ahead)
    hops, grads_z = sync(first_hops(ahead), grads_z)
    second_hops(*hops, pair)
    first_blocks, second_blocks, swapped, packed, grads_z = sync(
        first_blocks, second_blocks, swapped, packed, grads_z
    )
    grads_y.append(ring_gather(grads_z[1], "y"))
    first_parts = ring_gather(swapped, "x")
    swapped = lax.all_to_all(packed[1], "z", 0, 0, tiled=True)
    w_first, w_second = place_weights([first_blocks, second_blocks])
    w_qk = w_first[:, : q_width + kv_width]
    small = w_first[:, q_width + kv_width :]
    w_v = w_second[:, :kv_width]
    w_out = w_second[:, kv_width:].reshape(y_size, 2, -1, q_width).transpose(0, 2, 1, 3)
    w_out = w_out.reshape(q_width, MODEL_WIDTH)
    w_router = small[:, :E]
    gain_first = small[:, E].astype(F32)
    gain_second = small[:, E + 1].astype(F32)

    all_inputs = jnp.stack([inputs, other_inputs])
    all_lengths = jnp.concatenate([lengths[:, 0], other_lengths[:, 0]])
    act_rows = all_inputs.reshape(2 * count, MODEL_WIDTH).astype(F32)
    grad_final = grad_final_low.astype(F32)
    r_one = lax.rsqrt(jnp.mean(act_rows * act_rows, axis=-1) + epsilon)[:, None]
    normalized_input = (act_rows * r_one * gain_first).astype(BF16)
    segment, token_position = positions(all_lengths, block)
    blocks = 2 * micro
    qk_pre = dot(normalized_input, w_qk)
    values = dot(normalized_input, w_v).astype(BF16)
    qk_pre, values, grads_y[0] = sync(qk_pre, values, grads_y[0])
    grads_other = [[ring_step(part, "c") for part in grads_y[0]]]
    tables = rotary_tables(token_position.reshape(-1)) + (
        jnp.broadcast_to(segment.reshape(-1, 1), (blocks * block, block)),
        jnp.broadcast_to(segment[:, None, :], (blocks, 8, block)),
    )
    query, keys, mixed = attention_call(
        attention_kernel,
        [qk_pre, values],
        [q_width, kv_width, q_width],
        tables,
        block,
        [],
        "attention",
    )
    projected = dot(mixed, w_out)
    projected, first_parts, swapped, grads_other, grads_y = sync(
        projected, first_parts, swapped, grads_other, grads_y
    )
    second_parts = ring_gather(swapped, "x")
    grads_other.append([ring_step(part, "c") for part in grads_y[1]])
    own_act = act_rows[:count]
    resid = own_act + ring_sum([projected[:count], projected[count:]], "c", F32)

    r_two = lax.rsqrt(jnp.mean(resid * resid, axis=-1) + epsilon)[:, None]
    normed_two = (resid * r_two * gain_second).astype(BF16)
    chance = jax.nn.softmax(dot(normed_two, w_router), axis=-1)
    choice = routes.reshape(count, TOPK)
    chosen = jnp.any(choice[..., None] == jnp.arange(E, dtype=jnp.int32), axis=1).astype(F32)
    picked = chance * chosen
    picked_total = jnp.sum(picked, axis=-1, keepdims=True)
    gates = picked / picked_total

    high = lax.reduce_precision(gates, 8, 7)
    low = gates - high
    spare = jnp.zeros((count, LANES - 2 * E), BF16)
    sent = jnp.concatenate([normed_two, high.astype(BF16), low.astype(BF16), spare], axis=1)
    sent, grads_other = sync(sent, grads_other)
    rows, ahead, second_parts, others = sync(
        ring_gather(sent, "y"), ring_step(sent, "z"), second_parts, ring_step(sent, "c")
    )
    w_in_parts, w_back_parts = [first_parts, second_parts], down_parts
    rows, others = sync(rows, [others] + [ring_step(part, "c") for part in rows[1:]])
    width = w_in_parts[0][0].shape[-1] // (2 * counts[0])

    def plus(first, second, kind=BF16):
        return (first.astype(F32) + second.astype(F32)).astype(kind)

    def plus_all(first, second):
        return [plus(first[i], second[i]) for i in range(y_size)]

    def hops_y(parts):
        return ring_step(parts[1], "y") if y_size == 2 else ring_sum(parts, "y", BF16)

    def end_y(parts, arrived):
        return plus(arrived, parts[0]) if y_size == 2 else arrived

    def begin(parts, axis):
        return ring_step(parts[1], axis) if len(parts) == 2 else ring_sum(parts, axis, BF16)

    def finish(parts, arrived):
        return plus(arrived, parts[0]) if len(parts) == 2 else arrived

    sent_chunks, grad_chunks, weighted, grad_hidden, grads_gates = [], [], [], [], []
    results_c, grads_c, results_sum, grads_sum = [], [], {}, {}
    for z_step in range(z_size):
        sent_chunks += rows + others
        grad_chunks += grads_y[z_step] + grads_other[z_step]
        parts = run_experts(
            rows + others,
            grads_y[z_step] + grads_other[z_step],
            w_in_parts,
            w_back_parts,
            counts,
            group,
        )
        moved = {}
        if z_step + 1 < z_size:
            moved["rows"] = ring_gather(ahead, "y")
        if z_step + 2 < z_size:
            moved["ahead"] = ring_step(ahead, "z")
        if z_step <= 1:
            moved["grads_z"] = ring_step(grads_z[1 + z_step], "z")
        if z_step == 1:
            moved["grads"] = ring_gather(grads_z[2], "y")
        if z_step == 2:
            moved["grads"] = [ring_step(part, "z") for part in grads_y[2][1:]]
            moved["grads_other"] = [ring_step(grads_z[3], "c")]
        if z_step >= 2:
            moved["grad"] = hops_y(grads_c[z_step - 1])
        if z_step >= 1:
            moved["result"] = ring_step(last_results[1], "c")
        if z_step == 3:
            moved["step"] = ring_step(grads_sum[1], "z")
            moved["grad_zero"] = hops_y(grads_c[0])
            moved["result_one"] = hops_y(results_c[1])
        parts, moved = sync(parts, moved)
        weighted.append(parts[4])
        grad_hidden.append(parts[5])
        grads_gates.append(parts[6])
        grads_last = []
        if z_step <= 1:
            grads_z.append(moved["grads_z"])
        if z_step in (1, 2):
            grads_y.append(([grads_z[3]] if z_step == 2 else []) + moved["grads"])
            grads_other.append(moved.get("grads_other", []))
            missing = grads_y[-1][len(grads_other[-1]) :]
            grads_last = [ring_step(part, "c") for part in missing]
        arrived = ring_step(parts[3], "c")
        if z_step + 1 < z_size:
            ahead, rows = moved.get("ahead"), moved["rows"]
            others = [ring_step(part, "c") for part in rows]
        arrived, others, rows, grads_last = sync(arrived, others, rows, grads_last)
        if grads_last:
            grads_other[-1] = grads_other[-1] + grads_last
        if z_step >= 1:
            results_c.append(plus_all(moved["result"], last_results[0]))
        if z_step >= 2:
            grads_sum[z_step - 1] = end_y(grads_c[z_step - 1], moved["grad"])
        grads_c.append(plus_all(arrived, parts[2]))
        last_results = parts[:2]

    total = plus(moved["step"], grads_sum[2])
    grads_sum[0] = end_y(grads_c[0], moved["grad_zero"])
    results_sum[1] = end_y(results_c[1], moved["result_one"])
    spread = jnp.stack(grads_gates).reshape(z_size, 2, y_size, E, count)
    spread = ring_sum([spread[:, 0], spread[:, 1]], "c", F32)

    def in_grads(which):
        first, last = ranges[which]
        return expert_grads(sent_chunks, grad_hidden, first, last, 2 * width, False)

    def halves(part):
        middle = part.shape[0] // 2
        return part[:middle], part[middle:]

    grads_c, total, results_c, results_sum, last_results, spread, grad_hidden = sync(
        grads_c, total, results_c, results_sum, last_results, spread, grad_hidden
    )
    first_grads, last_grad, step, result_three, spread = sync(
        in_grads(0),
        hops_y(grads_c[3]),
        ring_step(total, "z"),
        ring_step(last_results[1], "c"),
        ring_sum([spread[:, i] for i in range(y_size)], "y", F32),
    )
    total = plus(step, end_y(grads_c[3], last_grad))
    grad_hidden, total, results_sum, results_c, first_grads, result_three = sync(
        grad_hidden, total, results_sum, results_c, first_grads, result_three
    )
    second_grads, step, result_two, result_step, grad_gates, one = sync(
        in_grads(1),
        ring_step(total, "z"),
        hops_y(results_c[2]),
        ring_step(results_sum[1], "z"),
        ring_sum([spread[i] for i in range(z_size)], "z", F32),
        ring_step(first_grads[2], "x"),
    )
    grad_gates = with_layout_constraint(grad_gates, Layout((0, 1))).T
    grad_experts = plus(step, grads_sum[0], F32)
    result_total = plus(result_step, end_y(results_c[2], result_two))
    grad_experts, first_grads, second_grads, results_c, result_total, result_three = sync(
        grad_experts, first_grads, second_grads, results_c, result_total, result_three
    )
    two = ring_step(first_grads[3], "x")
    second_one = ring_step(second_grads[2], "x")
    result_step = ring_step(result_total, "z")
    results_c.append(plus_all(result_three, last_results[0]))
    result_three = hops_y(results_c[3])

    def finish_x(parts, arrived, kind):
        rest = list(parts[2:]) + [parts[0]]
        total = plus(arrived, rest[0], kind)
        for part in rest[1:]:
            total = plus(ring_step(total, "x"), part, kind)
        return total

    def finish_in(parts, one, two):
        return jnp.concatenate([finish_x(parts[0::2], one, BF16), finish_x(parts[1::2], two, BF16)])

    grad_picked = chosen * (grad_gates - jnp.sum(grad_gates * gates, axis=-1, keepdims=True))
    grad_chance = grad_picked / picked_total
    grad_logits = (
        chance * (grad_chance - jnp.sum(chance * grad_chance, axis=-1, keepdims=True))
    ).astype(BF16)
    grad_w_router = dot(normed_two, grad_logits, ((0,), (0,)))
    grad_normed_two = grad_experts + dot(grad_logits, w_router, ((1,), (1,)))
    grad_resid, grad_gain_two = norm_back(grad_normed_two, resid, r_two, gain_second)
    grad_resid = grad_final + grad_resid

    grad_att = grad_resid.astype(BF16)
    grad_att = jnp.concatenate([grad_att, ring_step(grad_att, "c")])
    grad_w_out = dot(mixed, grad_att, ((0,), (0,))).astype(BF16)
    grad_mixed = dot(grad_att, w_out, ((1,), (1,))).astype(BF16)
    grad_mixed, grad_w_out, two, result_step, result_three, second_grads, results_c = sync(
        grad_mixed, grad_w_out, two, result_step, result_three, second_grads, results_c
    )
    first_sum = finish_in(first_grads, one, two)
    result_total = plus(result_step, end_y(results_c[3], result_three))
    out_parts = pick_weights([(grad_w_out, 0, MODEL_WIDTH)], "x", "y", False)
    first_sum, out_parts, grad_mixed, result_total, second_grads = sync(
        first_sum, out_parts, grad_mixed, result_total, second_grads
    )
    first_pieces = lax.all_to_all(first_sum, "z", 0, 0, tiled=True)
    second_two = ring_step(second_grads[3], "x")
    out_hop = begin(out_parts, "y")
    result_step = ring_step(result_total, "z")
    result_zero = hops_y(results_c[0])
    grad_qk_pre, grad_value_pre = attention_call(
        attention_back_kernel,
        [query, keys, values, grad_mixed],
        [q_width + kv_width, kv_width],
        tables,
        block,
        [pltpu.VMEM((block, q_width + kv_width), F32)],
        "attention_back",
    )
    grad_qk_pre, grad_value_pre, second_one, out_hop, out_parts = sync(
        grad_qk_pre, grad_value_pre, second_one, out_hop, out_parts
    )
    out_parts = finish(out_parts, out_hop)
    out_parts = [out_parts[i] for i in range(x_size)]
    out_hop = begin(out_parts, "x")
    grad_w_qk = dot(normalized_input, grad_qk_pre, ((0,), (0,))).astype(BF16)
    grad_w_v = dot(normalized_input, grad_value_pre, ((0,), (0,))).astype(BF16)
    grad_normed = dot(grad_qk_pre, w_qk, ((1,), (1,)))
    grad_normed = grad_normed + dot(grad_value_pre, w_v, ((1,), (1,)))
    grad_normed, other_normed, second_two, grad_w_qk, grad_w_v, result_step = sync(
        grad_normed[:count],
        ring_step(grad_normed[count:], "c"),
        second_two,
        grad_w_qk,
        grad_w_v,
        result_step,
    )
    second_sum = finish_in(second_grads, second_one, second_two)
    grad_normed = grad_normed + other_normed
    grad_rows, grad_gain_one = norm_back(grad_normed, own_act, r_one[:count], gain_first)
    grad_rows = grad_resid + grad_rows

    grad_small = jnp.concatenate(
        [grad_w_router, grad_gain_one[:, None], grad_gain_two[:, None]], axis=1
    )
    grad_small = jnp.pad(grad_small, ((0, 0), (0, LANES - grad_small.shape[1])))
    q_parts = pick_weights([(grad_w_qk, 0, q_width)], "x", "y", True)
    rest = [
        (grad_w_qk, q_width, kv_width),
        (grad_w_v, 0, kv_width),
        (grad_small.astype(BF16), 0, LANES),
    ]
    rest_parts = pick_weights(rest, "y", "x", True)
    q_parts, rest_parts, grad_rows, grad_chunks, result_zero, first_pieces, second_sum = sync(
        q_parts, rest_parts, grad_rows, grad_chunks, result_zero, first_pieces, second_sum
    )
    second_pieces = lax.all_to_all(second_sum, "z", 0, 0, tiled=True)
    grad_w_back, q_sum, rest_sum, out_hop, out_parts = sync(
        expert_grads(grad_chunks, weighted, 0, local_count, width, True),
        ring_sum(q_parts, "y", BF16),
        ring_sum(rest_parts, "x", BF16),
        out_hop,
        out_parts,
    )
    out_sum = finish(out_parts, out_hop)
    back_x = ring_step(grad_w_back[1], "x")
    q_sum, rest_sum, out_sum, first_pieces, second_pieces, result_step = sync(
        sum_along(q_sum, "x"),
        sum_along(rest_sum, "y"),
        out_sum,
        first_pieces,
        second_pieces,
        result_step,
    )
    grad_gate_up = unpack_experts(first_pieces, *ranges[0], local_count, [])
    outputs = resid + plus(result_step, end_y(results_c[0], result_zero), F32)
    grad_first, grad_second, grad_w_out, grad_gate_up, outputs = sync(
        *[sum_along(part, "z", F32) for part in (q_sum, rest_sum, out_sum)],
        grad_gate_up,
        outputs,
    )
    grad_w_gate, grad_w_up = unpack_experts(
        second_pieces, *ranges[1], local_count, list(grad_gate_up)
    )
    grad_w_down = finish_x(grad_w_back, back_x, F32)
    grad_both = jnp.concatenate([grad_first, grad_second], axis=-1)
    mine = lax.dynamic_index_in_dim(grad_both, core, 0, keepdims=False)
    theirs = lax.dynamic_index_in_dim(grad_both, 1 - core, 0, keepdims=False)
    got = ring_step(theirs, "c")

    def whole_columns(start, columns):
        parts = [part[:, start : start + columns].reshape(own_rows, y_size, -1) for part in (mine, got)]
        ordered = jnp.where(core == 0, jnp.stack(parts, 2), jnp.stack(parts[::-1], 2))
        return ordered.reshape(own_rows, 2 * columns)

    grad_small = (mine + got)[:, q_width + 2 * kv_width :]
    return (
        outputs.astype(BF16).reshape(inputs.shape),
        grad_rows.reshape(inputs.shape),
        grad_small[:, E],
        whole_columns(0, q_width),
        whole_columns(q_width, kv_width),
        whole_columns(q_width + kv_width, kv_width),
        grad_w_out,
        grad_small[:, E + 1],
        grad_small[:, :E],
        grad_w_gate,
        grad_w_up,
        grad_w_down,
    )


def solution(mesh):
    experts, shards = mesh.shape["expert"], mesh.shape["shard"]
    split = Mesh(
        mesh.devices.reshape(experts // 2, 2, SLICES, shards // SLICES), ("y", "c", "z", "x")
    )
    groups, within = ("y", "c"), ("z", "x")
    tokens = P(None, ALL, None)
    rows = P(ALL, None)
    expert = P(groups, within, None)
    return jax.shard_map(
        body,
        mesh=split,
        in_specs=(tokens,) * 4
        + (P(ALL), rows, rows, rows, rows, P(ALL), rows, expert, expert, expert),
        out_specs=(tokens, tokens, P(ALL), rows, rows, rows, rows, P(ALL), rows)
        + (expert, expert, expert),
        check_vma=False,
    )
```

```python
import functools
import itertools
import math

import jax
import jax.numpy as jnp
from jax import lax
from jax.experimental import pallas as pl
from jax.experimental.pallas import tpu as pltpu
from jax.experimental.layout import Layout, with_layout_constraint
from jax.sharding import Mesh, PartitionSpec as P

MODEL_WIDTH = 1536
QUERY_HEADS = 24
KEY_VALUE_HEADS = 8
HEAD_SIZE = 64
QUERY_PER_GROUP = QUERY_HEADS // KEY_VALUE_HEADS
E = 40
TOPK = 8
SLICES = 4
LANES = 128
VMEM_BYTES = 60 * 1024 * 1024

ALL = ("y", "c", "z", "x")
epsilon = 1e-05
F32 = jnp.float32
BF16 = jnp.bfloat16


def dot(left, right, dims=((1,), (0,))):
    return lax.dot_general(left, right, (dims, ((), ())), preferred_element_type=F32)


def sync(*values):
    return lax.optimization_barrier(values)


def ring_step(array, axis):
    size = lax.axis_size(axis)
    return lax.ppermute(array, axis, [(i, (i + 1) % size) for i in range(size)])


def ring_gather(block, axis):
    blocks = [block]
    for _ in range(lax.axis_size(axis) - 1):
        blocks.append(ring_step(blocks[-1], axis))
    return blocks


def ring_sum(parts, axis, kind):
    total = parts[1]
    for part in list(parts[2:]) + [parts[0]]:
        total = ring_step(total, axis).astype(F32) + part.astype(F32)
        total = total.astype(kind if part is parts[0] else part.dtype)
    return total


def direct_sum(parts, axis, kind):
    size = lax.axis_size(axis)
    total = parts[0].astype(F32)
    for step in range(1, size):
        to = [(i, (i - step) % size) for i in range(size)]
        total = total + lax.ppermute(parts[step], axis, to).astype(F32)
    return total.astype(kind)


def index_at(axis, step):
    return (lax.axis_index(axis) - step) % lax.axis_size(axis)


def move_kernel(moves, count_in, count_out, place_ref, *refs):
    sources, targets = refs[:count_in], refs[count_in : count_in + count_out]
    held, sems = refs[count_in + count_out : -1], refs[-1]
    copies = [[] for _ in targets]
    for number, (source, from_index, target, to_index) in enumerate(moves):
        picked = [
            tuple(place_ref[i[0]] if isinstance(i, tuple) else i for i in index)
            for index in (from_index, to_index)
        ]
        copy = pltpu.make_async_copy(
            sources[source].at[picked[0]], held[target].at[picked[1]], sems.at[number]
        )
        copy.start()
        copies[target].append(copy)
    out = []
    for target, arriving in enumerate(copies):
        for copy in arriving:
            copy.wait()
        out.append(
            pltpu.make_async_copy(held[target], targets[target], sems.at[len(moves) + target])
        )
        out[-1].start()
    for copy in out:
        copy.wait()


def move(moves, places, sources, shapes, name):
    anywhere = pl.BlockSpec(memory_space=pl.ANY)
    total = sum(math.prod(s.shape) * s.dtype.itemsize for s in shapes)
    return pl.pallas_call(
        functools.partial(move_kernel, moves, len(sources), len(shapes)),
        in_specs=[pl.BlockSpec(memory_space=pltpu.SMEM)] + [anywhere] * len(sources),
        out_specs=[anywhere] * len(shapes),
        out_shape=shapes,
        scratch_shapes=[pltpu.VMEM(s.shape, s.dtype) for s in shapes]
        + [pltpu.SemaphoreType.DMA((len(moves) + len(shapes),))],
        compiler_params=pltpu.CompilerParams(vmem_limit_bytes=VMEM_BYTES),
        cost_estimate=pl.CostEstimate(flops=0, bytes_accessed=2 * total, transcendentals=0),
        name=name,
    )(jnp.stack(places).astype(jnp.int32), *sources)


def places_of(axes):
    places, where = [], {}
    for axis in axes:
        for step in range(lax.axis_size(axis)):
            where[axis, step] = (len(places),)
            places.append(index_at(axis, step))
    return places, where


def place_weights(gathers):
    places, where = places_of(("y", "z", "x"))
    sizes = [lax.axis_size(axis) for axis in ("y", "z", "x")]
    moves, sources, shapes = [], [], []
    for number, blocks in enumerate(gathers):
        for (y_step, z_first, x_step), part in blocks.items():
            for i in range(part.shape[0]):
                spot = (where["y", y_step], slice(None), where["z", z_first + i], where["x", x_step])
                moves.append((len(sources), (i,), number, spot))
            sources.append(part)
        shape = (sizes[0], 2) + tuple(sizes[1:]) + sources[-1].shape[2:]
        shapes.append(jax.ShapeDtypeStruct(shape, sources[-1].dtype))
    whole = move(moves, places, sources, shapes, "place_weights")
    return [part.reshape(-1, part.shape[-1]) for part in whole]


def pick_weights(grads, first, second, with_core):
    sizes = {axis: lax.axis_size(axis) for axis in ("y", "z", "x")}
    core = (2,) if with_core else ()
    places, where = places_of(("y", "z", "x"))
    moves, sources, start = [], [], 0
    for number, (grad, column, columns) in enumerate(grads):
        shape = (sizes["y"],) + core + (sizes["z"], sizes["x"], -1, grad.shape[-1])
        sources.append(grad.reshape(shape))
        rows = slice(None)
        for y_step, z_step, x_step in itertools.product(
            range(sizes["y"]), range(sizes["z"]), range(sizes["x"])
        ):
            spot = [where["y", y_step], where["z", z_step], where["x", x_step]]
            if with_core:
                spot.insert(1, rows)
            spot += [rows, pl.ds(column, columns)]
            steps = {"y": y_step, "x": x_step}
            to = (steps[first], z_step) + (rows,) * (1 + len(core)) + (pl.ds(start, columns),)
            moves.append((number, tuple(spot), steps[second], to))
        start = start + columns
    tail = core + (sources[0].shape[-2], start)
    shape = jax.ShapeDtypeStruct((sizes[first], sizes["z"]) + tail, sources[0].dtype)
    return move(moves, places, sources, [shape] * sizes[second], "pick_weights")


def sum_along(parts, axis, kind=BF16):
    return ring_sum([parts[i] for i in range(parts.shape[0])], axis, kind)


def pack_kernel(gate_ref, up_ref, out_ref):
    width = out_ref.shape[-1] // 2
    for z in range(out_ref.shape[0]):
        out_ref[z, :, :width] = gate_ref[0, :, z * width : (z + 1) * width]
        out_ref[z, :, width:] = up_ref[0, :, z * width : (z + 1) * width]


def pack_experts(w_gate, w_up, first, last, slices):
    rows, hidden = w_gate.shape[1:]
    spec = pl.BlockSpec((1, rows, hidden), lambda e: (first + e, 0, 0))
    width = 2 * hidden // slices
    return pl.pallas_call(
        pack_kernel,
        grid=(last - first,),
        in_specs=[spec, spec],
        out_specs=pl.BlockSpec((slices, rows, width), lambda e: (0, 0, e)),
        out_shape=jax.ShapeDtypeStruct((slices, rows, (last - first) * width), w_gate.dtype),
        name="pack_experts",
    )(w_gate, w_up)


def unpack_kernel(part_ref, *refs):
    gate_ref, up_ref = refs[-2:]
    slices = part_ref.shape[0]
    width = gate_ref.shape[-1] // slices
    for z in range(slices):
        both = part_ref[z].astype(F32)
        gate_ref[0, :, z * width : (z + 1) * width] = both[:, :width]
        up_ref[0, :, z * width : (z + 1) * width] = both[:, width:]


def unpack_experts(part, first, last, local_count, earlier):
    slices, rows, columns = part.shape
    width = columns // (last - first)
    spec = pl.BlockSpec((1, rows, width // 2 * slices), lambda e: (first + e, 0, 0))
    shape = jax.ShapeDtypeStruct((local_count, rows, width // 2 * slices), F32)
    anywhere = pl.BlockSpec(memory_space=pl.ANY)
    return pl.pallas_call(
        unpack_kernel,
        grid=(last - first,),
        in_specs=[pl.BlockSpec((slices, rows, width), lambda e: (0, 0, e))]
        + [anywhere] * len(earlier),
        out_specs=[spec, spec],
        out_shape=[shape, shape],
        input_output_aliases={1 + i: i for i in range(len(earlier))},
        name="unpack_experts",
    )(part, *earlier)


def experts_kernel(counts, steps, x_size, place_ref, *refs):
    parts = len(counts)
    rows_in, grads_in, refs = refs[:steps], refs[steps : 2 * steps], refs[2 * steps :]
    w_in_parts, refs = [refs[i * x_size : (i + 1) * x_size] for i in range(parts)], refs[parts * x_size :]
    w_back_parts, refs = refs[:x_size], refs[x_size:]
    results, grads, (active_ref, hidden_ref, gates_ref) = refs[:2], refs[2:4], refs[4:7]
    rows_buf, grads_buf = refs[7:9]
    w_in, w_back, sems = refs[9 : 9 + parts], refs[9 + parts], refs[10 + parts]
    step = pl.program_id(0)
    half = steps // 2
    weights, late = [[] for _ in counts], [[] for _ in range(steps)]
    number = 0

    def copy_of(source, target):
        nonlocal number
        number = number + 1
        return pltpu.make_async_copy(source, target, sems.at[number - 1])

    first = 0
    for part, count in enumerate(counts):
        for x_step in range(x_size):
            place = place_ref[1 + x_step]
            source = w_in_parts[part][x_step]
            size = source.shape[1]
            for z in range(source.shape[0]):
                start = pl.multiple_of((z * x_size + place) * size, size)
                weights[part].append(copy_of(source.at[z], w_in[part].at[pl.ds(start, size)]))
            source = w_back_parts[x_step]
            size = source.shape[1]
            for e in range(first, first + count):
                start = pl.multiple_of((e * x_size + place) * size, size)
                weights[part].append(copy_of(source.at[e], w_back.at[pl.ds(start, size)]))
        first = first + count
    for i in range(steps):
        late[i] = [copy_of(rows_in[i], rows_buf.at[i]), copy_of(grads_in[i], grads_buf.at[i])]

    @pl.when(step == 0)
    def _():
        for some in late[:1] + weights + late[1:]:
            for copy in some:
                copy.start()

    for i in range(steps):

        @pl.when(step == i)
        def _(i=i):
            for copy in late[i]:
                copy.wait()

    local_count = sum(counts)
    width = w_back.shape[0] // local_count
    rows = rows_buf[step, :, :MODEL_WIDTH]
    grad_rows = grads_buf[step]
    first = place_ref[0] * local_count
    source = lax.broadcasted_iota(jnp.int32, (LANES, LANES), 0)
    wanted = lax.broadcasted_iota(jnp.int32, (LANES, LANES), 1) + first
    choose = ((source == wanted) | (source == wanted + E)).astype(F32).astype(BF16)
    gates = dot(rows_buf[step, :, MODEL_WIDTH:], choose)
    lane = lax.broadcasted_iota(jnp.int32, gates.shape, 1)
    grad_gates = jnp.zeros(gates.shape, F32)
    expert = 0
    for part, count in enumerate(counts):

        @pl.when(step == 0)
        def _(part=part):
            for copy in weights[part]:
                copy.wait()

        all_hidden = dot(rows, w_in[part][...])
        all_plain = dot(
            grad_rows, w_back[expert * width : (expert + count) * width, :], ((1,), (1,))
        )
        for i in range(count):
            here = slice(expert * width, (expert + 1) * width)
            hidden = all_hidden[:, 2 * width * i : 2 * width * (i + 1)]
            grad_plain = all_plain[:, width * i : width * (i + 1)]
            gate_part, up_part = hidden[:, :width], hidden[:, width:]
            sigmoid_gate = 1.0 / (1.0 + jnp.exp(-gate_part))
            silu = gate_part * sigmoid_gate
            active = silu * up_part
            weight = gates[:, expert : expert + 1]
            total = jnp.sum(active * grad_plain, axis=1, keepdims=True)
            grad_gates = jnp.where(lane == first + expert, total, grad_gates)
            active_ref[:, here] = (weight * active).astype(BF16)
            grad_active = weight * grad_plain
            start = 2 * width * expert
            hidden_ref[:, start : start + width] = (
                grad_active * up_part * (sigmoid_gate + silu * (1.0 - sigmoid_gate))
            ).astype(BF16)
            hidden_ref[:, start + width : start + 2 * width] = (grad_active * silu).astype(BF16)
            expert = expert + 1
    gates_ref[0] = grad_gates.T[:E]
    result = dot(active_ref[...], w_back[...]).astype(BF16)
    grad_in = jnp.zeros(rows.shape, F32)
    start = 0
    for part, count in enumerate(counts):
        size = 2 * width * count
        grad_in += dot(hidden_ref[:, start : start + size], w_in[part][...], ((1,), (1,)))
        start = start + size
    grad_in = grad_in.astype(BF16)

    for side, now in enumerate((step < half, step >= half)):

        @pl.when(now)
        def _(side=side):
            results[side][0] = result
            grads[side][0] = grad_in


def run_experts(rows, grads, w_in_parts, w_back_parts, counts, group):
    count, wide = rows[0].shape
    steps = len(rows)
    half = steps // 2
    local_count = sum(counts)
    x_size = len(w_in_parts[0])
    z_size, own_rows, columns = w_in_parts[0][0].shape
    width = columns // (2 * counts[0])
    copies = 2 * steps + x_size * (len(counts) * z_size + local_count)
    places, _ = places_of(("x",))
    anywhere = pl.BlockSpec(memory_space=pl.ANY)
    own = pl.BlockSpec((1, count, MODEL_WIDTH), lambda i: (jnp.minimum(i, half - 1), 0, 0))
    other = pl.BlockSpec((1, count, MODEL_WIDTH), lambda i: (jnp.maximum(i - half, 0), 0, 0))

    def by_row(columns):
        return pl.BlockSpec((count, columns), lambda i: (i, 0))

    side = jax.ShapeDtypeStruct((half, count, MODEL_WIDTH), BF16)
    flops = 2 * steps * count * MODEL_WIDTH * 6 * local_count * width
    return pl.pallas_call(
        functools.partial(experts_kernel, counts, steps, x_size),
        grid=(steps,),
        in_specs=[pl.BlockSpec(memory_space=pltpu.SMEM)]
        + [anywhere] * (2 * steps + (len(counts) + 1) * x_size),
        out_specs=[own, other, own, other]
        + [by_row(local_count * width), by_row(2 * local_count * width)]
        + [pl.BlockSpec((1, E, count), lambda i: (i, 0, 0))],
        out_shape=[side] * 4
        + [
            jax.ShapeDtypeStruct((steps * count, local_count * width), BF16),
            jax.ShapeDtypeStruct((steps * count, 2 * local_count * width), BF16),
            jax.ShapeDtypeStruct((steps, E, count), F32),
        ],
        scratch_shapes=[
            pltpu.VMEM((steps, count, wide), BF16),
            pltpu.VMEM((steps, count, MODEL_WIDTH), BF16),
        ]
        + [pltpu.VMEM((MODEL_WIDTH, part[0].shape[-1]), BF16) for part in w_in_parts]
        + [
            pltpu.VMEM((local_count * width, MODEL_WIDTH), BF16),
            pltpu.SemaphoreType.DMA((copies,)),
        ],
        compiler_params=pltpu.CompilerParams(vmem_limit_bytes=VMEM_BYTES),
        cost_estimate=pl.CostEstimate(
            flops=flops, bytes_accessed=30 * 1024 * 1024, transcendentals=0
        ),
        name="experts",
    )(
        jnp.stack([group] + places).astype(jnp.int32),
        *rows,
        *grads,
        *[part for parts in w_in_parts for part in parts],
        *w_back_parts,
    )


def expert_grads_kernel(count_left, count_right, back, place_ref, *refs):
    whole = refs[:count_left]
    columns = refs[count_left : count_left + count_right]
    outs, (buf, total, sems) = refs[count_left + count_right : -3], refs[-3:]
    rows_each = whole[0].shape[0]

    @pl.when(pl.program_id(0) == 0)
    def _():
        copies = [
            pltpu.make_async_copy(
                part.at[:, pl.ds(0, MODEL_WIDTH)],
                buf.at[pl.ds(number * rows_each, rows_each)],
                sems.at[number],
            )
            for number, part in enumerate(whole)
        ]
        for copy in copies:
            copy.start()
        for copy in copies:
            copy.wait()

    size = columns[0].shape[0]
    for i, part in enumerate(columns):
        rows = buf[i * size : (i + 1) * size, :]
        if back:
            term = dot(part[...], rows, ((0,), (0,)))
        else:
            term = dot(rows, part[...], ((0,), (0,)))
        if i == 0:
            total[...] = term
        else:
            total[...] += term
    blocks, own = outs[0].shape[0], outs[0].shape[1]
    devices = len(outs) if back else len(outs) // 2
    for number, out in enumerate(outs):
        step, half = (number, 0) if back else (number // 2, number % 2)
        for i in range(blocks):
            block = half * blocks + i
            start = pl.multiple_of((block * devices + place_ref[step]) * own, own)
            out[i] = total[pl.ds(start, own), :].astype(BF16)


def expert_grads(whole, columns, first, last, width, back):
    x_size = lax.axis_size("x")
    places, _ = places_of(("x",))
    tokens = len(whole) * whole[0].shape[0]
    experts = last - first
    anywhere = pl.BlockSpec(memory_space=pl.ANY)
    column = pl.BlockSpec((columns[0].shape[0], width), lambda e: (0, first + e))
    outs = x_size if back else 2 * x_size
    if back:
        own = width // x_size
        block = (1, own, MODEL_WIDTH)
        shape = (experts, own, MODEL_WIDTH)
        out = pl.BlockSpec(block, lambda e: (e, 0, 0))
        total = (width, MODEL_WIDTH)
    else:
        z_size = lax.axis_size("z")
        own = MODEL_WIDTH // (z_size * x_size)
        shape = (z_size // 2, own, experts * width)
        out = pl.BlockSpec((z_size // 2, own, width), lambda e: (0, 0, e))
        total = (MODEL_WIDTH, width)
    return pl.pallas_call(
        functools.partial(expert_grads_kernel, len(whole), len(columns), back),
        grid=(experts,),
        in_specs=[pl.BlockSpec(memory_space=pltpu.SMEM)]
        + [anywhere] * len(whole)
        + [column] * len(columns),
        out_specs=[out] * outs,
        out_shape=[jax.ShapeDtypeStruct(shape, BF16)] * outs,
        scratch_shapes=[
            pltpu.VMEM((tokens, MODEL_WIDTH), BF16),
            pltpu.VMEM(total, F32),
            pltpu.SemaphoreType.DMA((len(whole),)),
        ],
        compiler_params=pltpu.CompilerParams(vmem_limit_bytes=VMEM_BYTES),
        cost_estimate=pl.CostEstimate(
            flops=2 * tokens * MODEL_WIDTH * width * experts,
            bytes_accessed=2 * tokens * (MODEL_WIDTH + width * experts),
            transcendentals=0,
        ),
        name="expert_grads",
    )(jnp.stack(places).astype(jnp.int32), *whole, *columns)


def positions(lengths, count_of_tokens):
    seq_ends = jnp.cumsum(lengths, axis=-1)
    starts = seq_ends - lengths
    token_index = jnp.arange(count_of_tokens, dtype=jnp.int32)
    segment = jnp.sum((token_index[:, None] >= seq_ends[..., None, :]).astype(jnp.int32), axis=-1)
    choose = segment[..., None] == jnp.arange(lengths.shape[-1], dtype=jnp.int32)
    offset = jnp.sum(jnp.where(choose, starts[..., None, :], 0), axis=-1)
    return (segment, token_index - offset)


def rotary_tables(token_position):
    half_size = HEAD_SIZE // 2
    frequency = jnp.exp(jnp.arange(half_size, dtype=F32) * (-math.log(10000.0) / half_size))
    angles = token_position.astype(F32)[:, None] * frequency
    cosine, sine_part = jnp.cos(angles), jnp.sin(angles)
    repeat = LANES // HEAD_SIZE
    return (
        jnp.concatenate([cosine, cosine] * repeat, axis=1),
        jnp.concatenate([-sine_part, sine_part] * repeat, axis=1),
    )


def rotate(values, cosine, sine_part, direction):
    lane = lax.broadcasted_iota(jnp.int32, (values.shape[0], LANES), 1)
    first = lane % HEAD_SIZE < HEAD_SIZE // 2
    tiles = []
    for start in range(0, values.shape[1], LANES):
        tile = values[:, start : start + LANES]
        after = pltpu.roll(tile, LANES - HEAD_SIZE // 2, 1)
        before = pltpu.roll(tile, HEAD_SIZE // 2, 1)
        swapped = jnp.where(first, after, before)
        tiles.append(tile * cosine + direction * swapped * sine_part)
    return jnp.concatenate(tiles, axis=1)


def allowed_pairs(column_ref, row_ref):
    shape = column_ref.shape
    same = column_ref[...] == row_ref[0, :1, :]
    earlier = lax.broadcasted_iota(jnp.int32, shape, 0) >= lax.broadcasted_iota(jnp.int32, shape, 1)
    return jnp.concatenate([same & earlier] * QUERY_PER_GROUP, axis=0)


def group_rows(rows, group):
    heads = [group * QUERY_PER_GROUP + i for i in range(QUERY_PER_GROUP)]
    return jnp.concatenate([rows[:, HEAD_SIZE * h : HEAD_SIZE * (h + 1)] for h in heads], axis=0)


def masked_scores(query, keys, allowed):
    scores = dot(query, keys, ((1,), (1,))) * (1.0 / math.sqrt(HEAD_SIZE))
    return jnp.where(allowed, scores, -1000000000.0)


def attention_kernel(
    qk_ref, value_ref, cos_ref, sin_ref, column_ref, row_ref, query_ref, key_ref, mixed_ref, log_ref
):
    width = query_ref.shape[1]
    block = query_ref.shape[0]
    rotated = rotate(qk_ref[...], cos_ref[...], sin_ref[...], 1.0).astype(BF16)
    query_ref[...] = rotated[:, :width]
    key_ref[...] = rotated[:, width:]
    allowed = allowed_pairs(column_ref, row_ref)
    lane = lax.broadcasted_iota(jnp.int32, (block, LANES), 1)
    logs = jnp.zeros((block, LANES), F32)
    for group in range(key_ref.shape[1] // HEAD_SIZE):
        here = slice(HEAD_SIZE * group, HEAD_SIZE * (group + 1))
        query = group_rows(query_ref[...], group)
        scores = masked_scores(query, key_ref[:, here], allowed)
        row_max = jnp.max(scores, axis=-1, keepdims=True)
        shifted = jnp.exp(scores - row_max)
        row_total = jnp.sum(shifted, axis=-1, keepdims=True)
        log_total = row_max + jnp.log(row_total)
        mixed = dot((shifted / row_total).astype(BF16), value_ref[:, here]).astype(BF16)
        for i in range(QUERY_PER_GROUP):
            head = group * QUERY_PER_GROUP + i
            rows = slice(block * i, block * (i + 1))
            mixed_ref[:, HEAD_SIZE * head : HEAD_SIZE * (head + 1)] = mixed[rows]
            logs = jnp.where(lane == head, log_total[rows], logs)
    log_ref[...] = logs


def attention_back_kernel(
    query_ref,
    key_ref,
    value_ref,
    grad_ref,
    log_ref,
    cos_ref,
    sin_ref,
    column_ref,
    row_ref,
    grad_qk_ref,
    grad_value_ref,
    total,
):
    width = query_ref.shape[1]
    block = query_ref.shape[0]
    scale = 1.0 / math.sqrt(HEAD_SIZE)
    allowed = allowed_pairs(column_ref, row_ref)
    for group in range(key_ref.shape[1] // HEAD_SIZE):
        here = slice(HEAD_SIZE * group, HEAD_SIZE * (group + 1))
        query = group_rows(query_ref[...], group)
        grad_mixed = group_rows(grad_ref[...], group)
        heads = [group * QUERY_PER_GROUP + i for i in range(QUERY_PER_GROUP)]
        log_total = jnp.concatenate([log_ref[:, head : head + 1] for head in heads], axis=0)
        probs = jnp.exp(masked_scores(query, key_ref[:, here], allowed) - log_total)
        grad_probs = dot(grad_mixed, value_ref[:, here], ((1,), (1,)))
        grad_value_ref[:, here] = dot(probs.astype(BF16), grad_mixed, ((0,), (0,))).astype(BF16)
        spread = jnp.sum(probs * grad_probs, axis=-1, keepdims=True)
        grad_scores = (probs * (grad_probs - spread)).astype(BF16)
        grad_query = dot(grad_scores, key_ref[:, here]) * scale
        for i in range(QUERY_PER_GROUP):
            start = HEAD_SIZE * (group * QUERY_PER_GROUP + i)
            total[:, start : start + HEAD_SIZE] = grad_query[block * i : block * (i + 1)]
        start = width + HEAD_SIZE * group
        total[:, start : start + HEAD_SIZE] = dot(grad_scores, query, ((0,), (0,))) * scale
    grad_qk_ref[...] = rotate(total[...], cos_ref[...], sin_ref[...], -1.0).astype(BF16)


def attention_call(kernel, arrays, widths, tables, block, scratch, name):
    rows = arrays[0].shape[0]

    def by_row(columns):
        return pl.BlockSpec((block, columns), lambda i: (i, 0))

    return pl.pallas_call(
        kernel,
        grid=(rows // block,),
        in_specs=[by_row(a.shape[1]) for a in list(arrays) + list(tables[:3])]
        + [pl.BlockSpec((1,) + tables[3].shape[1:], lambda i: (i, 0, 0))],
        out_specs=[by_row(width) for width, _ in widths],
        out_shape=[jax.ShapeDtypeStruct((rows, width), kind) for width, kind in widths],
        scratch_shapes=scratch,
        compiler_params=pltpu.CompilerParams(vmem_limit_bytes=VMEM_BYTES // 2),
        cost_estimate=pl.CostEstimate(
            flops=2 * rows * block * 4 * MODEL_WIDTH, bytes_accessed=8 << 20, transcendentals=0
        ),
        name=name,
    )(*arrays, *tables)


def norm_back(grad_normed, values_in, inverse_root, gain):
    scaled = grad_normed * gain
    grad_gain = jnp.sum(grad_normed * values_in * inverse_root, axis=0)
    cubed = inverse_root * inverse_root * inverse_root
    grad_values = inverse_root * scaled - values_in * cubed * jnp.mean(
        scaled * values_in, axis=-1, keepdims=True
    )
    return (grad_values, grad_gain)


def body(
    inputs,
    cotangent,
    lengths,
    routes,
    norm_gain_one,
    w_query,
    key_projection_weight,
    value_projection_weight,
    w_out,
    norm_gain_two,
    w_router,
    w_gate,
    w_up,
    w_down,
):
    micro, block, _ = inputs.shape
    count = micro * block
    local_count = w_gate.shape[0]
    y_size, z_size, x_size = lax.axis_size("y"), lax.axis_size("z"), lax.axis_size("x")
    core = lax.axis_index("c")
    group = lax.axis_index("y") * 2 + core
    own_rows = w_query.shape[0]
    q_width, kv_width = MODEL_WIDTH // 2, KEY_VALUE_HEADS * HEAD_SIZE // 2
    kv_heads = KEY_VALUE_HEADS // 2

    def columns_of(weight, which):
        split = weight.reshape(own_rows, y_size, 2, -1)
        return lax.dynamic_index_in_dim(split, which, 2, keepdims=False).reshape(own_rows, -1)

    small = jnp.concatenate([w_router, norm_gain_one[:, None], norm_gain_two[:, None]], axis=1)
    small = jnp.pad(small, ((0, 0), (0, LANES - small.shape[1])))

    def both_cores(arrays):
        mine = jnp.concatenate([columns_of(a, core) for a in arrays], axis=1)
        theirs = jnp.concatenate([columns_of(a, 1 - core) for a in arrays], axis=1)
        return mine, theirs

    mine, theirs = both_cores([w_query, key_projection_weight, value_projection_weight])
    got, other_lengths = sync(
        ring_step(jnp.concatenate([theirs, small], axis=1), "c"), ring_step(lengths, "c")
    )
    mine = jnp.concatenate([mine, small], axis=1)
    both = jnp.where(core == 0, jnp.stack([mine, got]), jnp.stack([got, mine]))
    both = jnp.concatenate(
        [
            both[..., : q_width + kv_width],
            both[..., q_width + 2 * kv_width :],
            both[..., q_width + kv_width : q_width + 2 * kv_width],
            jnp.stack([w_out[:, :q_width], w_out[:, q_width:]]),
        ],
        axis=-1,
    )
    counts = [local_count // 2, local_count - local_count // 2]
    ranges = [(0, counts[0]), (counts[0], local_count)]
    grad_final_low = cotangent.reshape(count, MODEL_WIDTH)
    grads_z = [grad_final_low]
    grads_ahead = ring_step(grad_final_low, "z")
    grads_y = [ring_gather(grad_final_low, "y")]
    down_parts = ring_gather(w_down, "x")
    pair = z_size // 2
    first_width = q_width + kv_width + LANES
    first_blocks, second_blocks = {}, {}

    def first_hops(blocks):
        rows = jnp.stack(blocks)
        return ring_gather(rows[..., :first_width], "x"), ring_gather(rows[..., first_width:], "y")

    def second_hops(by_x, by_y, z_first):
        for x_step, one in enumerate(by_x):
            for y_step, two in enumerate(ring_gather(one, "y")):
                first_blocks[y_step, z_first, x_step] = two
        for y_step, one in enumerate(by_y):
            for x_step, two in enumerate(ring_gather(one, "x")):
                second_blocks[y_step, z_first, x_step] = two

    z_blocks = [both]
    for _ in range(pair - 1):
        z_blocks.append(ring_step(z_blocks[-1], "z"))
    others = ring_step(inputs, "c")
    packed = [pack_experts(w_gate, w_up, first, last, z_size) for first, last in ranges]
    z_blocks, others, grads_ahead, grads_y, packed = sync(
        z_blocks, others, grads_ahead, grads_y, packed
    )
    other_inputs = others
    grads_z.append(grads_ahead)
    ahead = []
    for _ in range(pair):
        ahead.append(ring_step((z_blocks + ahead)[-1], "z"))
    hops, ahead, down_parts, packed = sync(first_hops(z_blocks), ahead, down_parts, packed)
    swapped = lax.all_to_all(packed[0], "z", 0, 0, tiled=True)
    second_hops(*hops, 0)
    first_blocks, second_blocks, ahead = sync(first_blocks, second_blocks, ahead)
    hops, grads_z = sync(first_hops(ahead), grads_z)
    second_hops(*hops, pair)
    first_blocks, second_blocks, swapped, packed, grads_z = sync(
        first_blocks, second_blocks, swapped, packed, grads_z
    )
    grads_y.append(ring_gather(grads_z[1], "y"))
    first_parts = ring_gather(swapped, "x")
    swapped = lax.all_to_all(packed[1], "z", 0, 0, tiled=True)
    w_first, w_second = place_weights([first_blocks, second_blocks])
    w_qk = w_first[:, : q_width + kv_width]
    small = w_first[:, q_width + kv_width :]
    w_v = w_second[:, :kv_width]
    w_out = w_second[:, kv_width:].reshape(y_size, 2, -1, q_width).transpose(0, 2, 1, 3)
    w_out = w_out.reshape(q_width, MODEL_WIDTH)
    w_router = small[:, :E]
    gain_first = small[:, E].astype(F32)
    gain_second = small[:, E + 1].astype(F32)

    all_inputs = jnp.stack([inputs, other_inputs])
    all_lengths = jnp.concatenate([lengths[:, 0], other_lengths[:, 0]])
    act_rows = all_inputs.reshape(2 * count, MODEL_WIDTH).astype(F32)
    grad_final = grad_final_low.astype(F32)
    r_one = lax.rsqrt(jnp.mean(act_rows * act_rows, axis=-1) + epsilon)[:, None]
    normalized_input = (act_rows * r_one * gain_first).astype(BF16)
    segment, token_position = positions(all_lengths, block)
    blocks = 2 * micro
    qk_pre = dot(normalized_input, w_qk)
    values = dot(normalized_input, w_v).astype(BF16)
    qk_pre, values, grads_y[0] = sync(qk_pre, values, grads_y[0])
    grads_other = [[ring_step(part, "c") for part in grads_y[0]]]
    tables = rotary_tables(token_position.reshape(-1)) + (
        jnp.broadcast_to(segment.reshape(-1, 1), (blocks * block, block)),
        jnp.broadcast_to(segment[:, None, :], (blocks, 8, block)),
    )
    query, keys, mixed, logs = attention_call(
        attention_kernel,
        [qk_pre, values],
        [(q_width, BF16), (kv_width, BF16), (q_width, BF16), (LANES, F32)],
        tables,
        block,
        [],
        "attention",
    )
    projected = dot(mixed, w_out)
    projected, first_parts, swapped, grads_other, grads_y = sync(
        projected, first_parts, swapped, grads_other, grads_y
    )
    second_parts = ring_gather(swapped, "x")
    grads_other.append([ring_step(part, "c") for part in grads_y[1]])
    own_act = act_rows[:count]
    resid = own_act + ring_sum([projected[:count], projected[count:]], "c", F32)

    r_two = lax.rsqrt(jnp.mean(resid * resid, axis=-1) + epsilon)[:, None]
    normed_two = (resid * r_two * gain_second).astype(BF16)
    chance = jax.nn.softmax(dot(normed_two, w_router), axis=-1)
    choice = routes.reshape(count, TOPK)
    chosen = jnp.any(choice[..., None] == jnp.arange(E, dtype=jnp.int32), axis=1).astype(F32)
    picked = chance * chosen
    picked_total = jnp.sum(picked, axis=-1, keepdims=True)
    gates = picked / picked_total

    high = lax.reduce_precision(gates, 8, 7)
    low = gates - high
    spare = jnp.zeros((count, LANES - 2 * E), BF16)
    sent = jnp.concatenate([normed_two, high.astype(BF16), low.astype(BF16), spare], axis=1)
    sent, grads_other = sync(sent, grads_other)
    rows, ahead, second_parts, others = sync(
        ring_gather(sent, "y"), ring_step(sent, "z"), second_parts, ring_step(sent, "c")
    )
    w_in_parts, w_back_parts = [first_parts, second_parts], down_parts
    rows, others = sync(rows, [others] + [ring_step(part, "c") for part in rows[1:]])
    width = w_in_parts[0][0].shape[-1] // (2 * counts[0])

    def plus(first, second, kind=BF16):
        return (first.astype(F32) + second.astype(F32)).astype(kind)

    def plus_all(first, second):
        return [plus(first[i], second[i]) for i in range(y_size)]

    def hops_y(parts):
        return ring_step(parts[1], "y") if y_size == 2 else ring_sum(parts, "y", BF16)

    def end_y(parts, arrived):
        return plus(arrived, parts[0]) if y_size == 2 else arrived

    def begin(parts, axis):
        return ring_step(parts[1], axis) if len(parts) == 2 else ring_sum(parts, axis, BF16)

    def finish(parts, arrived):
        return plus(arrived, parts[0]) if len(parts) == 2 else arrived

    sent_chunks, grad_chunks, weighted, grad_hidden, grads_gates = [], [], [], [], []
    results_c, grads_c, results_sum, grads_sum = [], [], {}, {}
    for z_step in range(z_size):
        sent_chunks += rows + others
        grad_chunks += grads_y[z_step] + grads_other[z_step]
        parts = run_experts(
            rows + others,
            grads_y[z_step] + grads_other[z_step],
            w_in_parts,
            w_back_parts,
            counts,
            group,
        )
        moved = {}
        if z_step + 1 < z_size:
            moved["rows"] = ring_gather(ahead, "y")
        if z_step + 2 < z_size:
            moved["ahead"] = ring_step(ahead, "z")
        if z_step <= 1:
            moved["grads_z"] = ring_step(grads_z[1 + z_step], "z")
        if z_step == 1:
            moved["grads"] = ring_gather(grads_z[2], "y")
        if z_step == 2:
            moved["grads"] = [ring_step(part, "z") for part in grads_y[2][1:]]
            moved["grads_other"] = [ring_step(grads_z[3], "c")]
        if z_step >= 2:
            moved["grad"] = hops_y(grads_c[z_step - 1])
        if z_step >= 1:
            moved["result"] = ring_step(last_results[1], "c")
        if z_step == 3:
            moved["step"] = ring_step(grads_sum[1], "z")
            moved["grad_zero"] = hops_y(grads_c[0])
            moved["result_one"] = hops_y(results_c[1])
        parts, moved = sync(parts, moved)
        weighted.append(parts[4])
        grad_hidden.append(parts[5])
        grads_gates.append(parts[6])
        grads_last = []
        if z_step <= 1:
            grads_z.append(moved["grads_z"])
        if z_step in (1, 2):
            grads_y.append(([grads_z[3]] if z_step == 2 else []) + moved["grads"])
            grads_other.append(moved.get("grads_other", []))
            missing = grads_y[-1][len(grads_other[-1]) :]
            grads_last = [ring_step(part, "c") for part in missing]
        arrived = ring_step(parts[3], "c")
        if z_step + 1 < z_size:
            ahead, rows = moved.get("ahead"), moved["rows"]
            others = [ring_step(part, "c") for part in rows]
        arrived, others, rows, grads_last = sync(arrived, others, rows, grads_last)
        if grads_last:
            grads_other[-1] = grads_other[-1] + grads_last
        if z_step >= 1:
            results_c.append(plus_all(moved["result"], last_results[0]))
        if z_step >= 2:
            grads_sum[z_step - 1] = end_y(grads_c[z_step - 1], moved["grad"])
        grads_c.append(plus_all(arrived, parts[2]))
        last_results = parts[:2]

    total = plus(moved["step"], grads_sum[2])
    zero_hop = moved["grad_zero"]
    results_sum[1] = end_y(results_c[1], moved["result_one"])
    spread = jnp.stack(grads_gates).reshape(z_size, 2, y_size, E, count)
    spread = ring_sum([spread[:, 0], spread[:, 1]], "c", F32)

    def in_grads(which):
        first, last = ranges[which]
        return expert_grads(sent_chunks, grad_hidden, first, last, 2 * width, False)

    def halves(part):
        middle = part.shape[0] // 2
        return part[:middle], part[middle:]

    grads_c, total, results_c, results_sum, last_results, spread, grad_hidden = sync(
        grads_c, total, results_c, results_sum, last_results, spread, grad_hidden
    )
    first_grads, last_grad, step, result_three, spread = sync(
        in_grads(0),
        hops_y(grads_c[3]),
        ring_step(total, "z"),
        ring_step(last_results[1], "c"),
        ring_sum([spread[:, i] for i in range(y_size)], "y", F32),
    )
    total = plus(step, end_y(grads_c[3], last_grad))
    grad_hidden, total, results_sum, results_c, first_grads, result_three = sync(
        grad_hidden, total, results_sum, results_c, first_grads, result_three
    )
    second_grads, step, result_two, result_step, grad_gates, one, zero_hop, zero_parts = sync(
        in_grads(1),
        ring_step(total, "z"),
        hops_y(results_c[2]),
        ring_step(results_sum[1], "z"),
        ring_sum([spread[i] for i in range(z_size)], "z", F32),
        ring_step(first_grads[2], "x"),
        zero_hop,
        grads_c[0],
    )
    grad_gates = with_layout_constraint(grad_gates, Layout((0, 1))).T
    grad_experts = plus(step, end_y(zero_parts, zero_hop), F32)
    result_total = plus(result_step, end_y(results_c[2], result_two))
    grad_experts, first_grads, second_grads, results_c, result_total, result_three = sync(
        grad_experts, first_grads, second_grads, results_c, result_total, result_three
    )
    two = ring_step(first_grads[3], "x")
    second_one = ring_step(second_grads[2], "x")
    result_step = ring_step(result_total, "z")
    results_c.append(plus_all(result_three, last_results[0]))
    result_three = hops_y(results_c[3])

    def finish_x(parts, arrived, kind):
        rest = list(parts[2:]) + [parts[0]]
        total = plus(arrived, rest[0], kind)
        for part in rest[1:]:
            total = plus(ring_step(total, "x"), part, kind)
        return total

    def finish_in(parts, one, two):
        return jnp.concatenate([finish_x(parts[0::2], one, BF16), finish_x(parts[1::2], two, BF16)])

    grad_picked = chosen * (grad_gates - jnp.sum(grad_gates * gates, axis=-1, keepdims=True))
    grad_chance = grad_picked / picked_total
    grad_logits = (
        chance * (grad_chance - jnp.sum(chance * grad_chance, axis=-1, keepdims=True))
    ).astype(BF16)
    grad_w_router = dot(normed_two, grad_logits, ((0,), (0,)))
    grad_normed_two = grad_experts + dot(grad_logits, w_router, ((1,), (1,)))
    grad_resid, grad_gain_two = norm_back(grad_normed_two, resid, r_two, gain_second)
    grad_resid = grad_final + grad_resid

    grad_att = grad_resid.astype(BF16)
    grad_att = jnp.concatenate([grad_att, ring_step(grad_att, "c")])
    grad_w_out = dot(mixed, grad_att, ((0,), (0,))).astype(BF16)
    grad_mixed = dot(grad_att, w_out, ((1,), (1,))).astype(BF16)
    grad_mixed, grad_w_out, two, result_step, result_three, second_grads, results_c = sync(
        grad_mixed, grad_w_out, two, result_step, result_three, second_grads, results_c
    )
    first_sum = finish_in(first_grads, one, two)
    result_total = plus(result_step, end_y(results_c[3], result_three))
    out_parts = pick_weights([(grad_w_out, 0, MODEL_WIDTH)], "x", "y", False)
    first_sum, out_parts, grad_mixed, result_total, second_grads = sync(
        first_sum, out_parts, grad_mixed, result_total, second_grads
    )
    first_pieces = lax.all_to_all(first_sum, "z", 0, 0, tiled=True)
    second_two = ring_step(second_grads[3], "x")
    out_hop = begin(out_parts, "y")
    result_step = ring_step(result_total, "z")
    result_zero = hops_y(results_c[0])
    grad_qk_pre, grad_value_pre = attention_call(
        attention_back_kernel,
        [query, keys, values, grad_mixed, logs],
        [(q_width + kv_width, BF16), (kv_width, BF16)],
        tables,
        block,
        [pltpu.VMEM((block, q_width + kv_width), F32)],
        "attention_back",
    )
    grad_qk_pre, grad_value_pre, second_one, out_hop, out_parts = sync(
        grad_qk_pre, grad_value_pre, second_one, out_hop, out_parts
    )
    out_parts = finish(out_parts, out_hop)
    out_parts = [out_parts[i] for i in range(x_size)]
    out_hop = begin(out_parts, "x")
    grad_w_qk = dot(normalized_input, grad_qk_pre, ((0,), (0,))).astype(BF16)
    grad_w_v = dot(normalized_input, grad_value_pre, ((0,), (0,))).astype(BF16)
    grad_normed = dot(grad_qk_pre, w_qk, ((1,), (1,)))
    grad_normed = grad_normed + dot(grad_value_pre, w_v, ((1,), (1,)))
    grad_normed, other_normed, second_two, grad_w_qk, grad_w_v, result_step = sync(
        grad_normed[:count],
        ring_step(grad_normed[count:], "c"),
        second_two,
        grad_w_qk,
        grad_w_v,
        result_step,
    )
    second_sum = finish_in(second_grads, second_one, second_two)
    grad_normed = grad_normed + other_normed
    grad_rows, grad_gain_one = norm_back(grad_normed, own_act, r_one[:count], gain_first)
    grad_rows = grad_resid + grad_rows

    grad_small = jnp.concatenate(
        [grad_w_router, grad_gain_one[:, None], grad_gain_two[:, None]], axis=1
    )
    grad_small = jnp.pad(grad_small, ((0, 0), (0, LANES - grad_small.shape[1])))
    q_parts = pick_weights([(grad_w_qk, 0, q_width)], "x", "y", True)
    rest = [
        (grad_w_qk, q_width, kv_width),
        (grad_w_v, 0, kv_width),
        (grad_small.astype(BF16), 0, LANES),
    ]
    rest_parts = pick_weights(rest, "y", "x", True)
    q_parts, rest_parts, grad_rows, grad_chunks, result_zero, first_pieces, second_sum = sync(
        q_parts, rest_parts, grad_rows, grad_chunks, result_zero, first_pieces, second_sum
    )
    second_pieces = lax.all_to_all(second_sum, "z", 0, 0, tiled=True)
    grad_w_back, q_sum, rest_sum, out_hop, out_parts = sync(
        expert_grads(grad_chunks, weighted, 0, local_count, width, True),
        ring_sum(q_parts, "y", BF16),
        ring_sum(rest_parts, "x", BF16),
        out_hop,
        out_parts,
    )
    out_sum = finish(out_parts, out_hop)
    back_x = ring_step(grad_w_back[1], "x")
    q_sum, rest_sum, out_sum, first_pieces, second_pieces, result_step = sync(
        sum_along(q_sum, "x"),
        sum_along(rest_sum, "y"),
        out_sum,
        first_pieces,
        second_pieces,
        result_step,
    )
    grad_gate_up = unpack_experts(first_pieces, *ranges[0], local_count, [])
    outputs = resid + plus(result_step, end_y(results_c[0], result_zero), F32)
    grad_first, grad_second, grad_w_out, grad_gate_up, outputs = sync(
        *[sum_along(part, "z", F32) for part in (q_sum, rest_sum, out_sum)],
        grad_gate_up,
        outputs,
    )
    grad_w_gate, grad_w_up = unpack_experts(
        second_pieces, *ranges[1], local_count, list(grad_gate_up)
    )
    grad_w_down = finish_x(grad_w_back, back_x, F32)
    grad_both = jnp.concatenate([grad_first, grad_second], axis=-1)
    mine = lax.dynamic_index_in_dim(grad_both, core, 0, keepdims=False)
    theirs = lax.dynamic_index_in_dim(grad_both, 1 - core, 0, keepdims=False)
    got = ring_step(theirs, "c")

    def whole_columns(start, columns):
        parts = [part[:, start : start + columns].reshape(own_rows, y_size, -1) for part in (mine, got)]
        ordered = jnp.where(core == 0, jnp.stack(parts, 2), jnp.stack(parts[::-1], 2))
        return ordered.reshape(own_rows, 2 * columns)

    grad_small = (mine + got)[:, q_width + 2 * kv_width :]
    return (
        outputs.astype(BF16).reshape(inputs.shape),
        grad_rows.reshape(inputs.shape),
        grad_small[:, E],
        whole_columns(0, q_width),
        whole_columns(q_width, kv_width),
        whole_columns(q_width + kv_width, kv_width),
        grad_w_out,
        grad_small[:, E + 1],
        grad_small[:, :E],
        grad_w_gate,
        grad_w_up,
        grad_w_down,
    )


def solution(mesh):
    experts, shards = mesh.shape["expert"], mesh.shape["shard"]
    split = Mesh(
        mesh.devices.reshape(experts // 2, 2, SLICES, shards // SLICES), ("y", "c", "z", "x")
    )
    groups, within = ("y", "c"), ("z", "x")
    tokens = P(None, ALL, None)
    rows = P(ALL, None)
    expert = P(groups, within, None)
    return jax.shard_map(
        body,
        mesh=split,
        in_specs=(tokens,) * 4
        + (P(ALL), rows, rows, rows, rows, P(ALL), rows, expert, expert, expert),
        out_specs=(tokens, tokens, P(ALL), rows, rows, rows, rows, P(ALL), rows)
        + (expert, expert, expert),
        check_vma=False,
    )
```
